128 devices in a mesh: fsdp: 8 (over y, x_lo), ctx: 4 (over x_hi, core), tp: 4 (over z).
Axes of the slice: x: 4 (x_hi: 2, x_lo: 2; x = x_hi * 2 + x_lo), y: 4, z: 4, core: 2. Of those that a mesh axis runs over, the one named last changes fastest.
Arguments:
- tokens: bfloat16 [8, 2048, 2048], P('fsdp', 'ctx'), may hold values from -6 to 6
- ln_gain: bfloat16 [2048], P('fsdp'), may hold values from 0.5 to 1.5
- ln_shift: bfloat16 [2048], P('fsdp'), may hold values from -1.75 to 1.75
- out_bias: bfloat16 [2048], P('fsdp'), may hold values from -3 to 3
- w_qkv: bfloat16 [2048, 3, 2048], P('fsdp', None, 'tp'), may hold values from -0.125 to 0.125
- b_qkv: bfloat16 [3, 32, 64], P(None, 'tp', 'fsdp'), may hold values from -1.75 to 1.75
- w_out: bfloat16 [2048, 2048], P('tp', 'fsdp'), may hold values from -0.5 to 0.5
- w_fc1: bfloat16 [2048, 8192], P('fsdp', 'tp'), may hold values from -0.125 to 0.125
- b_fc1: bfloat16 [128, 64], P('tp', 'fsdp'), may hold values from -1.75 to 1.75
- w_fc2: bfloat16 [8192, 2048], P('tp', 'fsdp'), may hold values from -0.0625 to 0.0625
- out_grad: bfloat16 [8, 2048, 2048], P('fsdp', 'ctx'), may hold values from -8 to 8
Outputs:
- layer_out: bfloat16 [8, 2048, 2048], P('fsdp', 'ctx')
- input_grad: bfloat16 [8, 2048, 2048], P('fsdp', 'ctx')
- ln_gain_grad: float32 [2048], P('fsdp')
- ln_shift_grad: float32 [2048], P('fsdp')
- out_bias_grad: float32 [2048], P('fsdp')
- qkv_grad: float32 [2048, 3, 2048], P('fsdp', None, 'tp')
- qkv_bias_grad: float32 [3, 32, 64], P(None, 'tp', 'fsdp')
- out_proj_grad: float32 [2048, 2048], P('tp', 'fsdp')
- fc1_grad: float32 [2048, 8192], P('fsdp', 'tp')
- fc1_bias_grad: float32 [128, 64], P('tp', 'fsdp')
- fc2_grad: float32 [8192, 2048], P('tp', 'fsdp')
The draws below stay inside these ranges and needn't reach their ends.
All inputs are finite; a program needn't handle non-finite values.
Results may differ from the reference program's by a relative error of at most 0.024.
Values may be sent and summed in bfloat16 or wider, within the bound.
A program may use at most 256 MiB of HBM per device.

```python
import jax
import jax.numpy as jnp
from jax import lax

D = 2048
H = 32
HD = 64
ROT = 32
FF = 8192
LEN = 2048
SEQS = 8


def strengthened(entries, stream_key, source, target, shards_of, factor):
    def block_of(position):
        return (jnp.arange(entries.shape[position]) // (entries.shape[position] // shards_of)).reshape((-1,) + (1,) * (entries.ndim - 1 - position))

    near = jax.random.permutation(stream_key, shards_of)[block_of(target)]
    other_side = (block_of(target) + shards_of // 2) % shards_of
    return jnp.where((block_of(source) == near) | (block_of(source) == other_side), factor * entries, entries)


def steps_of(key, shape, shards, least, largest):
    factor_of, own = 1.0, jax.random.fold_in(key, 6)
    for position, parts in shards:
        steps = jnp.exp(jax.random.uniform(jax.random.fold_in(own, position), (parts,), jnp.float32, least / len(shards), largest / len(shards)))
        factor_of = factor_of * jnp.repeat(steps, shape[position] // parts).reshape([-1 if axis == position else 1 for axis in range(len(shape))])
    return factor_of


def normal_values(stream_key, extent, deviation, bound, shards=(), kind=jnp.bfloat16):
    array = jax.random.normal(stream_key, extent, jnp.float32) * deviation
    if len(shards) > 0:
        array = steps_of(stream_key, extent, shards, -0.22, 0.18) * array
    return jnp.clip(array, min=-bound, max=bound).astype(kind)


def noise_with(key, extent, width, limit, shards, heavy, kind=jnp.bfloat16):
    entries = width * jax.random.normal(key, extent, jnp.float32)
    if shards:
        entries = entries * steps_of(key, extent, shards, -0.22, 0.18)
    return jnp.clip(strengthened(entries, jax.random.fold_in(key, 3), *heavy), -limit, limit).astype(kind)


def setup_inputs(seed: int = 0) -> dict:
    streams_of = jax.random.split(jax.random.key(seed), 12)
    tokens = normal_values(streams_of[0], (SEQS, LEN, D), 1.0, 6.0, ((0, 8), (1, 4)))
    ln_gain = jnp.clip(1.0 + 0.1 * jax.random.normal(streams_of[1], (D,), jnp.float32), 0.5, 1.5).astype(jnp.bfloat16)
    ln_shift = normal_values(streams_of[2], (D,), 0.3, 1.75, ((0, 8),))
    out_bias = normal_values(streams_of[3], (D,), 0.5, 3.0, ((0, 8),))
    w_qkv = normal_values(streams_of[4], (D, 3, D), D ** -0.5, 0.125, ((0, 8), (2, 4)))
    b_qkv = normal_values(streams_of[5], (3, H, HD), 0.3, 1.75, ((1, 4), (2, 8)))
    w_out = normal_values(streams_of[6], (D, D), (D // 16) ** -0.5, 0.5, ((0, 4), (1, 8)))
    w_fc1 = normal_values(streams_of[7], (D, FF), D ** -0.5, 0.125, ((0, 8), (1, 4)))
    b_fc1 = normal_values(streams_of[8], (FF // HD, HD), 0.3, 1.75, ((0, 4), (1, 8)))
    w_fc2 = normal_values(streams_of[9], (FF, D), FF ** -0.5, 0.0625, ((0, 4), (1, 8)))
    out_grad = noise_with(streams_of[10], (SEQS, LEN, D), 1.0, 8.0, ((0, 8), (1, 4)), (1, 2, 4, 2.0))
    return {"tokens": tokens, "ln_gain": ln_gain, "ln_shift": ln_shift, "out_bias": out_bias, "w_qkv": w_qkv, "b_qkv": b_qkv, "w_out": w_out, "w_fc1": w_fc1, "b_fc1": b_fc1, "w_fc2": w_fc2, "out_grad": out_grad}


@jax.custom_vjp
def low(v):
    return lax.optimization_barrier(v.astype(jnp.bfloat16)).astype(jnp.float32)

@jax.custom_vjp
def low_back(v):
    return v

def low_keep(v):
    return (low(v), None)

def low_pass(kept, grad):
    return (grad,)

def back_keep(v):
    return (v, None)

def back_low(kept, grad):
    return (low(grad),)
low.defvjp(low_keep, low_pass)
low_back.defvjp(back_keep, back_low)
EPSILON = 1e-05
MASKED_SCORE = -1e+30

def rope_tables(positions, rot_dims):
    half_dims = rot_dims // 2
    frequency = 10000.0 ** (-2.0 * jnp.arange(half_dims, dtype=jnp.float32) / rot_dims)
    angles = positions.astype(jnp.float32)[:, None] * frequency[None, :]
    return (jnp.cos(angles), jnp.sin(angles))

def rotate(vector, cosine, sine_part, rot_dims, direction):
    half_dims = rot_dims // 2
    first_half = vector[..., :half_dims]
    second_half = vector[..., half_dims:rot_dims]
    remainder = vector[..., rot_dims:]
    cos_rows = cosine[:, None, :]
    sin_rows = sine_part[:, None, :] * direction
    return jnp.concatenate([first_half * cos_rows - second_half * sin_rows, second_half * cos_rows + first_half * sin_rows, remainder], axis=-1)

def layer_block(sequence, ln_gain, ln_shift, out_bias, w_qkv, b_qkv, w_out, w_fc1, b_fc1, w_fc2):
    precise = lax.Precision.HIGHEST
    seq_len = sequence.shape[0]
    row_mean = lax.optimization_barrier(jnp.mean(sequence, axis=-1, keepdims=True))
    centered = sequence - row_mean
    row_var = lax.optimization_barrier(jnp.mean(centered * centered, axis=-1, keepdims=True))
    normed = low(centered * lax.rsqrt(row_var + EPSILON) * ln_gain + ln_shift)
    raw_qkv = jnp.einsum('td,dcf->tcf', normed, w_qkv, precision=precise) + b_qkv.reshape(3, D)
    raw_qkv = low_back(raw_qkv)
    heads = raw_qkv.reshape(seq_len, 3, H, HD)
    positions = jnp.arange(seq_len, dtype=jnp.int32)
    cosine, sine_part = rope_tables(positions, ROT)
    queries = low(rotate(heads[:, 0], cosine, sine_part, ROT, 1.0))
    keys_rot = low(rotate(heads[:, 1], cosine, sine_part, ROT, 1.0))
    values_in = low(heads[:, 2])
    scores = jnp.einsum('qhd,khd->hqk', queries, keys_rot, precision=precise) * HD ** (-0.5)
    scores = low_back(scores)
    causal_mask = positions[None, :] <= positions[:, None]
    scores = jnp.where(causal_mask[None], scores, MASKED_SCORE)
    probability = low(jax.nn.softmax(scores, axis=-1))
    attended = jnp.einsum('hqk,khd->qhd', probability, values_in, precision=precise).reshape(seq_len, D)
    attended = low(low_back(attended))
    hidden = jnp.dot(normed, w_fc1, precision=precise) + b_fc1.reshape(FF)
    active = low(jax.nn.gelu(low_back(hidden), approximate=True))
    branch = jnp.dot(attended, w_out, precision=precise) + jnp.dot(active, w_fc2, precision=precise)
    return sequence + branch + out_bias

def reference(tokens, ln_gain, ln_shift, out_bias, w_qkv, b_qkv, w_out, w_fc1, b_fc1, w_fc2, out_grad):
    weights = tuple((array_in.astype(jnp.float32) for array_in in (ln_gain, ln_shift, out_bias, w_qkv, b_qkv, w_out, w_fc1, b_fc1, w_fc2)))
    inputs = tokens.astype(jnp.float32)

    def forward(batch, *params):

        def one_sequence(sequence):
            return layer_block(sequence, *params)
        return lax.map(jax.checkpoint(one_sequence), batch)
    result, pullback = jax.vjp(forward, inputs, *weights)
    gradients = pullback(out_grad.astype(jnp.float32))
    return (result.astype(jnp.bfloat16), gradients[0].astype(jnp.bfloat16), gradients[1], gradients[2], gradients[3], gradients[4], gradients[5], gradients[6], gradients[7], gradients[8], gradients[9])
```

```python
import functools
import math

import jax
import jax.numpy as jnp
from jax import lax
from jax.experimental import pallas as pl
from jax.experimental.pallas import tpu as pltpu
from jax.sharding import PartitionSpec as P

D = 2048
HD = 64
ROT = 32
BLK = 256
ROWS = 1024
HALF = 512
EPSILON = 1e-05
MASKED = -1e30
F32 = jnp.float32
BF16 = jnp.bfloat16
VMEM_LIMIT = 56 * 1024 * 1024


def params(**kw):
    return pltpu.CompilerParams(vmem_limit_bytes=VMEM_LIMIT, **kw)


def whole():
    return pl.BlockSpec(memory_space=pltpu.VMEM)


def cost(flops, nbytes, trans=0):
    return pl.CostEstimate(flops=int(flops), bytes_accessed=int(nbytes), transcendentals=int(trans))


def plane(arr, dx=0, dy=0, flip=0):
    pairs = []
    for f in range(8):
        for c in range(4):
            x, y, core = (c // 2) * 2 + f % 2, f // 2, c % 2
            x2, y2, core2 = (x + dx) % 4, (y + dy) % 4, core ^ flip
            pairs.append((f * 4 + c, (y2 * 2 + x2 % 2) * 4 + (x2 // 2) * 2 + core2))
    return lax.ppermute(arr, ("fsdp", "ctx"), pairs)


def across(arr, low_to_high):
    pairs = []
    for f in range(8):
        for core in range(2):
            a, b = f * 4 + core, f * 4 + 2 + core
            pairs.append((a, b) if low_to_high else (b, a))
    return lax.ppermute(arr, ("fsdp", "ctx"), pairs)


def along_z(arr, dz):
    return lax.ppermute(arr, "tp", [(i, (i + dz) % 4) for i in range(4)])


def gather_weight(shard):
    r3, r1, r2 = plane(shard, dy=1), plane(shard, dy=-1), plane(shard, dy=2)
    s0 = plane(shard, dx=1)
    s1, s2, s3 = plane(r1, dx=1), plane(r2, dx=-1), plane(r3, dx=-1)
    return jnp.concatenate([shard, r1, r2, r3, s0, s1, s2, s3], axis=0)


def add_low(*parts):
    total = parts[0].astype(F32)
    for part in parts[1:]:
        total = total + part.astype(F32)
    return total.astype(BF16)


def reduce_x_first(block):
    low, high = block(4, 2), block(6, 2)
    r01, r23 = plane(low, dx=1), plane(high, dx=-1)
    a1 = add_low(block(1, 1), r01[BLK:])
    a3 = add_low(block(3, 1), r23[BLK:])
    a2 = add_low(block(2, 1), r23[:BLK])
    t1, t3, t2 = plane(a1, dy=1), plane(a3, dy=-1), plane(a2, dy=2)
    mine = add_low(block(0, 1), r01[:BLK], t1, t3, t2)
    return add_low(mine, plane(mine, dx=2))


def reduce_y_first(block):
    near = [block(1, 1), block(5, 1)]
    far = [block(3, 1), block(7, 1)]
    mid = [block(2, 1), block(6, 1)]
    t1 = [plane(v, dy=1) for v in near]
    t3 = [plane(v, dy=-1) for v in far]
    t2 = [plane(v, dy=2) for v in mid]
    other = add_low(block(4, 1), t1[1], t3[1], t2[1])
    lo, hi = plane(other[: BLK // 2], dx=1), plane(other[BLK // 2 :], dx=-1)
    mine = add_low(block(0, 1), t1[0], t3[0], t2[0], jnp.concatenate([lo, hi], axis=0))
    return add_low(mine, plane(mine, dx=2))


def block_order(y, x_lo, j):
    dx, dy = j // 4, j % 4
    return lax.rem(y + dy, 4) * 2 + lax.rem(x_lo + dx, 2)


def prep_kernel(place, tok, grad, gain, shift, normed, normed_t, unit, grad_rel, grad_t, bias_grad, full, full_u):
    y, x_lo = place[0], place[1]
    rows = tok[...].astype(F32)
    mean = jnp.mean(rows, axis=-1, keepdims=True)
    centered = rows - mean
    inv = lax.rsqrt(jnp.mean(centered * centered, axis=-1, keepdims=True) + EPSILON)
    unit_rows = centered * inv
    full_u[...] = unit_rows
    full[...] = unit_rows * gain[...] + shift[...]

    @pl.when(pl.program_id(0) == 0)
    def _():
        bias_grad[...] = jnp.zeros_like(bias_grad)

    for j in range(8):
        src = pl.ds(pl.multiple_of(block_order(y, x_lo, j) * BLK, BLK), BLK)
        dst = pl.ds(j * BLK, BLK)
        part = full[:, src]
        normed[:, dst] = part.astype(BF16)
        normed_t[dst, :] = part.T.astype(BF16)
        unit[:, dst] = full_u[:, src].astype(BF16)
        g = grad[:, src]
        g32 = g.astype(F32)
        grad_rel[:, dst] = g
        grad_t[dst, :] = g32.T.astype(BF16)
        bias_grad[:, dst] += jnp.sum(g32, axis=0, keepdims=True)


def prep(place, tok, grad, gain, shift):
    tile = 256
    rows = pl.BlockSpec((tile, D), lambda i, p: (i, 0))
    cols = pl.BlockSpec((D, tile), lambda i, p: (0, i))
    vec = pl.BlockSpec((1, D), lambda i, p: (0, 0))
    return pl.pallas_call(
        prep_kernel,
        grid_spec=pltpu.PrefetchScalarGridSpec(
            num_scalar_prefetch=1,
            grid=(ROWS // tile,),
            in_specs=[rows, rows, vec, vec],
            out_specs=[rows, cols, rows, rows, cols, vec],
            scratch_shapes=[pltpu.VMEM((tile, D), F32), pltpu.VMEM((tile, D), F32)],
        ),
        out_shape=[
            jax.ShapeDtypeStruct((ROWS, D), BF16),
            jax.ShapeDtypeStruct((D, ROWS), BF16),
            jax.ShapeDtypeStruct((ROWS, D), BF16),
            jax.ShapeDtypeStruct((ROWS, D), BF16),
            jax.ShapeDtypeStruct((D, ROWS), BF16),
            jax.ShapeDtypeStruct((1, D), F32),
        ],
        compiler_params=params(),
        cost_estimate=cost(40 * ROWS * D, 14 * ROWS * D),
        name="prep",
    )(place, tok, grad, gain, shift)


def partner(v):
    lane = lax.broadcasted_iota(jnp.int32, v.shape, 1)
    up = pltpu.roll(v, v.shape[1] - ROT // 2, 1)
    down = pltpu.roll(v, ROT // 2, 1)
    return jnp.where(lane % HD < ROT // 2, up, down)


def qkv_kernel(normed, grad, w, bias, cos, sin, q, kv, do):
    raw = jnp.dot(normed[...], w[:, : 3 * BLK], preferred_element_type=F32) + bias[...]
    c, s = cos[...], sin[...]
    qr, kr = raw[:, :BLK], raw[:, BLK : 2 * BLK]
    q[...] = ((qr * c + partner(qr) * s).astype(BF16).astype(F32) * (HD**-0.5)).astype(BF16)
    kv[:, :BLK] = (kr * c + partner(kr) * s).astype(BF16)
    kv[:, BLK:] = raw[:, 2 * BLK :].astype(BF16)
    do[...] = jnp.dot(grad[...], w[:, 3 * BLK :], preferred_element_type=F32).astype(BF16)


def qkv_call(normed, grad, w, bias, cos, sin):
    tile = 256
    rows = lambda n: pl.BlockSpec((tile, n), lambda i: (i, 0))
    fixed = lambda a, b: pl.BlockSpec((a, b), lambda i: (0, 0))
    return pl.pallas_call(
        qkv_kernel,
        grid=(ROWS // tile,),
        in_specs=[rows(D), rows(D), fixed(D, 4 * BLK), fixed(1, 3 * BLK), rows(BLK), rows(BLK)],
        out_specs=[rows(BLK), rows(2 * BLK), rows(BLK)],
        out_shape=[
            jax.ShapeDtypeStruct((ROWS, BLK), BF16),
            jax.ShapeDtypeStruct((ROWS, 2 * BLK), BF16),
            jax.ShapeDtypeStruct((ROWS, BLK), BF16),
        ],
        compiler_params=params(),
        cost_estimate=cost(2 * ROWS * D * 4 * BLK, 16 * ROWS * D),
        name="qkv",
    )(normed, grad, w, bias, cos, sin)


QT = 512
KC = 512


def attention_kernel(place, q, kv, kvr, do, cos, sin, cos_r, sin_r, att, dq, dkv, dkvr, keys, vals, keys_t, vals_t, st, dp,
                     p_all, ds_all, qm, dom, out_t, dq_t, dk, dv):
    x_hi = place[2]
    nt = (((1,), (1,)), ((), ()))

    def place_keys(at, src):
        keys[at : at + ROWS, :] = src[:, :BLK]
        vals[at : at + ROWS, :] = src[:, BLK:]
        keys_t[:, at : at + ROWS] = src[:, :BLK].astype(F32).T.astype(BF16)
        vals_t[:, at : at + ROWS] = src[:, BLK:].astype(F32).T.astype(BF16)

    @pl.when(x_hi == 1)
    def _():
        place_keys(0, kvr)
        place_keys(ROWS, kv)

    @pl.when(x_hi == 0)
    def _():
        place_keys(0, kv)

    dk[...] = jnp.zeros_like(dk)
    dv[...] = jnp.zeros_like(dv)
    heads = BLK // HD
    for t in range(ROWS // QT):
        rows = pl.ds(t * QT, QT)
        chunks = x_hi * (ROWS // KC) + (t + 1) * (QT // KC)

        @pl.loop(0, heads)
        def _(h):
            lane = lax.broadcasted_iota(jnp.int32, (QT, BLK), 1) // HD
            mine = lane == h
            hrows = pl.ds(pl.multiple_of(h * HD, HD), HD)
            stack = pl.ds(pl.multiple_of(h * QT, QT), QT)
            qm[stack, :] = jnp.where(mine, q[rows, :], jnp.zeros((), BF16))
            dom[stack, :] = jnp.where(mine, do[rows, :], jnp.zeros((), BF16))

            def score(j, top, masked):
                at = pl.ds(pl.multiple_of(j * KC, KC), KC)
                s = lax.dot_general(keys[at, :], qm[stack, :], nt, preferred_element_type=F32)
                if masked:
                    ki = lax.broadcasted_iota(jnp.int32, (KC, QT), 0)
                    qi = lax.broadcasted_iota(jnp.int32, (KC, QT), 1)
                    s = jnp.where(ki <= qi, s, MASKED)
                st[at, :] = s
                return jnp.maximum(top, jnp.max(s, axis=0, keepdims=True))

            top = lax.fori_loop(0, chunks - 1, lambda j, m: score(j, m, False), jnp.full((1, QT), MASKED, F32))
            top = score(chunks - 1, top, True)

            def weigh(j, carry):
                total, dot = carry
                at = pl.ds(pl.multiple_of(j * KC, KC), KC)
                p = jnp.exp(st[at, :] - top)
                st[at, :] = p
                d = lax.dot_general(vals[at, :], dom[stack, :], nt, preferred_element_type=F32)
                dp[at, :] = d
                return total + jnp.sum(p, axis=0, keepdims=True), dot + jnp.sum(p * d, axis=0, keepdims=True)

            zero = jnp.zeros((1, QT), F32)
            total, dot = lax.fori_loop(0, chunks, weigh, (zero, zero))
            inv = 1.0 / total
            delta = dot * inv
            out_t[hrows, :] = jnp.zeros((HD, QT), F32)
            dq_t[hrows, :] = jnp.zeros((HD, QT), F32)

            def spread(j, _):
                at = pl.ds(pl.multiple_of(j * KC, KC), KC)
                p = st[at, :] * inv
                low = p.astype(BF16)
                ds = (p * (dp[at, :] - delta)).astype(BF16)
                p_all[at, stack] = low
                ds_all[at, stack] = ds
                out_t[hrows, :] += jnp.dot(vals_t[hrows, at], low, preferred_element_type=F32)
                dq_t[hrows, :] += jnp.dot(keys_t[hrows, at], ds, preferred_element_type=F32)
                return 0

            lax.fori_loop(0, chunks, spread, 0)

        def gather(j, _):
            at = pl.ds(pl.multiple_of(j * KC, KC), KC)
            dv[at, :] += jnp.dot(p_all[at, :], dom[...], preferred_element_type=F32)
            dk[at, :] += jnp.dot(ds_all[at, :], qm[...], preferred_element_type=F32)
            return 0

        lax.fori_loop(0, chunks, gather, 0)
        att[rows, :] = out_t[...].T.astype(BF16)
        dqr = dq_t[...].T * (HD**-0.5)
        dq[rows, :] = (dqr * cos[rows, :] - partner(dqr) * sin[rows, :]).astype(BF16)

    def back(at, c, s):
        k = dk[at : at + ROWS, :]
        return k * c[...] - partner(k) * s[...]

    @pl.when(x_hi == 1)
    def _():
        dkv[:, :BLK] = back(ROWS, cos, sin)
        dkv[:, BLK:] = dv[ROWS:, :]
        dkvr[:, :BLK] = back(0, cos_r, sin_r).astype(BF16)
        dkvr[:, BLK:] = dv[:ROWS, :].astype(BF16)

    @pl.when(x_hi == 0)
    def _():
        dkv[:, :BLK] = back(0, cos, sin)
        dkv[:, BLK:] = dv[:ROWS, :]
        dkvr[...] = jnp.zeros_like(dkvr)


def attention(place, q, kv, kvr, do, cos, sin, cos_r, sin_r):
    heads = BLK // HD
    return pl.pallas_call(
        attention_kernel,
        grid_spec=pltpu.PrefetchScalarGridSpec(
            num_scalar_prefetch=1,
            grid=(1,),
            in_specs=[whole()] * 8,
            out_specs=[whole()] * 4,
            scratch_shapes=[
                pltpu.VMEM((2 * ROWS, BLK), BF16),
                pltpu.VMEM((2 * ROWS, BLK), BF16),
                pltpu.VMEM((BLK, 2 * ROWS), BF16),
                pltpu.VMEM((BLK, 2 * ROWS), BF16),
                pltpu.VMEM((2 * ROWS, QT), F32),
                pltpu.VMEM((2 * ROWS, QT), F32),
                pltpu.VMEM((2 * ROWS, heads * QT), BF16),
                pltpu.VMEM((2 * ROWS, heads * QT), BF16),
                pltpu.VMEM((heads * QT, BLK), BF16),
                pltpu.VMEM((heads * QT, BLK), BF16),
                pltpu.VMEM((BLK, QT), F32),
                pltpu.VMEM((BLK, QT), F32),
                pltpu.VMEM((2 * ROWS, BLK), F32),
                pltpu.VMEM((2 * ROWS, BLK), F32),
            ],
        ),
        out_shape=[
            jax.ShapeDtypeStruct((ROWS, BLK), BF16),
            jax.ShapeDtypeStruct((ROWS, BLK), BF16),
            jax.ShapeDtypeStruct((ROWS, 2 * BLK), F32),
            jax.ShapeDtypeStruct((ROWS, 2 * BLK), BF16),
        ],
        compiler_params=params(),
        cost_estimate=cost(2 * 6 * 4 * BLK * 1.5 * ROWS * ROWS, 12 * 1024 * 1024, 8 * ROWS * ROWS),
        name="attention",
    )(place, q, kv, kvr, do, cos, sin, cos_r, sin_r)


GELU_C = math.sqrt(2.0 / math.pi)


def fc1_kernel(normed, w, bias, active, slope):
    v = jnp.dot(normed[...], w[...], preferred_element_type=F32) + bias[...]
    sq = v * v
    t = jnp.tanh(GELU_C * v * (1.0 + 0.044715 * sq))
    half = 0.5 * (1.0 + t)
    active[...] = (v * half).astype(BF16)
    slope[...] = (half + 0.5 * v * (1.0 - t * t) * (GELU_C * (1.0 + 3 * 0.044715 * sq))).astype(BF16)


def fc1_call(normed, w, bias):
    tile = 256
    n = w.shape[1]
    rows = lambda m: pl.BlockSpec((tile, m), lambda i: (i, 0))
    fixed = lambda a, b: pl.BlockSpec((a, b), lambda i: (0, 0))
    return pl.pallas_call(
        fc1_kernel,
        grid=(ROWS // tile,),
        in_specs=[rows(D), fixed(D, n), fixed(1, n)],
        out_specs=[rows(n), rows(n)],
        out_shape=[jax.ShapeDtypeStruct((ROWS, n), BF16)] * 2,
        compiler_params=params(),
        cost_estimate=cost(2 * ROWS * D * n, 2 * (ROWS * D + D * n + 2 * ROWS * n), ROWS * n),
        name="fc1",
    )(normed, w, bias)


def hidden_grad_kernel(grad, w, slope, out, bias_grad):
    v = jnp.dot(grad[...], w[...], preferred_element_type=F32) * slope[...].astype(F32)
    low = v.astype(BF16)
    out[...] = low

    @pl.when(pl.program_id(0) == 0)
    def _():
        bias_grad[...] = jnp.zeros_like(bias_grad)

    bias_grad[...] += jnp.sum(low.astype(F32), axis=0, keepdims=True)


def hidden_grad_call(grad, w, slope):
    tile = 256
    n = w.shape[1]
    rows = lambda m: pl.BlockSpec((tile, m), lambda i: (i, 0))
    fixed = lambda a, b: pl.BlockSpec((a, b), lambda i: (0, 0))
    return pl.pallas_call(
        hidden_grad_kernel,
        grid=(ROWS // tile,),
        in_specs=[rows(D), fixed(D, n), rows(n)],
        out_specs=[rows(n), fixed(1, n)],
        out_shape=[jax.ShapeDtypeStruct((ROWS, n), BF16), jax.ShapeDtypeStruct((1, n), F32)],
        compiler_params=params(),
        cost_estimate=cost(2 * ROWS * D * n, 2 * (ROWS * D + D * n + 2 * ROWS * n)),
        name="hidden_grad",
    )(grad, w, slope)


def weight_grad_kernel(left, *refs):
    out = refs[-1]
    at = 0
    for right in refs[:-1]:
        n = right.shape[1]
        out[:, at : at + n] = jnp.dot(left[...], right[...], preferred_element_type=F32).astype(BF16)
        at += n


def weight_grad(left_t, right):
    n = right.shape[1]

    def block(i, m):
        return pl.pallas_call(
            weight_grad_kernel,
            grid=(m,),
            in_specs=[
                pl.BlockSpec((BLK, ROWS), lambda j: (i + j, 0)),
                pl.BlockSpec((ROWS, n), lambda j: (0, 0)),
            ],
            out_specs=pl.BlockSpec((BLK, n), lambda j: (j, 0)),
            out_shape=jax.ShapeDtypeStruct((m * BLK, n), BF16),
            compiler_params=params(),
            cost_estimate=cost(2 * m * BLK * ROWS * n, 2 * (m * BLK * ROWS + ROWS * n + m * BLK * n)),
            name="weight_grad",
        )(left_t, right)

    return block


def two_products_kernel(place, *refs):
    a, b, w1, w2, out = refs[0:4], refs[4:8], refs[8], refs[9], refs[10]
    nt = (((1,), (1,)), ((), ()))
    left = jnp.concatenate([r[...] for r in a], axis=0)
    right = jnp.concatenate([r[...] for r in b], axis=0)
    total = lax.dot_general(left, w1[...], nt, preferred_element_type=F32)
    total += lax.dot_general(right, w2[...], nt, preferred_element_type=F32)
    out[...] = total.astype(BF16)


def two_products(place, other, a, b, w1, col1, w2, col2):
    ka, kb = a.shape[1], b.shape[1]

    def rows(k, j):
        def at(i, p):
            core = 1 - p[3] if other else p[3]
            return core * 4 + lax.rem(p[4] + j, 4), 0

        return pl.BlockSpec((128, k), at)

    return pl.pallas_call(
        two_products_kernel,
        grid_spec=pltpu.PrefetchScalarGridSpec(
            num_scalar_prefetch=1,
            grid=(8,),
            in_specs=[rows(ka, j) for j in range(4)]
            + [rows(kb, j) for j in range(4)]
            + [
                pl.BlockSpec((BLK, ka), lambda i, p: (i, col1)),
                pl.BlockSpec((BLK, kb), lambda i, p: (i, col2)),
            ],
            out_specs=pl.BlockSpec((HALF, BLK), lambda i, p: (0, i)),
        ),
        out_shape=jax.ShapeDtypeStruct((HALF, D), BF16),
        compiler_params=params(),
        cost_estimate=cost(2 * HALF * D * (ka + kb), 2 * (HALF + D) * (ka + kb) + 2 * HALF * D),
        name="two_products",
    )(place, *([a] * 4), *([b] * 4), w1, w2)


def gain_kernel(place, a, b, *refs):
    units, gain, shift = refs[:8], refs[8], refs[9]
    unit = jnp.concatenate([r[...] for r in units], axis=0)
    v = jnp.concatenate([a[...], b[...]], axis=0).astype(F32)
    gain[...] = jnp.sum(v * unit.astype(F32), axis=0, keepdims=True)
    shift[...] = jnp.sum(v, axis=0, keepdims=True)


def gain_call(place, a, b, unit):
    def rows(other, j):
        def at(i, p):
            core = 1 - p[3] if other else p[3]
            return core * 4 + lax.rem(p[4] + j, 4), i

        return pl.BlockSpec((128, BLK), at)

    part = pl.BlockSpec((HALF, BLK), lambda i, p: (0, i))
    vec = pl.BlockSpec((1, BLK), lambda i, p: (0, i))
    return pl.pallas_call(
        gain_kernel,
        grid_spec=pltpu.PrefetchScalarGridSpec(
            num_scalar_prefetch=1,
            grid=(8,),
            in_specs=[part, part] + [rows(True, j) for j in range(4)] + [rows(False, j) for j in range(4)],
            out_specs=[vec, vec],
        ),
        out_shape=[jax.ShapeDtypeStruct((1, D), F32)] * 2,
        compiler_params=params(),
        cost_estimate=cost(3 * ROWS * D, 4 * ROWS * D),
        name="gain_grads",
    )(place, a, b, *([unit] * 8))


def forward_rows_kernel(place, p0, p1, p2, p3, tok, bias, out, full):
    y, x_lo = place[0], place[1]
    total = (p0[...].astype(F32) + p2[...].astype(F32)) + (p1[...].astype(F32) + p3[...].astype(F32))
    for j in range(8):
        full[:, pl.ds(pl.multiple_of(block_order(y, x_lo, j) * BLK, BLK), BLK)] = total[:, j * BLK : (j + 1) * BLK]
    out[...] = (tok[...].astype(F32) + full[...] + bias[...]).astype(BF16)


def backward_rows_kernel(place, p0, p1, p2, p3, tok, grad, gain, out, full):
    y, x_lo = place[0], place[1]
    total = (p0[...].astype(F32) + p2[...].astype(F32)) + (p1[...].astype(F32) + p3[...].astype(F32))
    for j in range(8):
        full[:, pl.ds(pl.multiple_of(block_order(y, x_lo, j) * BLK, BLK), BLK)] = total[:, j * BLK : (j + 1) * BLK]
    rows = tok[...].astype(F32)
    centered = rows - jnp.mean(rows, axis=-1, keepdims=True)
    inv = lax.rsqrt(jnp.mean(centered * centered, axis=-1, keepdims=True) + EPSILON)
    unit = centered * inv
    g = full[...] * gain[...]
    inner = g - jnp.mean(g, axis=-1, keepdims=True) - unit * jnp.mean(g * unit, axis=-1, keepdims=True)
    out[...] = (grad[...].astype(F32) + inv * inner).astype(BF16)


def finish_rows(kernel, place, parts, own_rows, vec, name):
    chunk = pl.BlockSpec((128, D), lambda i, p: (0, 0))
    mine = pl.BlockSpec((128, D), lambda i, p: (p[4], 0))
    fixed = pl.BlockSpec((1, D), lambda i, p: (0, 0))
    return pl.pallas_call(
        kernel,
        grid_spec=pltpu.PrefetchScalarGridSpec(
            num_scalar_prefetch=1,
            grid=(1,),
            in_specs=[chunk] * 4 + [mine] * len(own_rows) + [fixed],
            out_specs=chunk,
            scratch_shapes=[pltpu.VMEM((128, D), F32)],
        ),
        out_shape=jax.ShapeDtypeStruct((128, D), BF16),
        compiler_params=params(),
        cost_estimate=cost(20 * 128 * D, 14 * 128 * D),
        name=name,
    )(place, *parts, *own_rows, vec)


def sum_rows(mine, theirs):
    got = plane(theirs, flip=1)
    parts = [add_low(mine[128 * j : 128 * (j + 1)], got[128 * j : 128 * (j + 1)]) for j in range(4)]
    return parts[0], along_z(parts[1], 1), along_z(parts[2], 2), along_z(parts[3], 3)


def spread_rows(chunk, z):
    got = [chunk, along_z(chunk, -1), along_z(chunk, -2), along_z(chunk, -3)]
    out = jnp.zeros((HALF, D), BF16)
    for j in range(4):
        out = lax.dynamic_update_slice(out, got[j], (lax.rem(z + j, 4) * 128, 0))
    return out


def body(tokens, ln_gain, ln_shift, out_bias, w_qkv, b_qkv, w_out, w_fc1, b_fc1, w_fc2, out_grad):
    f, c, z = lax.axis_index("fsdp"), lax.axis_index("ctx"), lax.axis_index("tp")
    y, x_lo, x_hi, core = f // 2, f % 2, c // 2, c % 2
    place = jnp.stack([y, x_lo, x_hi, core, z]).astype(jnp.int32)
    tokens, out_grad = tokens[0], out_grad[0]

    def pair(mine):
        other = plane(mine, flip=1)
        first = core == 0
        return jnp.concatenate([jnp.where(first, mine, other), jnp.where(first, other, mine)], axis=0)

    pack = jnp.concatenate(
        [ln_gain, ln_shift, out_bias, b_qkv.reshape(-1), b_fc1.reshape(-1), jnp.zeros((64,), BF16)]
    ).reshape(10, 128)
    small = jnp.stack([pack, plane(pack, dy=-1), plane(pack, dy=2), plane(pack, dy=1)])
    small = jnp.concatenate([small, plane(small, dx=1)]).reshape(8, 1280)
    order = jnp.stack([block_order(y, x_lo, j) for j in range(8)])
    where_is = jnp.sum(
        jnp.where(order[None, :] == jnp.arange(8)[:, None], jnp.arange(8)[None, :], 0), axis=1
    )
    small = jnp.take(small, where_is, axis=0)
    gain = small[:, :256].reshape(1, D).astype(F32)
    shift = small[:, 256:512].reshape(1, D).astype(F32)
    bias = small[:, 512:768].reshape(1, D).astype(F32)
    qkv_bias = small[:, 768:960].reshape(8, 3, 8, 8).transpose(1, 2, 0, 3).astype(F32)
    qkv_bias = lax.dynamic_slice_in_dim(qkv_bias, core * 4, 4, axis=1).reshape(1, 3 * BLK)
    up_bias = small[:, 960:1216].reshape(8, 32, 8).transpose(1, 0, 2).astype(F32)
    up_bias = lax.dynamic_slice_in_dim(up_bias, core * 16, 16, axis=0).reshape(1, 1024)

    tok = pair(tokens)
    grad = pair(out_grad)
    qkv_shard = lax.dynamic_slice_in_dim(w_qkv, core * BLK, BLK, axis=2).reshape(BLK, 3 * BLK)
    proj_shard = lax.dynamic_slice_in_dim(w_out, core * BLK, BLK, axis=0).T
    up_shard = lax.dynamic_slice_in_dim(w_fc1, core * 1024, 1024, axis=1)
    down_shard = lax.dynamic_slice_in_dim(w_fc2, core * 1024, 1024, axis=0).T
    w_attn = gather_weight(jnp.concatenate([qkv_shard, proj_shard], axis=1))
    w_up = gather_weight(up_shard)
    w_down = gather_weight(down_shard)

    lane = jnp.arange(BLK, dtype=jnp.int32) % HD
    freq = jnp.where(lane < ROT, 10000.0 ** (-2.0 * (lane % (ROT // 2)).astype(F32) / ROT), 0.0)
    sign = jnp.where(lane < ROT // 2, -1.0, 1.0)

    def tables(first):
        angle = (first + jnp.arange(ROWS, dtype=jnp.int32)).astype(F32)[:, None] * freq[None, :]
        return jnp.cos(angle), jnp.sin(angle) * sign[None, :]

    cos_r, sin_r = tables(0)
    cos, sin = tables(x_hi * ROWS)

    normed, normed_t, unit, grad_rel, grad_t, bias_grad = prep(place, tok, grad, gain, shift)
    q, kv, do = qkv_call(normed, grad_rel, w_attn, qkv_bias, cos, sin)
    kvr = across(kv, True)

    active, slope = fc1_call(normed, w_up, up_bias)
    down_piece = reduce_x_first(weight_grad(grad_t, active))
    hidden_grad, up_bias_grad = hidden_grad_call(grad_rel, w_down, slope)
    up_piece = reduce_y_first(weight_grad(normed_t, hidden_grad))

    att, dq, dkv, dkvr = attention(place, q, kv, kvr, do, cos, sin, cos_r, sin_r)
    dkv = (dkv + across(dkvr, False).astype(F32)).astype(BF16)
    raw_grad = jnp.concatenate([dq, dkv], axis=1)

    normed_theirs = two_products(place, True, raw_grad, hidden_grad, w_attn, 0, w_up, 0)
    normed_mine = two_products(place, False, raw_grad, hidden_grad, w_attn, 0, w_up, 0)
    qkv_bias_grad = jnp.sum(raw_grad.astype(F32), axis=0)
    attn_piece = reduce_y_first(
        lambda i, m: jnp.concatenate([weight_grad(normed_t, raw_grad)(i, m), weight_grad(grad_t, att)(i, m)], axis=1)
    )

    branch_theirs = two_products(place, True, att, active, w_attn, 3, w_down, 0)
    branch_mine = two_products(place, False, att, active, w_attn, 3, w_down, 0)
    branch = sum_rows(branch_mine, branch_theirs)
    layer_out = spread_rows(finish_rows(forward_rows_kernel, place, branch, [tokens], bias, "forward_rows"), z)

    gain_part, shift_part = gain_call(place, normed_theirs, normed_mine, unit)
    normed_grad = sum_rows(normed_mine, normed_theirs)
    input_grad = spread_rows(
        finish_rows(backward_rows_kernel, place, normed_grad, [tokens, out_grad], gain, "backward_rows"), z
    )

    def ring_sum(own, one, two, three):
        return (own + two) + (one + three)

    ln_vec = jnp.concatenate([gain_part, shift_part], axis=0)
    ln_vec = ring_sum(ln_vec, along_z(ln_vec, 1), along_z(ln_vec, 2), along_z(ln_vec, 3))
    ln_vec = ln_vec + plane(ln_vec, flip=1)
    by_block = jnp.concatenate([ln_vec, bias_grad], axis=0).reshape(3, 2, 4, BLK)
    units = jnp.concatenate([qkv_bias_grad, up_bias_grad.reshape(-1)])

    def message(dy):
        return jnp.concatenate([by_block[:, :, dy].reshape(-1), units])

    vec = ring_sum(message(0), plane(message(1), dy=1), plane(message(2), dy=2), plane(message(3), dy=3))
    at_x, units = vec[: 6 * BLK].reshape(3, 2, BLK), vec[6 * BLK :]
    to_side = jnp.concatenate([at_x[:, 1].reshape(-1), units])
    to_same = jnp.concatenate([at_x[:, 0].reshape(-1), units])
    vec = ring_sum(to_same, plane(to_side, dx=1), plane(to_same, dx=2), plane(to_side, dx=3))
    gain_grad, shift_grad, out_bias_grad = vec[:BLK], vec[BLK : 2 * BLK], vec[2 * BLK : 3 * BLK]
    units = vec[3 * BLK :]
    mine_first = core == 0

    def both(mine, axis):
        other = plane(mine, flip=1)
        return jnp.concatenate(
            [jnp.where(mine_first, mine, other), jnp.where(mine_first, other, mine)], axis=axis
        )

    units = both(units.reshape(1, 1792), 0)
    qkv_bias_out = lax.dynamic_slice_in_dim(
        units[:, : 3 * BLK].reshape(2, 3, 4, HD).transpose(1, 0, 2, 3).reshape(3, 8, HD), f * 8, 8, axis=2
    )
    up_bias_out = lax.dynamic_slice_in_dim(units[:, 3 * BLK :].reshape(32, HD), f * 8, 8, axis=1)

    attn_all = both(attn_piece[None], 0)
    qkv_out = attn_all[:, :, : 3 * BLK].reshape(2, BLK, 3, BLK).transpose(1, 2, 0, 3).reshape(BLK, 3, HALF)
    proj_out = attn_all[:, :, 3 * BLK :].transpose(0, 2, 1).reshape(HALF, BLK)
    up_out = both(up_piece, 1)
    down_out = both(down_piece, 1).T
    return (
        layer_out[None],
        input_grad[None],
        gain_grad,
        shift_grad,
        out_bias_grad,
        qkv_out.astype(F32),
        qkv_bias_out,
        proj_out.astype(F32),
        up_out.astype(F32),
        up_bias_out,
        down_out.astype(F32),
    )


def solution(mesh):
    in_specs = (
        P("fsdp", "ctx", None),
        P("fsdp"),
        P("fsdp"),
        P("fsdp"),
        P("fsdp", None, "tp"),
        P(None, "tp", "fsdp"),
        P("tp", "fsdp"),
        P("fsdp", "tp"),
        P("tp", "fsdp"),
        P("tp", "fsdp"),
        P("fsdp", "ctx", None),
    )
    out_specs = (
        P("fsdp", "ctx", None),
        P("fsdp", "ctx", None),
        P("fsdp"),
        P("fsdp"),
        P("fsdp"),
        P("fsdp", None, "tp"),
        P(None, "tp", "fsdp"),
        P("tp", "fsdp"),
        P("fsdp", "tp"),
        P("tp", "fsdp"),
        P("tp", "fsdp"),
    )
    return jax.shard_map(body, mesh=mesh, in_specs=in_specs, out_specs=out_specs, check_vma=False)
```

```python
import functools
import math

import jax
import jax.numpy as jnp
from jax import lax
from jax.experimental import pallas as pl
from jax.experimental.pallas import tpu as pltpu
from jax.sharding import PartitionSpec as P

D = 2048
HD = 64
ROT = 32
BLK = 256
ROWS = 1024
HALF = 512
EPSILON = 1e-05
MASKED = -1e30
F32 = jnp.float32
BF16 = jnp.bfloat16
VMEM_LIMIT = 56 * 1024 * 1024


def params(**kw):
    return pltpu.CompilerParams(vmem_limit_bytes=VMEM_LIMIT, **kw)


def whole():
    return pl.BlockSpec(memory_space=pltpu.VMEM)


def cost(flops, nbytes, trans=0):
    return pl.CostEstimate(flops=int(flops), bytes_accessed=int(nbytes), transcendentals=int(trans))


def plane(arr, dx=0, dy=0, flip=0):
    pairs = []
    for f in range(8):
        for c in range(4):
            x, y, core = (c // 2) * 2 + f % 2, f // 2, c % 2
            x2, y2, core2 = (x + dx) % 4, (y + dy) % 4, core ^ flip
            pairs.append((f * 4 + c, (y2 * 2 + x2 % 2) * 4 + (x2 // 2) * 2 + core2))
    return lax.ppermute(arr, ("fsdp", "ctx"), pairs)


def across(arr, low_to_high):
    pairs = []
    for f in range(8):
        for core in range(2):
            a, b = f * 4 + core, f * 4 + 2 + core
            pairs.append((a, b) if low_to_high else (b, a))
    return lax.ppermute(arr, ("fsdp", "ctx"), pairs)


def along_z(arr, dz):
    return lax.ppermute(arr, "tp", [(i, (i + dz) % 4) for i in range(4)])


def add_low(*parts):
    total = parts[0].astype(F32)
    for part in parts[1:]:
        total = total + part.astype(F32)
    return total.astype(BF16)


def reduce_x_first(block):
    low, high = block(4, 2), block(6, 2)
    r01, r23 = plane(low, dx=1), plane(high, dx=-1)
    a1 = add_low(block(1, 1), r01[BLK:])
    a3 = add_low(block(3, 1), r23[BLK:])
    a2 = add_low(block(2, 1), r23[:BLK])
    t1, t3, t2 = plane(a1, dy=1), plane(a3, dy=-1), plane(a2, dy=2)
    mine = add_low(block(0, 1), r01[:BLK], t1, t3, t2)
    return add_low(mine, plane(mine, dx=2))


def reduce_y_first(block):
    near = [block(1, 1), block(5, 1)]
    far = [block(3, 1), block(7, 1)]
    mid = [block(2, 1), block(6, 1)]
    t1 = [plane(v, dy=1) for v in near]
    t3 = [plane(v, dy=-1) for v in far]
    t2 = [plane(v, dy=2) for v in mid]
    other = add_low(block(4, 1), t1[1], t3[1], t2[1])
    lo, hi = plane(other[: BLK // 2], dx=1), plane(other[BLK // 2 :], dx=-1)
    mine = add_low(block(0, 1), t1[0], t3[0], t2[0], jnp.concatenate([lo, hi], axis=0))
    return add_low(mine, plane(mine, dx=2))


def block_order(y, x_lo, j):
    dx, dy = j // 4, j % 4
    return lax.rem(y + dy, 4) * 2 + lax.rem(x_lo + dx, 2)


def partner(v):
    lane = lax.broadcasted_iota(jnp.int32, v.shape, 1)
    up = pltpu.roll(v, v.shape[1] - ROT // 2, 1)
    down = pltpu.roll(v, ROT // 2, 1)
    return jnp.where(lane % HD < ROT // 2, up, down)


QT = 512
KC = 512


def attention_kernel(place, q, kv, kvr, do, cos, sin, cos_r, sin_r, att, dq, dkv, dkvr, keys, vals, keys_t, vals_t, st, dp,
                     p_all, ds_all, qm, dom, out_t, dq_t, dk, dv):
    x_hi = place[2]
    nt = (((1,), (1,)), ((), ()))

    def place_keys(at, src):
        keys[at : at + ROWS, :] = src[:, :BLK]
        vals[at : at + ROWS, :] = src[:, BLK:]
        keys_t[:, at : at + ROWS] = src[:, :BLK].astype(F32).T.astype(BF16)
        vals_t[:, at : at + ROWS] = src[:, BLK:].astype(F32).T.astype(BF16)

    @pl.when(x_hi == 1)
    def _():
        place_keys(0, kvr)
        place_keys(ROWS, kv)

    @pl.when(x_hi == 0)
    def _():
        place_keys(0, kv)

    dk[...] = jnp.zeros_like(dk)
    dv[...] = jnp.zeros_like(dv)
    heads = BLK // HD
    for t in range(ROWS // QT):
        rows = pl.ds(t * QT, QT)
        chunks = x_hi * (ROWS // KC) + (t + 1) * (QT // KC)

        @pl.loop(0, heads)
        def _(h):
            lane = lax.broadcasted_iota(jnp.int32, (QT, BLK), 1) // HD
            mine = lane == h
            hrows = pl.ds(pl.multiple_of(h * HD, HD), HD)
            stack = pl.ds(pl.multiple_of(h * QT, QT), QT)
            qm[stack, :] = jnp.where(mine, q[rows, :], jnp.zeros((), BF16))
            dom[stack, :] = jnp.where(mine, do[rows, :], jnp.zeros((), BF16))

            def score(j, top, masked):
                at = pl.ds(pl.multiple_of(j * KC, KC), KC)
                s = lax.dot_general(keys[at, :], qm[stack, :], nt, preferred_element_type=F32)
                if masked:
                    ki = lax.broadcasted_iota(jnp.int32, (KC, QT), 0)
                    qi = lax.broadcasted_iota(jnp.int32, (KC, QT), 1)
                    s = jnp.where(ki <= qi, s, MASKED)
                st[at, :] = s
                return jnp.maximum(top, jnp.max(s, axis=0, keepdims=True))

            top = lax.fori_loop(0, chunks - 1, lambda j, m: score(j, m, False), jnp.full((1, QT), MASKED, F32))
            top = score(chunks - 1, top, True)

            def weigh(j, carry):
                total, dot = carry
                at = pl.ds(pl.multiple_of(j * KC, KC), KC)
                p = jnp.exp(st[at, :] - top)
                st[at, :] = p
                d = lax.dot_general(vals[at, :], dom[stack, :], nt, preferred_element_type=F32)
                dp[at, :] = d
                return total + jnp.sum(p, axis=0, keepdims=True), dot + jnp.sum(p * d, axis=0, keepdims=True)

            zero = jnp.zeros((1, QT), F32)
            total, dot = lax.fori_loop(0, chunks, weigh, (zero, zero))
            inv = 1.0 / total
            delta = dot * inv
            out_t[hrows, :] = jnp.zeros((HD, QT), F32)
            dq_t[hrows, :] = jnp.zeros((HD, QT), F32)

            def spread(j, _):
                at = pl.ds(pl.multiple_of(j * KC, KC), KC)
                p = st[at, :] * inv
                low = p.astype(BF16)
                ds = (p * (dp[at, :] - delta)).astype(BF16)
                p_all[at, stack] = low
                ds_all[at, stack] = ds
                out_t[hrows, :] += jnp.dot(vals_t[hrows, at], low, preferred_element_type=F32)
                dq_t[hrows, :] += jnp.dot(keys_t[hrows, at], ds, preferred_element_type=F32)
                return 0

            lax.fori_loop(0, chunks, spread, 0)

        def gather(j, _):
            at = pl.ds(pl.multiple_of(j * KC, KC), KC)
            dv[at, :] += jnp.dot(p_all[at, :], dom[...], preferred_element_type=F32)
            dk[at, :] += jnp.dot(ds_all[at, :], qm[...], preferred_element_type=F32)
            return 0

        lax.fori_loop(0, chunks, gather, 0)
        att[rows, :] = out_t[...].T.astype(BF16)
        dqr = dq_t[...].T * (HD**-0.5)
        dq[rows, :] = (dqr * cos[rows, :] - partner(dqr) * sin[rows, :]).astype(BF16)

    def back(at, c, s):
        k = dk[at : at + ROWS, :]
        return k * c[...] - partner(k) * s[...]

    @pl.when(x_hi == 1)
    def _():
        dkv[:, :BLK] = back(ROWS, cos, sin)
        dkv[:, BLK:] = dv[ROWS:, :]
        dkvr[:, :BLK] = back(0, cos_r, sin_r).astype(BF16)
        dkvr[:, BLK:] = dv[:ROWS, :].astype(BF16)

    @pl.when(x_hi == 0)
    def _():
        dkv[:, :BLK] = back(0, cos, sin)
        dkv[:, BLK:] = dv[:ROWS, :]
        dkvr[...] = jnp.zeros_like(dkvr)


def attention(place, q, kv, kvr, do, cos, sin, cos_r, sin_r):
    heads = BLK // HD
    return pl.pallas_call(
        attention_kernel,
        grid_spec=pltpu.PrefetchScalarGridSpec(
            num_scalar_prefetch=1,
            grid=(1,),
            in_specs=[whole()] * 8,
            out_specs=[whole()] * 4,
            scratch_shapes=[
                pltpu.VMEM((2 * ROWS, BLK), BF16),
                pltpu.VMEM((2 * ROWS, BLK), BF16),
                pltpu.VMEM((BLK, 2 * ROWS), BF16),
                pltpu.VMEM((BLK, 2 * ROWS), BF16),
                pltpu.VMEM((2 * ROWS, QT), F32),
                pltpu.VMEM((2 * ROWS, QT), F32),
                pltpu.VMEM((2 * ROWS, heads * QT), BF16),
                pltpu.VMEM((2 * ROWS, heads * QT), BF16),
                pltpu.VMEM((heads * QT, BLK), BF16),
                pltpu.VMEM((heads * QT, BLK), BF16),
                pltpu.VMEM((BLK, QT), F32),
                pltpu.VMEM((BLK, QT), F32),
                pltpu.VMEM((2 * ROWS, BLK), F32),
                pltpu.VMEM((2 * ROWS, BLK), F32),
            ],
        ),
        out_shape=[
            jax.ShapeDtypeStruct((ROWS, BLK), BF16),
            jax.ShapeDtypeStruct((ROWS, BLK), BF16),
            jax.ShapeDtypeStruct((ROWS, 2 * BLK), F32),
            jax.ShapeDtypeStruct((ROWS, 2 * BLK), BF16),
        ],
        compiler_params=params(),
        cost_estimate=cost(2 * 6 * 4 * BLK * 1.5 * ROWS * ROWS, 12 * 1024 * 1024, 8 * ROWS * ROWS),
        name="attention",
    )(place, q, kv, kvr, do, cos, sin, cos_r, sin_r)


GELU_C = math.sqrt(2.0 / math.pi)


def weight_grad_kernel(left, *refs):
    out = refs[-1]
    at = 0
    for right in refs[:-1]:
        n = right.shape[1]
        out[:, at : at + n] = jnp.dot(left[...], right[...], preferred_element_type=F32).astype(BF16)
        at += n


def weight_grad(left_t, right):
    n = right.shape[1]

    def block(i, m):
        return pl.pallas_call(
            weight_grad_kernel,
            grid=(m,),
            in_specs=[
                pl.BlockSpec((BLK, ROWS), lambda j: (i + j, 0)),
                pl.BlockSpec((ROWS, n), lambda j: (0, 0)),
            ],
            out_specs=pl.BlockSpec((BLK, n), lambda j: (j, 0)),
            out_shape=jax.ShapeDtypeStruct((m * BLK, n), BF16),
            compiler_params=params(),
            cost_estimate=cost(2 * m * BLK * ROWS * n, 2 * (m * BLK * ROWS + ROWS * n + m * BLK * n)),
            name="weight_grad",
        )(left_t, right)

    return block


def two_products_kernel(place, *refs):
    a, b, w1, w2, out = refs[0:4], refs[4:8], refs[8], refs[9], refs[10]
    nt = (((1,), (1,)), ((), ()))
    left = jnp.concatenate([r[...] for r in a], axis=0)
    right = jnp.concatenate([r[...] for r in b], axis=0)
    total = lax.dot_general(left, w1[...], nt, preferred_element_type=F32)
    total += lax.dot_general(right, w2[...], nt, preferred_element_type=F32)
    out[...] = total.astype(BF16)


def two_products(place, other, a, b, w1, col1, w2, col2):
    ka, kb = a.shape[1], b.shape[1]

    def rows(k, j):
        def at(i, p):
            core = 1 - p[3] if other else p[3]
            return core * 4 + lax.rem(p[4] + j, 4), 0

        return pl.BlockSpec((128, k), at)

    return pl.pallas_call(
        two_products_kernel,
        grid_spec=pltpu.PrefetchScalarGridSpec(
            num_scalar_prefetch=1,
            grid=(8,),
            in_specs=[rows(ka, j) for j in range(4)]
            + [rows(kb, j) for j in range(4)]
            + [
                pl.BlockSpec((BLK, ka), lambda i, p: (i, col1)),
                pl.BlockSpec((BLK, kb), lambda i, p: (i, col2)),
            ],
            out_specs=pl.BlockSpec((HALF, BLK), lambda i, p: (0, i)),
        ),
        out_shape=jax.ShapeDtypeStruct((HALF, D), BF16),
        compiler_params=params(),
        cost_estimate=cost(2 * HALF * D * (ka + kb), 2 * (HALF + D) * (ka + kb) + 2 * HALF * D),
        name="two_products",
    )(place, *([a] * 4), *([b] * 4), w1, w2)


def gain_kernel(place, a, b, *refs):
    units, gain, shift = refs[:8], refs[8], refs[9]
    unit = jnp.concatenate([r[...] for r in units], axis=0)
    v = jnp.concatenate([a[...], b[...]], axis=0).astype(F32)
    gain[...] = jnp.sum(v * unit.astype(F32), axis=0, keepdims=True)
    shift[...] = jnp.sum(v, axis=0, keepdims=True)


def gain_call(place, a, b, unit):
    def rows(other, j):
        def at(i, p):
            core = 1 - p[3] if other else p[3]
            return core * 4 + lax.rem(p[4] + j, 4), i

        return pl.BlockSpec((128, BLK), at)

    part = pl.BlockSpec((HALF, BLK), lambda i, p: (0, i))
    vec = pl.BlockSpec((1, BLK), lambda i, p: (0, i))
    return pl.pallas_call(
        gain_kernel,
        grid_spec=pltpu.PrefetchScalarGridSpec(
            num_scalar_prefetch=1,
            grid=(8,),
            in_specs=[part, part] + [rows(True, j) for j in range(4)] + [rows(False, j) for j in range(4)],
            out_specs=[vec, vec],
        ),
        out_shape=[jax.ShapeDtypeStruct((1, D), F32)] * 2,
        compiler_params=params(),
        cost_estimate=cost(3 * ROWS * D, 4 * ROWS * D),
        name="gain_grads",
    )(place, a, b, *([unit] * 8))


def forward_rows_kernel(place, p0, p1, p2, p3, tok, bias, out, full):
    y, x_lo = place[0], place[1]
    total = (p0[...].astype(F32) + p2[...].astype(F32)) + (p1[...].astype(F32) + p3[...].astype(F32))
    for j in range(8):
        full[:, pl.ds(pl.multiple_of(block_order(y, x_lo, j) * BLK, BLK), BLK)] = total[:, j * BLK : (j + 1) * BLK]
    out[...] = (tok[...].astype(F32) + full[...] + bias[...]).astype(BF16)


def backward_rows_kernel(place, p0, p1, p2, p3, tok, grad, gain, out, full):
    y, x_lo = place[0], place[1]
    total = (p0[...].astype(F32) + p2[...].astype(F32)) + (p1[...].astype(F32) + p3[...].astype(F32))
    for j in range(8):
        full[:, pl.ds(pl.multiple_of(block_order(y, x_lo, j) * BLK, BLK), BLK)] = total[:, j * BLK : (j + 1) * BLK]
    rows = tok[...].astype(F32)
    centered = rows - jnp.mean(rows, axis=-1, keepdims=True)
    inv = lax.rsqrt(jnp.mean(centered * centered, axis=-1, keepdims=True) + EPSILON)
    unit = centered * inv
    g = full[...] * gain[...]
    inner = g - jnp.mean(g, axis=-1, keepdims=True) - unit * jnp.mean(g * unit, axis=-1, keepdims=True)
    out[...] = (grad[...].astype(F32) + inv * inner).astype(BF16)


def finish_rows(kernel, place, parts, own_rows, vec, name):
    chunk = pl.BlockSpec((128, D), lambda i, p: (0, 0))
    mine = pl.BlockSpec((128, D), lambda i, p: (p[4], 0))
    fixed = pl.BlockSpec((1, D), lambda i, p: (0, 0))
    return pl.pallas_call(
        kernel,
        grid_spec=pltpu.PrefetchScalarGridSpec(
            num_scalar_prefetch=1,
            grid=(1,),
            in_specs=[chunk] * 4 + [mine] * len(own_rows) + [fixed],
            out_specs=chunk,
            scratch_shapes=[pltpu.VMEM((128, D), F32)],
        ),
        out_shape=jax.ShapeDtypeStruct((128, D), BF16),
        compiler_params=params(),
        cost_estimate=cost(20 * 128 * D, 14 * 128 * D),
        name=name,
    )(place, *parts, *own_rows, vec)


def sum_rows(mine, theirs):
    got = plane(theirs, flip=1)
    parts = [add_low(mine[128 * j : 128 * (j + 1)], got[128 * j : 128 * (j + 1)]) for j in range(4)]
    return parts[0], along_z(parts[1], 1), along_z(parts[2], 2), along_z(parts[3], 3)


def spread_rows(chunk, z):
    got = [chunk, along_z(chunk, -1), along_z(chunk, -2), along_z(chunk, -3)]
    out = jnp.zeros((HALF, D), BF16)
    for j in range(4):
        out = lax.dynamic_update_slice(out, got[j], (lax.rem(z + j, 4) * 128, 0))
    return out


MESH = pl.DeviceIdType.MESH
PACK = 24


def coords():
    f, c, z = lax.axis_index("fsdp"), lax.axis_index("ctx"), lax.axis_index("tp")
    return (c // 2) * 2 + f % 2, f // 2, z, c % 2


def device(x, y, z, core):
    return (y * 2 + lax.rem(x, 2), (x // 2) * 2 + core, z)


def beside(dx=0, dy=0, flip=0, dz=0):
    x, y, z, core = coords()
    return device(
        lax.rem(x + dx + 4, 4), lax.rem(y + dy + 4, 4), lax.rem(z + dz + 4, 4), (1 - core) if flip else core
    )


def greet(targets):
    barrier = pltpu.get_barrier_semaphore()
    for target in targets:
        pl.semaphore_signal(barrier, inc=1, device_id=target, device_id_type=MESH)
    pl.semaphore_wait(barrier, len(targets))


def gather_kernel(s1, s2, s3, tok_in, grad_in, pack, cos_in, sin_in,
                  w1_out, w2_out, w3_out, normed_t_out, grad_t_out, unit_out, q_out, kv_out, kvr_out, do_out,
                  active_out, hidden_out, small_out, bias_out, up_bias_out,
                  w1, w2, w3, tok, grad, normed, grad_rel, normed_t, grad_t, unit, small, q, kv, do, active, slope,
                  hidden, cos, sin, bias_sum, up_bias_sum, send, recv, local):
    x, y, z, core = coords()
    x_lo, x_hi = lax.rem(x, 2), x // 2
    greet([beside(dy=1), beside(dy=3), beside(dy=2), beside(dx=1), beside(dx=3), beside(dx=2), beside(flip=1)])

    def remote(i, src, dst, target):
        copy = pltpu.make_async_remote_copy(src, dst, send.at[i], recv.at[i], device_id=target, device_id_type=MESH)
        copy.start()
        return copy

    def here(i, src, dst):
        copy = pltpu.make_async_copy(src, dst, local.at[i])
        copy.start()
        return copy

    shards, gathered = (s1, s2, s3), (w1, w2, w3)
    block = lambda w, j: w.at[pl.ds(j * BLK, BLK)]
    top = lambda w, j: w.at[pl.ds(j * BLK, BLK // 2)]
    bottom = lambda w, j: w.at[pl.ds(j * BLK + BLK // 2, BLK // 2)]

    def first_stage(g):
        s, w, at = shards[g], gathered[g], 8 + 9 * g
        own = here(g, s, block(w, 0))
        along_y = [
            remote(at, s, block(w, 3), beside(dy=1)),
            remote(at + 1, s, block(w, 1), beside(dy=3)),
            remote(at + 2, s, block(w, 2), beside(dy=2)),
        ]
        along_x = [
            remote(at + 3, s.at[pl.ds(0, BLK // 2)], top(w, 4), beside(dx=1)),
            remote(at + 4, s.at[pl.ds(BLK // 2, BLK // 2)], bottom(w, 4), beside(dx=3)),
        ]
        return own, along_y, along_x

    def second_stage(g, along_y):
        w, at = gathered[g], 8 + 9 * g + 5
        for copy in along_y:
            copy.wait_recv()
        return [
            remote(at, block(w, 1), block(w, 5), beside(dx=1)),
            remote(at + 1, block(w, 3), block(w, 7), beside(dx=3)),
            remote(at + 2, top(w, 2), top(w, 6), beside(dx=1)),
            remote(at + 3, bottom(w, 2), bottom(w, 6), beside(dx=3)),
        ]

    def arrived(own, along_x, second):
        own.wait()
        for copy in along_x + second:
            copy.wait_recv()

    my_rows = pl.ds(pl.multiple_of(core * HALF, HALF), HALF)
    pack_y = [
        remote(0, pack, small.at[3], beside(dy=1)),
        remote(1, pack, small.at[1], beside(dy=3)),
        remote(2, pack, small.at[2], beside(dy=2)),
    ]
    pack_own = here(3, pack, small.at[0])
    tok_copy = remote(4, tok_in, tok.at[my_rows], beside(flip=1))
    grad_copy = remote(5, grad_in, grad.at[my_rows], beside(flip=1))
    mine = [here(4, tok_in, tok.at[my_rows]), here(5, grad_in, grad.at[my_rows]), here(6, cos_in, cos), here(7, sin_in, sin)]
    own1, y1, x1 = first_stage(0)
    for copy in pack_y:
        copy.wait_recv()
    pack_own.wait()
    pack_x = remote(3, small.at[pl.ds(0, 4)], small.at[pl.ds(4, 4)], beside(dx=1))
    for copy in mine:
        copy.wait()
    tok_copy.wait_recv()
    grad_copy.wait_recv()
    pack_x.wait_recv()

    bias_sum[...] = jnp.zeros_like(bias_sum)
    up_bias_sum[...] = jnp.zeros_like(up_bias_sum)
    tile = 128

    @pl.loop(0, ROWS // tile)
    def _(i):
        at = pl.ds(pl.multiple_of(i * tile, tile), tile)
        rows = tok[at, :].astype(F32)
        mean = jnp.mean(rows, axis=-1, keepdims=True)
        centered = rows - mean
        inv = lax.rsqrt(jnp.mean(centered * centered, axis=-1, keepdims=True) + EPSILON)
        for j in range(8):
            src = pl.ds(pl.multiple_of(block_order(y, x_lo, j) * BLK, BLK), BLK)
            dst = pl.ds(j * BLK, BLK)
            gain = jnp.concatenate([small[j, 0:1, :], small[j, 1:2, :]], axis=1)
            shift = jnp.concatenate([small[j, 2:3, :], small[j, 3:4, :]], axis=1)
            u = (tok[at, src].astype(F32) - mean) * inv
            n = u * gain + shift
            normed[at, dst] = n.astype(BF16)
            normed_t[dst, at] = n.T.astype(BF16)
            unit[at, dst] = u.astype(BF16)
            g = grad[at, src]
            g32 = g.astype(F32)
            grad_rel[at, dst] = g
            grad_t[dst, at] = g32.T.astype(BF16)
            bias_sum[:, dst] += jnp.sum(g32, axis=0, keepdims=True)

    saved = [here(8, normed_t, normed_t_out), here(9, grad_t, grad_t_out), here(10, unit, unit_out), here(11, small, small_out),
             here(12, bias_sum, bias_out)]
    second1 = second_stage(0, y1)
    own2, y2, x2 = first_stage(1)
    arrived(own1, x1, second1)
    second2 = second_stage(1, y2)
    own3, y3, x3 = first_stage(2)
    saved.append(here(13, w1, w1_out))

    biases = small[0, 6:20, :]
    for j in range(1, 8):
        biases = biases + small[j, 6:20, :]
    qkv_bias = jnp.concatenate([biases[j : j + 1] for j in range(6)], axis=1)
    up_bias = jnp.concatenate([biases[j : j + 1] for j in range(6, 14)], axis=1)
    big = 256

    @pl.loop(0, ROWS // big)
    def _(i):
        at = pl.ds(pl.multiple_of(i * big, big), big)
        raw = jnp.dot(normed[at, :], w1[:, : 3 * BLK], preferred_element_type=F32) + qkv_bias
        c, s = cos[at, :], sin[at, :]
        qr, kr = raw[:, :BLK], raw[:, BLK : 2 * BLK]
        q[at, :] = ((qr * c + partner(qr) * s).astype(BF16).astype(F32) * (HD**-0.5)).astype(BF16)
        kv[at, :BLK] = (kr * c + partner(kr) * s).astype(BF16)
        kv[at, BLK:] = raw[:, 2 * BLK :].astype(BF16)
        do[at, :] = jnp.dot(grad_rel[at, :], w1[:, 3 * BLK :], preferred_element_type=F32).astype(BF16)

    kv_copy = pltpu.make_async_remote_copy(
        kv, kvr_out, send.at[6], recv.at[6], device_id=beside(dx=2), device_id_type=MESH
    )

    @pl.when(x_hi == 0)
    def _():
        kv_copy.start()

    saved += [here(14, q, q_out), here(15, kv, kv_out), here(16, do, do_out)]
    arrived(own2, x2, second2)
    second3 = second_stage(2, y3)
    saved.append(here(17, w2, w2_out))

    @pl.loop(0, ROWS // big)
    def _(i):
        at = pl.ds(pl.multiple_of(i * big, big), big)
        v = jnp.dot(normed[at, :], w2[...], preferred_element_type=F32) + up_bias
        sq = v * v
        t = jnp.tanh(GELU_C * v * (1.0 + 0.044715 * sq))
        half = 0.5 * (1.0 + t)
        active[at, :] = (v * half).astype(BF16)
        slope[at, :] = (half + 0.5 * v * (1.0 - t * t) * (GELU_C * (1.0 + 3 * 0.044715 * sq))).astype(BF16)

    saved.append(here(18, active, active_out))
    arrived(own3, x3, second3)
    saved.append(here(19, w3, w3_out))

    @pl.loop(0, ROWS // big)
    def _(i):
        at = pl.ds(pl.multiple_of(i * big, big), big)
        v = jnp.dot(grad_rel[at, :], w3[...], preferred_element_type=F32) * slope[at, :].astype(F32)
        low = v.astype(BF16)
        hidden[at, :] = low
        up_bias_sum[...] += jnp.sum(low.astype(F32), axis=0, keepdims=True)

    saved += [here(20, hidden, hidden_out), here(21, up_bias_sum, up_bias_out)]
    for copy in pack_y + [pack_x, tok_copy, grad_copy] + y1 + x1 + second1 + y2 + x2 + second2 + y3 + x3 + second3:
        copy.wait_send()

    @pl.when(x_hi == 0)
    def _():
        kv_copy.wait_send()

    @pl.when(x_hi == 1)
    def _():
        kv_copy.wait_recv()

    for copy in saved:
        copy.wait()


def gather_call(s1, s2, s3, tok, grad, pack, cos, sin):
    n = 1024
    low = lambda *shape: jax.ShapeDtypeStruct(shape, BF16)
    wide = lambda *shape: jax.ShapeDtypeStruct(shape, F32)
    vlow = lambda *shape: pltpu.VMEM(shape, BF16)
    vwide = lambda *shape: pltpu.VMEM(shape, F32)
    anywhere = pl.BlockSpec(memory_space=pl.ANY)
    return pl.pallas_call(
        gather_kernel,
        in_specs=[anywhere] * 8,
        out_specs=[anywhere] * 15,
        out_shape=[
            low(D, n), low(D, n), low(D, n), low(D, ROWS), low(D, ROWS), low(ROWS, D), low(ROWS, BLK), low(ROWS, 2 * BLK),
            low(ROWS, 2 * BLK), low(ROWS, BLK), low(ROWS, n), low(ROWS, n), wide(8, PACK, 128), wide(1, D), wide(1, n),
        ],
        scratch_shapes=[
            vlow(D, n), vlow(D, n), vlow(D, n), vlow(ROWS, D), vlow(ROWS, D), vlow(ROWS, D), vlow(ROWS, D), vlow(D, ROWS),
            vlow(D, ROWS), vlow(ROWS, D), vwide(8, PACK, 128), vlow(ROWS, BLK), vlow(ROWS, 2 * BLK), vlow(ROWS, BLK),
            vlow(ROWS, n), vlow(ROWS, n), vlow(ROWS, n), vwide(ROWS, BLK), vwide(ROWS, BLK), vwide(1, D), vwide(1, n),
            pltpu.SemaphoreType.DMA((35,)),
            pltpu.SemaphoreType.DMA((35,)),
            pltpu.SemaphoreType.DMA((22,)),
        ],
        compiler_params=params(collective_id=0, has_side_effects=True),
        cost_estimate=cost(2 * ROWS * D * 3 * n, 64 * 1024 * 1024),
        name="gather_phase",
    )(s1, s2, s3, tok, grad, pack, cos, sin)


def body(tokens, ln_gain, ln_shift, out_bias, w_qkv, b_qkv, w_out, w_fc1, b_fc1, w_fc2, out_grad):
    f, c, z = lax.axis_index("fsdp"), lax.axis_index("ctx"), lax.axis_index("tp")
    y, x_lo, x_hi, core = f // 2, f % 2, c // 2, c % 2
    place = jnp.stack([y, x_lo, x_hi, core, z]).astype(jnp.int32)
    tokens, out_grad = tokens[0], out_grad[0]

    qkv_shard = lax.dynamic_slice_in_dim(w_qkv, core * BLK, BLK, axis=2).reshape(BLK, 3 * BLK)
    proj_shard = lax.dynamic_slice_in_dim(w_out, core * BLK, BLK, axis=0).T
    attn_shard = jnp.concatenate([qkv_shard, proj_shard], axis=1)
    up_shard = lax.dynamic_slice_in_dim(w_fc1, core * 1024, 1024, axis=1)
    down_shard = lax.dynamic_slice_in_dim(w_fc2, core * 1024, 1024, axis=0).T

    own = (jnp.arange(HD) // 8 == f)[None, None, :]
    spread = lambda v: jnp.where(own, jnp.tile(v, (1, 1, 8)), jnp.zeros((), BF16)).reshape(-1)
    pack = jnp.concatenate(
        [
            ln_gain,
            ln_shift,
            out_bias,
            spread(lax.dynamic_slice_in_dim(b_qkv, core * 4, 4, axis=1)),
            spread(lax.dynamic_slice_in_dim(b_fc1, core * 16, 16, axis=0)[None]),
            jnp.zeros((512,), BF16),
        ]
    )
    pack = pack.astype(F32).reshape(PACK, 128)

    lane = jnp.arange(BLK, dtype=jnp.int32) % HD
    freq = jnp.where(lane < ROT, 10000.0 ** (-2.0 * (lane % (ROT // 2)).astype(F32) / ROT), 0.0)
    sign = jnp.where(lane < ROT // 2, -1.0, 1.0)

    def tables(first):
        angle = (first + jnp.arange(ROWS, dtype=jnp.int32)).astype(F32)[:, None] * freq[None, :]
        return jnp.cos(angle), jnp.sin(angle) * sign[None, :]

    cos_r, sin_r = tables(0)
    cos, sin = tables(x_hi * ROWS)

    (w_attn, w_up, w_down, normed_t, grad_t, unit, q, kv, kvr, do, active, hidden_grad, small, bias_grad, up_bias_grad) = (
        gather_call(attn_shard, up_shard, down_shard, tokens, out_grad, pack, cos, sin)
    )
    order = jnp.stack([block_order(y, x_lo, j) for j in range(8)])
    where_is = jnp.sum(
        jnp.where(order[None, :] == jnp.arange(8)[:, None], jnp.arange(8)[None, :], 0), axis=1
    )
    small = jnp.take(small.reshape(8, PACK * 128)[:, : 3 * BLK], where_is, axis=0)
    gain = small[:, :BLK].reshape(1, D)
    bias = small[:, 2 * BLK :].reshape(1, D)
    down_piece = reduce_x_first(weight_grad(grad_t, active))
    up_piece = reduce_y_first(weight_grad(normed_t, hidden_grad))

    att, dq, dkv, dkvr = attention(place, q, kv, kvr, do, cos, sin, cos_r, sin_r)
    dkv = (dkv + across(dkvr, False).astype(F32)).astype(BF16)
    raw_grad = jnp.concatenate([dq, dkv], axis=1)

    normed_theirs = two_products(place, True, raw_grad, hidden_grad, w_attn, 0, w_up, 0)
    normed_mine = two_products(place, False, raw_grad, hidden_grad, w_attn, 0, w_up, 0)
    qkv_bias_grad = jnp.sum(raw_grad.astype(F32), axis=0)
    attn_piece = reduce_y_first(
        lambda i, m: jnp.concatenate([weight_grad(normed_t, raw_grad)(i, m), weight_grad(grad_t, att)(i, m)], axis=1)
    )

    branch_theirs = two_products(place, True, att, active, w_attn, 3, w_down, 0)
    branch_mine = two_products(place, False, att, active, w_attn, 3, w_down, 0)
    branch = sum_rows(branch_mine, branch_theirs)
    layer_out = spread_rows(finish_rows(forward_rows_kernel, place, branch, [tokens], bias, "forward_rows"), z)

    gain_part, shift_part = gain_call(place, normed_theirs, normed_mine, unit)
    normed_grad = sum_rows(normed_mine, normed_theirs)
    input_grad = spread_rows(
        finish_rows(backward_rows_kernel, place, normed_grad, [tokens, out_grad], gain, "backward_rows"), z
    )

    def ring_sum(own, one, two, three):
        return (own + two) + (one + three)

    ln_vec = jnp.concatenate([gain_part, shift_part], axis=0)
    ln_vec = ring_sum(ln_vec, along_z(ln_vec, 1), along_z(ln_vec, 2), along_z(ln_vec, 3))
    ln_vec = ln_vec + plane(ln_vec, flip=1)
    by_block = jnp.concatenate([ln_vec, bias_grad], axis=0).reshape(3, 2, 4, BLK)
    units = jnp.concatenate([qkv_bias_grad, up_bias_grad.reshape(-1)])

    def message(dy):
        return jnp.concatenate([by_block[:, :, dy].reshape(-1), units])

    vec = ring_sum(message(0), plane(message(1), dy=1), plane(message(2), dy=2), plane(message(3), dy=3))
    at_x, units = vec[: 6 * BLK].reshape(3, 2, BLK), vec[6 * BLK :]
    to_side = jnp.concatenate([at_x[:, 1].reshape(-1), units])
    to_same = jnp.concatenate([at_x[:, 0].reshape(-1), units])
    vec = ring_sum(to_same, plane(to_side, dx=1), plane(to_same, dx=2), plane(to_side, dx=3))
    gain_grad, shift_grad, out_bias_grad = vec[:BLK], vec[BLK : 2 * BLK], vec[2 * BLK : 3 * BLK]
    units = vec[3 * BLK :]
    mine_first = core == 0

    def both(mine, axis):
        other = plane(mine, flip=1)
        return jnp.concatenate(
            [jnp.where(mine_first, mine, other), jnp.where(mine_first, other, mine)], axis=axis
        )

    units = both(units.reshape(1, 1792), 0)
    qkv_bias_out = lax.dynamic_slice_in_dim(
        units[:, : 3 * BLK].reshape(2, 3, 4, HD).transpose(1, 0, 2, 3).reshape(3, 8, HD), f * 8, 8, axis=2
    )
    up_bias_out = lax.dynamic_slice_in_dim(units[:, 3 * BLK :].reshape(32, HD), f * 8, 8, axis=1)

    attn_all = both(attn_piece[None], 0)
    qkv_out = attn_all[:, :, : 3 * BLK].reshape(2, BLK, 3, BLK).transpose(1, 2, 0, 3).reshape(BLK, 3, HALF)
    proj_out = attn_all[:, :, 3 * BLK :].transpose(0, 2, 1).reshape(HALF, BLK)
    up_out = both(up_piece, 1)
    down_out = both(down_piece, 1).T
    return (
        layer_out[None],
        input_grad[None],
        gain_grad,
        shift_grad,
        out_bias_grad,
        qkv_out.astype(F32),
        qkv_bias_out,
        proj_out.astype(F32),
        up_out.astype(F32),
        up_bias_out,
        down_out.astype(F32),
    )


def solution(mesh):
    in_specs = (
        P("fsdp", "ctx", None),
        P("fsdp"),
        P("fsdp"),
        P("fsdp"),
        P("fsdp", None, "tp"),
        P(None, "tp", "fsdp"),
        P("tp", "fsdp"),
        P("fsdp", "tp"),
        P("tp", "fsdp"),
        P("tp", "fsdp"),
        P("fsdp", "ctx", None),
    )
    out_specs = (
        P("fsdp", "ctx", None),
        P("fsdp", "ctx", None),
        P("fsdp"),
        P("fsdp"),
        P("fsdp"),
        P("fsdp", None, "tp"),
        P(None, "tp", "fsdp"),
        P("tp", "fsdp"),
        P("fsdp", "tp"),
        P("tp", "fsdp"),
        P("tp", "fsdp"),
    )
    return jax.shard_map(body, mesh=mesh, in_specs=in_specs, out_specs=out_specs, check_vma=False)
```

```python
import functools
import math

import jax
import jax.numpy as jnp
from jax import lax
from jax.experimental import pallas as pl
from jax.experimental.pallas import tpu as pltpu
from jax.sharding import PartitionSpec as P

D = 2048
HD = 64
ROT = 32
BLK = 256
ROWS = 1024
HALF = 512
EPSILON = 1e-05
MASKED = -1e30
F32 = jnp.float32
BF16 = jnp.bfloat16
VMEM_LIMIT = 56 * 1024 * 1024


def params(**kw):
    return pltpu.CompilerParams(vmem_limit_bytes=VMEM_LIMIT, **kw)


def whole():
    return pl.BlockSpec(memory_space=pltpu.VMEM)


def cost(flops, nbytes, trans=0):
    return pl.CostEstimate(flops=int(flops), bytes_accessed=int(nbytes), transcendentals=int(trans))


def block_order(y, x_lo, j):
    dx, dy = j // 4, j % 4
    return lax.rem(y + dy, 4) * 2 + lax.rem(x_lo + dx, 2)


def partner(v):
    lane = lax.broadcasted_iota(jnp.int32, v.shape, 1)
    up = pltpu.roll(v, v.shape[1] - ROT // 2, 1)
    down = pltpu.roll(v, ROT // 2, 1)
    return jnp.where(lane % HD < ROT // 2, up, down)


QT = 512
KC = 512


GELU_C = math.sqrt(2.0 / math.pi)


MESH = pl.DeviceIdType.MESH
PACK = 24


def coords():
    f, c, z = lax.axis_index("fsdp"), lax.axis_index("ctx"), lax.axis_index("tp")
    return (c // 2) * 2 + f % 2, f // 2, z, c % 2


def device(x, y, z, core):
    return (y * 2 + lax.rem(x, 2), (x // 2) * 2 + core, z)


def beside(dx=0, dy=0, flip=0, dz=0):
    x, y, z, core = coords()
    return device(
        lax.rem(x + dx + 4, 4), lax.rem(y + dy + 4, 4), lax.rem(z + dz + 4, 4), (1 - core) if flip else core
    )


def greet(targets):
    barrier = pltpu.get_barrier_semaphore()
    for target in targets:
        pl.semaphore_signal(barrier, inc=1, device_id=target, device_id_type=MESH)
    pl.semaphore_wait(barrier, len(targets))


def gather_kernel(s1, s2, s3, tok_in, grad_in, pack, cos_in, sin_in,
                  w1_out, w2_out, w3_out, normed_t_out, grad_t_out, unit_out, q_out, kv_out, kvr_out, do_out,
                  active_out, hidden_out, small_out, bias_out, up_bias_out,
                  w1, w2, w3, tok, grad, normed, grad_rel, normed_t, grad_t, unit, small, q, kv, do, active, slope,
                  hidden, cos, sin, bias_sum, up_bias_sum, send, recv, local):
    x, y, z, core = coords()
    x_lo, x_hi = lax.rem(x, 2), x // 2
    greet([beside(dy=1), beside(dy=3), beside(dy=2), beside(dx=1), beside(dx=3), beside(dx=2), beside(flip=1)])

    def remote(i, src, dst, target):
        copy = pltpu.make_async_remote_copy(src, dst, send.at[i], recv.at[i], device_id=target, device_id_type=MESH)
        copy.start()
        return copy

    def here(i, src, dst):
        copy = pltpu.make_async_copy(src, dst, local.at[i])
        copy.start()
        return copy

    shards, gathered = (s1, s2, s3), (w1, w2, w3)
    block = lambda w, j: w.at[pl.ds(j * BLK, BLK)]
    top = lambda w, j: w.at[pl.ds(j * BLK, BLK // 2)]
    bottom = lambda w, j: w.at[pl.ds(j * BLK + BLK // 2, BLK // 2)]

    def first_stage(g):
        s, w, at = shards[g], gathered[g], 8 + 9 * g
        own = here(g, s, block(w, 0))
        along_y = [
            remote(at, s, block(w, 3), beside(dy=1)),
            remote(at + 1, s, block(w, 1), beside(dy=3)),
            remote(at + 2, s, block(w, 2), beside(dy=2)),
        ]
        along_x = [
            remote(at + 3, s.at[pl.ds(0, BLK // 2)], top(w, 4), beside(dx=1)),
            remote(at + 4, s.at[pl.ds(BLK // 2, BLK // 2)], bottom(w, 4), beside(dx=3)),
        ]
        return own, along_y, along_x

    def second_stage(g, along_y):
        w, at = gathered[g], 8 + 9 * g + 5
        for copy in along_y:
            copy.wait_recv()
        return [
            remote(at, block(w, 1), block(w, 5), beside(dx=1)),
            remote(at + 1, block(w, 3), block(w, 7), beside(dx=3)),
            remote(at + 2, top(w, 2), top(w, 6), beside(dx=1)),
            remote(at + 3, bottom(w, 2), bottom(w, 6), beside(dx=3)),
        ]

    def arrived(own, along_x, second):
        own.wait()
        for copy in along_x + second:
            copy.wait_recv()

    my_rows = pl.ds(pl.multiple_of(core * HALF, HALF), HALF)
    pack_y = [
        remote(0, pack, small.at[3], beside(dy=1)),
        remote(1, pack, small.at[1], beside(dy=3)),
        remote(2, pack, small.at[2], beside(dy=2)),
    ]
    pack_own = here(3, pack, small.at[0])
    tok_copy = remote(4, tok_in, tok.at[my_rows], beside(flip=1))
    grad_copy = remote(5, grad_in, grad.at[my_rows], beside(flip=1))
    mine = [here(4, tok_in, tok.at[my_rows]), here(5, grad_in, grad.at[my_rows]), here(6, cos_in, cos), here(7, sin_in, sin)]
    own1, y1, x1 = first_stage(0)
    for copy in pack_y:
        copy.wait_recv()
    pack_own.wait()
    pack_x = remote(3, small.at[pl.ds(0, 4)], small.at[pl.ds(4, 4)], beside(dx=1))
    for copy in mine:
        copy.wait()
    tok_copy.wait_recv()
    grad_copy.wait_recv()
    pack_x.wait_recv()

    bias_sum[...] = jnp.zeros_like(bias_sum)
    up_bias_sum[...] = jnp.zeros_like(up_bias_sum)
    tile = 128

    @pl.loop(0, ROWS // tile)
    def _(i):
        at = pl.ds(pl.multiple_of(i * tile, tile), tile)
        rows = tok[at, :].astype(F32)
        mean = jnp.mean(rows, axis=-1, keepdims=True)
        centered = rows - mean
        inv = lax.rsqrt(jnp.mean(centered * centered, axis=-1, keepdims=True) + EPSILON)
        for j in range(8):
            src = pl.ds(pl.multiple_of(block_order(y, x_lo, j) * BLK, BLK), BLK)
            dst = pl.ds(j * BLK, BLK)
            gain = jnp.concatenate([small[j, 0:1, :], small[j, 1:2, :]], axis=1)
            shift = jnp.concatenate([small[j, 2:3, :], small[j, 3:4, :]], axis=1)
            u = (tok[at, src].astype(F32) - mean) * inv
            n = u * gain + shift
            normed[at, dst] = n.astype(BF16)
            normed_t[dst, at] = n.T.astype(BF16)
            unit[at, dst] = u.astype(BF16)
            g = grad[at, src]
            g32 = g.astype(F32)
            grad_rel[at, dst] = g
            grad_t[dst, at] = g32.T.astype(BF16)
            bias_sum[:, dst] += jnp.sum(g32, axis=0, keepdims=True)

    saved = [here(8, normed_t, normed_t_out), here(9, grad_t, grad_t_out), here(10, unit, unit_out), here(11, small, small_out),
             here(12, bias_sum, bias_out)]
    second1 = second_stage(0, y1)
    own2, y2, x2 = first_stage(1)
    arrived(own1, x1, second1)
    second2 = second_stage(1, y2)
    own3, y3, x3 = first_stage(2)
    saved.append(here(13, w1, w1_out))

    biases = small[0, 6:20, :]
    for j in range(1, 8):
        biases = biases + small[j, 6:20, :]
    qkv_bias = jnp.concatenate([biases[j : j + 1] for j in range(6)], axis=1)
    up_bias = jnp.concatenate([biases[j : j + 1] for j in range(6, 14)], axis=1)
    big = 256

    @pl.loop(0, ROWS // big)
    def _(i):
        at = pl.ds(pl.multiple_of(i * big, big), big)
        raw = jnp.dot(normed[at, :], w1[:, : 3 * BLK], preferred_element_type=F32) + qkv_bias
        c, s = cos[at, :], sin[at, :]
        qr, kr = raw[:, :BLK], raw[:, BLK : 2 * BLK]
        q[at, :] = ((qr * c + partner(qr) * s).astype(BF16).astype(F32) * (HD**-0.5)).astype(BF16)
        kv[at, :BLK] = (kr * c + partner(kr) * s).astype(BF16)
        kv[at, BLK:] = raw[:, 2 * BLK :].astype(BF16)
        do[at, :] = jnp.dot(grad_rel[at, :], w1[:, 3 * BLK :], preferred_element_type=F32).astype(BF16)

    kv_copy = pltpu.make_async_remote_copy(
        kv, kvr_out, send.at[6], recv.at[6], device_id=beside(dx=2), device_id_type=MESH
    )

    @pl.when(x_hi == 0)
    def _():
        kv_copy.start()

    saved += [here(14, q, q_out), here(15, kv, kv_out), here(16, do, do_out)]
    arrived(own2, x2, second2)
    second3 = second_stage(2, y3)
    saved.append(here(17, w2, w2_out))

    @pl.loop(0, ROWS // big)
    def _(i):
        at = pl.ds(pl.multiple_of(i * big, big), big)
        v = jnp.dot(normed[at, :], w2[...], preferred_element_type=F32) + up_bias
        sq = v * v
        t = jnp.tanh(GELU_C * v * (1.0 + 0.044715 * sq))
        half = 0.5 * (1.0 + t)
        active[at, :] = (v * half).astype(BF16)
        slope[at, :] = (half + 0.5 * v * (1.0 - t * t) * (GELU_C * (1.0 + 3 * 0.044715 * sq))).astype(BF16)

    saved.append(here(18, active, active_out))
    arrived(own3, x3, second3)
    saved.append(here(19, w3, w3_out))

    @pl.loop(0, ROWS // big)
    def _(i):
        at = pl.ds(pl.multiple_of(i * big, big), big)
        v = jnp.dot(grad_rel[at, :], w3[...], preferred_element_type=F32) * slope[at, :].astype(F32)
        low = v.astype(BF16)
        hidden[at, :] = low
        up_bias_sum[...] += jnp.sum(low.astype(F32), axis=0, keepdims=True)

    saved += [here(20, hidden, hidden_out), here(21, up_bias_sum, up_bias_out)]
    for copy in pack_y + [pack_x, tok_copy, grad_copy] + y1 + x1 + second1 + y2 + x2 + second2 + y3 + x3 + second3:
        copy.wait_send()

    @pl.when(x_hi == 0)
    def _():
        kv_copy.wait_send()

    @pl.when(x_hi == 1)
    def _():
        kv_copy.wait_recv()

    for copy in saved:
        copy.wait()


def gather_call(s1, s2, s3, tok, grad, pack, cos, sin):
    n = 1024
    low = lambda *shape: jax.ShapeDtypeStruct(shape, BF16)
    wide = lambda *shape: jax.ShapeDtypeStruct(shape, F32)
    vlow = lambda *shape: pltpu.VMEM(shape, BF16)
    vwide = lambda *shape: pltpu.VMEM(shape, F32)
    anywhere = pl.BlockSpec(memory_space=pl.ANY)
    return pl.pallas_call(
        gather_kernel,
        in_specs=[anywhere] * 8,
        out_specs=[anywhere] * 15,
        out_shape=[
            low(D, n), low(D, n), low(D, n), low(D, ROWS), low(D, ROWS), low(ROWS, D), low(ROWS, BLK), low(ROWS, 2 * BLK),
            low(ROWS, 2 * BLK), low(ROWS, BLK), low(ROWS, n), low(ROWS, n), wide(8, PACK, 128), wide(1, D), wide(1, n),
        ],
        scratch_shapes=[
            vlow(D, n), vlow(D, n), vlow(D, n), vlow(ROWS, D), vlow(ROWS, D), vlow(ROWS, D), vlow(ROWS, D), vlow(D, ROWS),
            vlow(D, ROWS), vlow(ROWS, D), vwide(8, PACK, 128), vlow(ROWS, BLK), vlow(ROWS, 2 * BLK), vlow(ROWS, BLK),
            vlow(ROWS, n), vlow(ROWS, n), vlow(ROWS, n), vwide(ROWS, BLK), vwide(ROWS, BLK), vwide(1, D), vwide(1, n),
            pltpu.SemaphoreType.DMA((35,)),
            pltpu.SemaphoreType.DMA((35,)),
            pltpu.SemaphoreType.DMA((22,)),
        ],
        compiler_params=params(collective_id=0, has_side_effects=True),
        cost_estimate=cost(2 * ROWS * D * 3 * n, 64 * 1024 * 1024),
        name="gather_phase",
    )(s1, s2, s3, tok, grad, pack, cos, sin)


class Copies:
    def __init__(self, send, recv, local):
        self.send, self.recv, self.local = send, recv, local
        self.remotes = self.locals = 0
        self.sent = []

    def make(self, src, dst, target):
        i = self.remotes
        self.remotes += 1
        return pltpu.make_async_remote_copy(
            src, dst, self.send.at[i], self.recv.at[i], device_id=target, device_id_type=MESH
        )

    def remote(self, src, dst, target):
        copy = self.make(src, dst, target)
        copy.start()
        self.sent.append(copy)
        return copy

    def here(self, src, dst):
        copy = pltpu.make_async_copy(src, dst, self.local.at[self.locals])
        self.locals += 1
        copy.start()
        return copy


def weight_blocks(base, step, lefts, rights, adds, out):
    m, n = out.shape[0], len(lefts)

    def inner(*refs):
        dst, at = refs[-1], 0
        for left, right in zip(refs[:n], rights):
            width = right.shape[1]
            total = jnp.dot(left[...], right[...], preferred_element_type=F32)
            for add in refs[n:-1]:
                total += add[0, :, at : at + width].astype(F32)
            dst[0, :, at : at + width] = total.astype(BF16)
            at += width

    pltpu.emit_pipeline(
        inner,
        grid=(m,),
        in_specs=[pl.BlockSpec((BLK, ROWS), lambda j: (base + step * j, 0)) for _ in lefts]
        + [pl.BlockSpec((1, BLK, 1024), lambda j, k=k: (k + j, 0, 0)) for _, k in adds],
        out_specs=[pl.BlockSpec((1, BLK, 1024), lambda j: (j, 0, 0))],
    )(*lefts, *[ref for ref, _ in adds], out)


def add_blocks(parts, out):
    def inner(*refs):
        total = refs[0][...].astype(F32)
        for ref in refs[1:-1]:
            total += ref[...].astype(F32)
        refs[-1][...] = total.astype(BF16)

    spec = pl.BlockSpec((1, BLK // 2, 1024), lambda j: (0, j, 0))
    pltpu.emit_pipeline(inner, grid=(2,), in_specs=[spec] * len(parts), out_specs=[spec])(*parts, out)


def row_products(half, a, b, w1, col1, w2, out, wa, wb, sems, unit=None, ub=None, vec=None):
    nt = (((1,), (1,)), ((), ()))
    ka = a.shape[1]
    rows = pl.ds(pl.multiple_of(half * HALF, HALF), HALF)

    def fetch(j, slot):
        at = pl.ds(pl.multiple_of(j * BLK, BLK), BLK)
        found = [
            pltpu.make_async_copy(w1.at[at, pl.ds(col1, ka)], wa.at[slot, :, pl.ds(0, ka)], sems.at[slot, 0]),
            pltpu.make_async_copy(w2.at[at], wb.at[slot], sems.at[slot, 1]),
        ]
        if unit is not None:
            found.append(pltpu.make_async_copy(unit.at[rows, at], ub.at[slot], sems.at[slot, 2]))
        return found

    for copy in fetch(0, 0):
        copy.start()

    @pl.loop(0, 8)
    def _(j):
        slot = lax.rem(j, 2)
        for copy in fetch(j, slot):
            copy.wait()

        @pl.when(j < 7)
        def _():
            for copy in fetch(j + 1, 1 - slot):
                copy.start()

        total = lax.dot_general(a[rows, :], wa[slot, :, :ka], nt, preferred_element_type=F32)
        total += lax.dot_general(b[rows, :], wb[slot], nt, preferred_element_type=F32)
        out[:, pl.ds(pl.multiple_of(j * BLK, BLK), BLK)] = total.astype(BF16)
        if unit is not None:
            vec[j, 0:1, :] = jnp.sum(total * ub[slot].astype(F32), axis=0, keepdims=True)
            vec[j, 1:2, :] = jnp.sum(total, axis=0, keepdims=True)


def add_rows(mine, got):
    @pl.loop(0, 4)
    def _(i):
        at = pl.ds(pl.multiple_of(i * 128, 128), 128)
        mine[at, :] = (mine[at, :].astype(F32) + got[at, :].astype(F32)).astype(BF16)


def reduce_kernel(w1, w2, w3, normed_t, grad_t, unit, q_in, kv_in, kvr_in, do_in, active_in, hidden_in, small_in, bias_in,
                  up_bias_in, tok_in, grad_in, cos_in, sin_in, cos_r_in, sin_r_in,
                  layer_out, input_grad, piece1, piece2, piece3, vec_out,
                  a_s1, a_r1, a_s2, a_r2, a_m, a_x, a_f,
                  b_s1, b_r1, b_s2, b_r2, b_m, b_x, b_f,
                  c_s1, c_r1, c_s2, c_r2, c_m, c_x, c_f,
                  q, do, keys, vals, keys_t, vals_t, active, hidden, att, raw, small, cos, sin, cos_r, sin_r,
                  st, dp, dk, dv, qm, dom, out_t, dq_t, dkv_s, dkv_r, wa, wb, ub, theirs, br_m, br_c, br_z, br_o, ng_m, ng_c, ng_z, ng_o, tok, grad,
                  vec_t, vec_m, va, va_r, vb_r, units, my, my_r, mx, mx_r, last, last_r, bias_v, up_bias_v, vec_v, send, recv, local, sems):
    x, y, z, core = coords()
    x_lo, x_hi = lax.rem(x, 2), x // 2
    other = 1 - core
    up, down, far = beside(dy=1), beside(dy=3), beside(dy=2)
    right, left, over = beside(dx=1), beside(dx=3), beside(dx=2)
    mate = beside(flip=1)
    along = [beside(dz=1), beside(dz=2), beside(dz=3)]
    greet([up, down, far, right, left, over, mate] + along)
    copies = Copies(send, recv, local)
    here, remote = copies.here, copies.remote
    nt = (((1,), (1,)), ((), ()))

    load_active, load_hidden = here(active_in, active), here(hidden_in, hidden)
    loads = [here(q_in, q), here(do_in, do), here(small_in, small), here(cos_in, cos), here(sin_in, sin),
             here(cos_r_in, cos_r), here(sin_r_in, sin_r), here(bias_in, bias_v), here(up_bias_in, up_bias_v)]
    z_rows = pl.ds(pl.multiple_of(z * 128, 128), 128)
    loads += [here(tok_in.at[z_rows], tok), here(grad_in.at[z_rows], grad)]
    own_keys = pl.ds(pl.multiple_of(x_hi * ROWS, ROWS), ROWS)
    loads += [here(kv_in.at[:, pl.ds(0, BLK)], keys.at[own_keys]), here(kv_in.at[:, pl.ds(BLK, BLK)], vals.at[own_keys])]
    far_keys = pltpu.make_async_copy(kvr_in.at[:, pl.ds(0, BLK)], keys.at[pl.ds(0, ROWS)], local.at[copies.locals])
    far_vals = pltpu.make_async_copy(kvr_in.at[:, pl.ds(BLK, BLK)], vals.at[pl.ds(0, ROWS)], local.at[copies.locals + 1])
    copies.locals += 2

    @pl.when(x_hi == 1)
    def _():
        far_keys.start()
        far_vals.start()

    load_active.wait()
    weight_blocks(4, 1, [grad_t], [active], [], a_s1.at[pl.ds(0, 2)])
    a1 = remote(a_s1.at[pl.ds(0, 2)], a_r1.at[pl.ds(0, 2)], right)
    weight_blocks(6, 1, [grad_t], [active], [], a_s1.at[pl.ds(2, 2)])
    a2 = remote(a_s1.at[pl.ds(2, 2)], a_r1.at[pl.ds(2, 2)], left)

    load_hidden.wait()

    def along_y_first(lefts, rights, s1, r1):
        sends = []
        for k, (base, target) in enumerate(((2, far), (1, up), (3, down))):
            part = pl.ds(2 * k, 2)
            weight_blocks(base, 4, lefts, rights, [], s1.at[part])
            sends.append(remote(s1.at[part], r1.at[part], target))
        return sends

    def then_x(lefts, rights, first, r1, s2, r2):
        for copy in first:
            copy.wait_recv()
        weight_blocks(4, 1, lefts, rights, [(r1, 1), (r1, 3), (r1, 5)], s2)
        upper, lower = pl.ds(0, BLK // 2), pl.ds(BLK // 2, BLK // 2)
        return [remote(s2.at[0, upper], r2.at[0, upper], right), remote(s2.at[0, lower], r2.at[0, lower], left)]

    def then_over(lefts, rights, second, r1, r2, m, got):
        for copy in second:
            copy.wait_recv()
        weight_blocks(0, 1, lefts, rights, [(r1, 0), (r1, 2), (r1, 4), (r2, 0)], m)
        return remote(m, got, over)

    def to_both(third, m, got, final, piece):
        third.wait_recv()
        add_blocks([m, got], final)
        spot = piece.at[pl.ds(core, 1)]
        return here(final, spot), remote(final, spot, mate)

    b1 = along_y_first([normed_t], [hidden], b_s1, b_r1)

    for copy in loads:
        copy.wait()

    @pl.when(x_hi == 1)
    def _():
        far_keys.wait()
        far_vals.wait()

    @pl.loop(0, (x_hi + 1) * (ROWS // KC))
    def _(j):
        at = pl.ds(pl.multiple_of(j * KC, KC), KC)
        keys_t[:, at] = keys[at, :].astype(F32).T.astype(BF16)
        vals_t[:, at] = vals[at, :].astype(F32).T.astype(BF16)
        dk[at, :] = jnp.zeros((KC, BLK), F32)
        dv[at, :] = jnp.zeros((KC, BLK), F32)

    out_t[...] = jnp.zeros_like(out_t)
    dq_t[...] = jnp.zeros_like(dq_t)

    def head(pair, side):
        lanes = slice(pair * 128, pair * 128 + 128)
        hrows = slice((2 * pair + side) * HD, (2 * pair + side + 1) * HD)
        trows = slice(side * HD, (side + 1) * HD)
        for t in range(ROWS // QT):
            rows = slice(t * QT, (t + 1) * QT)
            chunks = x_hi * (ROWS // KC) + (t + 1) * (QT // KC)
            mine = lax.broadcasted_iota(jnp.int32, (QT, 128), 1) // HD == side
            qm[...] = jnp.where(mine, q[rows, lanes], jnp.zeros((), BF16))
            dom[...] = jnp.where(mine, do[rows, lanes], jnp.zeros((), BF16))

            def score(j, top, masked):
                at = pl.ds(pl.multiple_of(j * KC, KC), KC)
                s = lax.dot_general(keys[at, lanes], qm[...], nt, preferred_element_type=F32)
                if masked:
                    ki = lax.broadcasted_iota(jnp.int32, (KC, QT), 0)
                    qi = lax.broadcasted_iota(jnp.int32, (KC, QT), 1)
                    s = jnp.where(ki <= qi, s, MASKED)
                st[at, :] = s
                return jnp.maximum(top, jnp.max(s, axis=0, keepdims=True))

            top = lax.fori_loop(0, chunks - 1, lambda j, m: score(j, m, False), jnp.full((1, QT), MASKED, F32))
            top = score(chunks - 1, top, True)

            def weigh(j, carry):
                total, dot = carry
                at = pl.ds(pl.multiple_of(j * KC, KC), KC)
                p = jnp.exp(st[at, :] - top)
                st[at, :] = p
                d = lax.dot_general(vals[at, lanes], dom[...], nt, preferred_element_type=F32)
                dp[at, :] = d
                return total + jnp.sum(p, axis=0, keepdims=True), dot + jnp.sum(p * d, axis=0, keepdims=True)

            zero = jnp.zeros((1, QT), F32)
            total, dot = lax.fori_loop(0, chunks, weigh, (zero, zero))
            inv = 1.0 / total
            delta = dot * inv

            def spread(j, _):
                at = pl.ds(pl.multiple_of(j * KC, KC), KC)
                p = st[at, :] * inv
                low = p.astype(BF16)
                ds = (p * (dp[at, :] - delta)).astype(BF16)
                out_t[trows, rows] += jnp.dot(vals_t[hrows, at], low, preferred_element_type=F32)
                dq_t[trows, rows] += jnp.dot(keys_t[hrows, at], ds, preferred_element_type=F32)
                dv[at, lanes] += jnp.dot(low, dom[...], preferred_element_type=F32)
                dk[at, lanes] += jnp.dot(ds, qm[...], preferred_element_type=F32)
                return 0

            lax.fori_loop(0, chunks, spread, 0)

    def turn_back(v, c, s):
        return v * c - partner(v) * s

    def end_pair(pair):
        lanes = slice(pair * 128, pair * 128 + 128)
        for t in range(ROWS // QT):
            rows = slice(t * QT, (t + 1) * QT)
            att[rows, lanes] = out_t[:, rows].T.astype(BF16)
            raw[rows, lanes] = turn_back(dq_t[:, rows].T * (HD**-0.5), cos[rows, :], sin[rows, :]).astype(BF16)
        out_t[...] = jnp.zeros_like(out_t)
        dq_t[...] = jnp.zeros_like(dq_t)
        copy = copies.make(dkv_s.at[pair], dkv_r.at[pair], over)

        @pl.when(x_hi == 1)
        def _():
            dkv_s[pair, :, :128] = turn_back(dk[:ROWS, lanes], cos_r[...], sin_r[...]).astype(BF16)
            dkv_s[pair, :, 128:] = dv[:ROWS, lanes].astype(BF16)
            copy.start()

        return copy

    head(0, 0)
    a1.wait_recv()
    a2.wait_recv()
    weight_blocks(2, 1, [grad_t], [active], [(a_r1, 2)], a_s2.at[pl.ds(0, 2)])
    weight_blocks(1, 1, [grad_t], [active], [(a_r1, 1)], a_s2.at[pl.ds(2, 1)])
    a_y = [
        remote(a_s2.at[pl.ds(0, 1)], a_r2.at[pl.ds(0, 1)], far),
        remote(a_s2.at[pl.ds(1, 1)], a_r2.at[pl.ds(1, 1)], down),
        remote(a_s2.at[pl.ds(2, 1)], a_r2.at[pl.ds(2, 1)], up),
    ]
    head(0, 1)
    pair0 = end_pair(0)
    head(1, 0)
    b2 = then_x([normed_t], [hidden], b1, b_r1, b_s2, b_r2)
    head(1, 1)
    pair1 = end_pair(1)

    row_products(other, att, active, w1, 3 * BLK, w3, theirs, wa, wb, sems)
    br_core = remote(theirs, br_c, mate)
    row_products(core, att, active, w1, 3 * BLK, w3, br_m, wa, wb, sems)
    for copy in a_y:
        copy.wait_recv()
    weight_blocks(0, 1, [grad_t], [active], [(a_r1, 0), (a_r2, 0), (a_r2, 1), (a_r2, 2)], a_m)
    a3 = remote(a_m, a_x, over)

    def to_z(total, got):
        out = []
        for k in range(3):
            rows = pl.ds(pl.multiple_of(lax.rem(z + k + 1, 4) * 128, 128), 128)
            out.append(remote(total.at[rows], got.at[k], along[k]))
        return out

    def from_z(chunk, whole_rows):
        rows = pl.ds(pl.multiple_of(z * 128, 128), 128)
        return here(chunk, whole_rows.at[rows]), [remote(chunk, whole_rows.at[rows], target) for target in along]

    br_core.wait_recv()
    add_rows(br_m, br_c)
    br_sent = to_z(br_m, br_z)

    def local_grads(pair, more):
        lanes = slice(pair * 128, pair * 128 + 128)
        k = turn_back(dk[own_keys, lanes], cos[...], sin[...])
        v = dv[own_keys, lanes]
        if more:
            k = k + dkv_r[pair, :, :128].astype(F32)
            v = v + dkv_r[pair, :, 128:].astype(F32)
        raw[:, BLK + pair * 128 : BLK + pair * 128 + 128] = k.astype(BF16)
        raw[:, 2 * BLK + pair * 128 : 2 * BLK + pair * 128 + 128] = v.astype(BF16)

    for pair, copy in enumerate((pair0, pair1)):

        @pl.when(x_hi == 1)
        def _():
            local_grads(pair, False)
            copy.wait_send()

        @pl.when(x_hi == 0)
        def _():
            copy.wait_recv()
            local_grads(pair, True)

    br_core.wait_send()
    copies.sent = [copy for copy in copies.sent if copy is not br_core]
    row_products(other, raw, hidden, w1, 0, w2, theirs, wa, wb, sems, unit, ub, vec_t)
    ng_core = remote(theirs, ng_c, mate)
    row_products(core, raw, hidden, w1, 0, w2, ng_m, wa, wb, sems, unit, ub, vec_m)
    pair_left, pair_right = [normed_t, grad_t], [raw, att]
    c1 = along_y_first(pair_left, pair_right, c_s1, c_r1)
    ng_core.wait_recv()
    add_rows(ng_m, ng_c)
    ng_sent = to_z(ng_m, ng_z)

    va[...] = jnp.zeros_like(va)
    for j in range(8):
        va[j, 0:2, :] = vec_t[j, 0:2, :] + vec_m[j, 0:2, :]
    va_sent = [remote(va, va_r.at[k], along[k]) for k in range(3)]

    for copy in b2:
        copy.wait_recv()
    b3 = then_over([normed_t], [hidden], [], b_r1, b_r2, b_m, b_x)
    a4 = to_both(a3, a_m, a_x, a_f, piece3)

    for copy in br_sent:
        copy.wait_recv()

    tile = 32

    def share(total, got, i, j):
        at = pl.ds(pl.multiple_of(i * tile, tile), tile)
        from_all = pl.ds(pl.multiple_of(z * 128 + i * tile, tile), tile)
        cols = slice(j * BLK, (j + 1) * BLK)
        return (total[from_all, cols].astype(F32) + got[1, at, cols].astype(F32)) + (
            got[0, at, cols].astype(F32) + got[2, at, cols].astype(F32)
        )

    def line(row, j):
        return jnp.concatenate([small[j, row : row + 1, :], small[j, row + 1 : row + 2, :]], axis=1)

    def spot(j):
        return pl.ds(pl.multiple_of(block_order(y, x_lo, j) * BLK, BLK), BLK)

    @pl.loop(0, 128 // tile)
    def _(i):
        at = pl.ds(pl.multiple_of(i * tile, tile), tile)
        for j in range(8):
            value = tok[at, spot(j)].astype(F32) + share(br_m, br_z, i, j) + line(4, j)
            br_o[at, spot(j)] = value.astype(BF16)

    br_own, br_out = from_z(br_o, layer_out)

    for copy in va_sent:
        copy.wait_recv()
    va_total = (va[...] + va_r[1]) + (va_r[0] + va_r[2])
    vec_v[0] = va_total
    vb = remote(vec_v.at[0], vb_r, mate)

    for copy in ng_sent:
        copy.wait_recv()

    @pl.loop(0, 128 // tile)
    def _(i):
        at = pl.ds(pl.multiple_of(i * tile, tile), tile)
        rows = tok[at, :].astype(F32)
        mean = jnp.mean(rows, axis=-1, keepdims=True)
        centered = rows - mean
        inv = lax.rsqrt(jnp.mean(centered * centered, axis=-1, keepdims=True) + EPSILON)

        def terms(j):
            u = (tok[at, spot(j)].astype(F32) - mean) * inv
            return u, share(ng_m, ng_z, i, j) * line(0, j)

        first = second = jnp.zeros((tile, 1), F32)
        for j in range(8):
            u, g = terms(j)
            first += jnp.sum(g, axis=-1, keepdims=True)
            second += jnp.sum(g * u, axis=-1, keepdims=True)
        first, second = first / D, second / D
        for j in range(8):
            u, g = terms(j)
            ng_o[at, spot(j)] = (grad[at, spot(j)].astype(F32) + inv * (g - first - u * second)).astype(BF16)

    ng_own, ng_out = from_z(ng_o, input_grad)

    vb.wait_recv()
    units[...] = jnp.zeros_like(units)
    units[0:3, :] = jnp.sum(raw[...].astype(F32), axis=0, keepdims=True).reshape(3, BLK)
    for j in range(4):
        units[3 + j : 4 + j, :] = up_bias_v[:, j * BLK : (j + 1) * BLK]
    for j in range(8):
        dy, dx = j % 4, j // 4
        my[dy, dx] = vec_v[0, j] + vb_r[j]
        my[dy, dx, 2:3, :] = bias_v[:, j * BLK : (j + 1) * BLK]
    for dy in range(4):
        my[dy, 2] = units[...]
    my_sent = [remote(my.at[1], my_r.at[0], up), remote(my.at[2], my_r.at[1], far), remote(my.at[3], my_r.at[2], down)]

    c2 = then_x(pair_left, pair_right, c1, c_r1, c_s2, c_r2)
    b4 = to_both(b3, b_m, b_x, b_f, piece2)

    for copy in my_sent:
        copy.wait_recv()
    here_sum = (my[0] + my_r[1]) + (my_r[0] + my_r[2])
    mx[0, 0] = here_sum[0]
    mx[0, 1] = here_sum[2]
    mx[1, 0] = here_sum[1]
    mx[1, 1] = here_sum[2]
    mx_sent = [remote(mx.at[1], mx_r.at[0], right), remote(mx.at[0], mx_r.at[1], over), remote(mx.at[1], mx_r.at[2], left)]

    c3 = then_over(pair_left, pair_right, c2, c_r1, c_r2, c_m, c_x)

    for copy in mx_sent:
        copy.wait_recv()
    last[...] = (mx[0] + mx_r[1]) + (mx_r[0] + mx_r[2])
    vec_copy = remote(last.at[1], last_r, mate)
    vec_copy.wait_recv()
    last_saved = [here(last, vec_out.at[pl.ds(0, 2)]), here(last_r, vec_out.at[2])]
    c4 = to_both(c3, c_m, c_x, c_f, piece1)

    for own, copy in (a4, b4, c4):
        own.wait()
        copy.wait_recv()
    br_own.wait()
    ng_own.wait()
    for copy in br_out + ng_out:
        copy.wait_recv()
    for copy in last_saved:
        copy.wait()
    for copy in copies.sent:
        copy.wait_send()


def reduce_call(*args):
    low = lambda *shape: jax.ShapeDtypeStruct(shape, BF16)
    wide = lambda *shape: jax.ShapeDtypeStruct(shape, F32)
    vlow = lambda *shape: pltpu.VMEM(shape, BF16)
    vwide = lambda *shape: pltpu.VMEM(shape, F32)
    anywhere = pl.BlockSpec(memory_space=pl.ANY)
    blocks = lambda m: low(m, BLK, 1024)
    x_first = [blocks(4), blocks(4), blocks(3), blocks(3), blocks(1), blocks(1), blocks(1)]
    y_first = [blocks(6), blocks(6), blocks(1), blocks(1), blocks(1), blocks(1), blocks(1)]
    outs = (
        [low(HALF, D), low(HALF, D), blocks(2), blocks(2), blocks(2), wide(3, 8, BLK)]
        + x_first + y_first + y_first
    )
    result = pl.pallas_call(
        reduce_kernel,
        in_specs=[anywhere] * 21,
        out_specs=[anywhere] * len(outs),
        out_shape=outs,
        scratch_shapes=[
            vlow(ROWS, BLK), vlow(ROWS, BLK), vlow(2 * ROWS, BLK), vlow(2 * ROWS, BLK), vlow(BLK, 2 * ROWS),
            vlow(BLK, 2 * ROWS), vlow(ROWS, 1024), vlow(ROWS, 1024), vlow(ROWS, BLK), vlow(ROWS, 3 * BLK),
            vwide(8, PACK, 128), vwide(ROWS, 128), vwide(ROWS, 128), vwide(ROWS, 128), vwide(ROWS, 128),
            vwide(2 * ROWS, QT), vwide(2 * ROWS, QT), vwide(2 * ROWS, BLK), vwide(2 * ROWS, BLK), vlow(QT, 128),
            vlow(QT, 128), vwide(128, ROWS), vwide(128, ROWS), vlow(2, ROWS, BLK), vlow(2, ROWS, BLK), vlow(2, BLK, 3 * BLK),
            vlow(2, BLK, 1024), vlow(2, HALF, BLK), vlow(HALF, D), vlow(HALF, D), vlow(HALF, D), vlow(3, 128, D), vlow(128, D),
            vlow(HALF, D), vlow(HALF, D), vlow(3, 128, D), vlow(128, D), vlow(128, D), vlow(128, D),
            vwide(8, 8, BLK), vwide(8, 8, BLK),
            vwide(8, 8, BLK), vwide(3, 8, 8, BLK), vwide(8, 8, BLK), vwide(8, BLK), vwide(4, 3, 8, BLK),
            vwide(3, 3, 8, BLK), vwide(2, 2, 8, BLK), vwide(3, 2, 8, BLK), vwide(2, 8, BLK), vwide(8, BLK),
            vwide(1, D), vwide(1, 1024), vwide(2, 8, 8, BLK),
            pltpu.SemaphoreType.DMA((64,)),
            pltpu.SemaphoreType.DMA((64,)),
            pltpu.SemaphoreType.DMA((32,)),
            pltpu.SemaphoreType.DMA((2, 3)),
        ],
        compiler_params=params(collective_id=1, has_side_effects=True),
        cost_estimate=cost(2 * ROWS * D * 5 * 1024, 128 * 1024 * 1024),
        name="reduce_phase",
    )(*args)
    return result[:6]


def body(tokens, ln_gain, ln_shift, out_bias, w_qkv, b_qkv, w_out, w_fc1, b_fc1, w_fc2, out_grad):
    f, c = lax.axis_index("fsdp"), lax.axis_index("ctx")
    x_hi, core = c // 2, c % 2
    tokens, out_grad = tokens[0], out_grad[0]

    qkv_shard = lax.dynamic_slice_in_dim(w_qkv, core * BLK, BLK, axis=2).reshape(BLK, 3 * BLK)
    proj_shard = lax.dynamic_slice_in_dim(w_out, core * BLK, BLK, axis=0).T
    attn_shard = jnp.concatenate([qkv_shard, proj_shard], axis=1)
    up_shard = lax.dynamic_slice_in_dim(w_fc1, core * 1024, 1024, axis=1)
    down_shard = lax.dynamic_slice_in_dim(w_fc2, core * 1024, 1024, axis=0).T

    own = (jnp.arange(HD) // 8 == f)[None, None, :]
    spread = lambda v: jnp.where(own, jnp.tile(v, (1, 1, 8)), jnp.zeros((), BF16)).reshape(-1)
    pack = jnp.concatenate(
        [
            ln_gain,
            ln_shift,
            out_bias,
            spread(lax.dynamic_slice_in_dim(b_qkv, core * 4, 4, axis=1)),
            spread(lax.dynamic_slice_in_dim(b_fc1, core * 16, 16, axis=0)[None]),
            jnp.zeros((512,), BF16),
        ]
    )
    pack = pack.astype(F32).reshape(PACK, 128)

    lane = jnp.arange(BLK, dtype=jnp.int32) % HD
    freq = jnp.where(lane < ROT, 10000.0 ** (-2.0 * (lane % (ROT // 2)).astype(F32) / ROT), 0.0)
    sign = jnp.where(lane < ROT // 2, -1.0, 1.0)

    def tables(first):
        angle = (first + jnp.arange(ROWS, dtype=jnp.int32)).astype(F32)[:, None] * freq[None, :]
        return jnp.cos(angle), jnp.sin(angle) * sign[None, :]

    cos_r, sin_r = tables(0)
    cos, sin = tables(x_hi * ROWS)

    (w_attn, w_up, w_down, normed_t, grad_t, unit, q, kv, kvr, do, active, hidden_grad, small, bias_grad, up_bias_grad) = (
        gather_call(attn_shard, up_shard, down_shard, tokens, out_grad, pack, cos, sin)
    )
    half = lambda table: table[:, :128]
    layer_out, input_grad, attn_all, up_all, down_all, vec = reduce_call(
        w_attn, w_up, w_down, normed_t, grad_t, unit, q, kv, kvr, do, active, hidden_grad, small, bias_grad, up_bias_grad,
        tokens, out_grad, half(cos), half(sin), half(cos_r), half(sin_r)
    )
    gain_grad, shift_grad, out_bias_grad = vec[0, 0], vec[0, 1], vec[0, 2]
    units = jnp.where(core == 0, vec[1:], vec[:0:-1]).reshape(2, 8 * BLK)
    qkv_bias_out = lax.dynamic_slice_in_dim(
        units[:, : 3 * BLK].reshape(2, 3, 4, HD).transpose(1, 0, 2, 3).reshape(3, 8, HD), f * 8, 8, axis=2
    )
    up_bias_out = lax.dynamic_slice_in_dim(units[:, 3 * BLK : 7 * BLK].reshape(32, HD), f * 8, 8, axis=1)
    qkv_out = attn_all[:, :, : 3 * BLK].reshape(2, BLK, 3, BLK).transpose(1, 2, 0, 3).reshape(BLK, 3, HALF)
    proj_out = attn_all[:, :, 3 * BLK :].transpose(0, 2, 1).reshape(HALF, BLK)
    up_out = up_all.transpose(1, 0, 2).reshape(BLK, 2048)
    down_out = down_all.transpose(0, 2, 1).reshape(2048, BLK)
    return (
        layer_out[None],
        input_grad[None],
        gain_grad,
        shift_grad,
        out_bias_grad,
        qkv_out.astype(F32),
        qkv_bias_out,
        proj_out.astype(F32),
        up_out.astype(F32),
        up_bias_out,
        down_out.astype(F32),
    )


def solution(mesh):
    in_specs = (
        P("fsdp", "ctx", None),
        P("fsdp"),
        P("fsdp"),
        P("fsdp"),
        P("fsdp", None, "tp"),
        P(None, "tp", "fsdp"),
        P("tp", "fsdp"),
        P("fsdp", "tp"),
        P("tp", "fsdp"),
        P("tp", "fsdp"),
        P("fsdp", "ctx", None),
    )
    out_specs = (
        P("fsdp", "ctx", None),
        P("fsdp", "ctx", None),
        P("fsdp"),
        P("fsdp"),
        P("fsdp"),
        P("fsdp", None, "tp"),
        P(None, "tp", "fsdp"),
        P("tp", "fsdp"),
        P("fsdp", "tp"),
        P("tp", "fsdp"),
        P("tp", "fsdp"),
    )
    return jax.shard_map(body, mesh=mesh, in_specs=in_specs, out_specs=out_specs, check_vma=False)
```

```python
import math

import jax
import jax.numpy as jnp
import numpy as np
from jax import lax
from jax.experimental import pallas as pl
from jax.experimental.pallas import tpu as pltpu
from jax.sharding import PartitionSpec as P

D = 2048
HD = 64
ROT = 32
BLK = 256
ROWS = 1024
HALF = 512
EPSILON = 1e-05
MASKED = -1e30
F32 = jnp.float32
BF16 = jnp.bfloat16
VMEM_LIMIT = 62 * 1024 * 1024


def params(**kw):
    return pltpu.CompilerParams(vmem_limit_bytes=VMEM_LIMIT, **kw)


def whole():
    return pl.BlockSpec(memory_space=pltpu.VMEM)


def cost(flops, nbytes, trans=0):
    return pl.CostEstimate(flops=int(flops), bytes_accessed=int(nbytes), transcendentals=int(trans))


def block_order(y, x_lo, j):
    dx, dy = j // 4, j % 4
    return lax.rem(y + dy, 4) * 2 + lax.rem(x_lo + dx, 2)


def partner(v):
    lane = lax.broadcasted_iota(jnp.int32, v.shape, 1)
    up = pltpu.roll(v, v.shape[1] - ROT // 2, 1)
    down = pltpu.roll(v, ROT // 2, 1)
    return jnp.where(lane % HD < ROT // 2, up, down)


QT = 256
KC = 512


def rope_table():
    lane = np.arange(128) % HD
    freq = np.where(lane < ROT, 10000.0 ** (-2.0 * (lane % (ROT // 2)) / ROT), 0.0)
    sign = np.where(lane < ROT // 2, -1.0, 1.0)
    coarse, fine = np.arange(64)[:, None] * 32 * freq, np.arange(32)[:, None] * freq
    parts = [np.cos(coarse), np.sin(coarse) * sign, np.cos(fine), np.sin(fine) * sign]
    return np.concatenate(parts).astype(np.float32)


ROPE = rope_table()
GELU_C = math.sqrt(2.0 / math.pi)


MESH = pl.DeviceIdType.MESH
PACK = 24


def coords():
    f, c, z = lax.axis_index("fsdp"), lax.axis_index("ctx"), lax.axis_index("tp")
    return (c // 2) * 2 + f % 2, f // 2, z, c % 2


def device(x, y, z, core):
    return (y * 2 + lax.rem(x, 2), (x // 2) * 2 + core, z)


def beside(dx=0, dy=0, flip=0, dz=0):
    x, y, z, core = coords()
    return device(
        lax.rem(x + dx + 4, 4), lax.rem(y + dy + 4, 4), lax.rem(z + dz + 4, 4), (1 - core) if flip else core
    )


def greet(targets):
    barrier = pltpu.get_barrier_semaphore()
    for target in targets:
        pl.semaphore_signal(barrier, inc=1, device_id=target, device_id_type=MESH)
    pl.semaphore_wait(barrier, len(targets))


class Copies:
    def __init__(self, send, recv, local):
        self.send, self.recv, self.local = send, recv, local
        self.remotes = self.locals = 0
        self.sent = []

    def make(self, src, dst, target):
        i = self.remotes
        self.remotes += 1
        return pltpu.make_async_remote_copy(
            src, dst, self.send.at[i], self.recv.at[i], device_id=target, device_id_type=MESH
        )

    def remote(self, src, dst, target):
        copy = self.make(src, dst, target)
        copy.start()
        self.sent.append(copy)
        return copy

    def here(self, src, dst):
        copy = pltpu.make_async_copy(src, dst, self.local.at[self.locals])
        self.locals += 1
        copy.start()
        return copy


def rope_rows(table, first, cos, sin, count):
    @pl.loop(0, count // 32)
    def _(i):
        at = pl.ds(pl.multiple_of(i * 32, 32), 32)
        ch, sh = table[pl.ds(first // 32 + i, 1), :], table[pl.ds(64 + first // 32 + i, 1), :]
        cl, sl = table[128:160, :], table[160:192, :]
        cos[at, :] = ch * cl - sh * sl
        sin[at, :] = sh * cl + ch * sl


def turn(v, c, s):
    return v * c + partner(v) * s


def gather_kernel(s1_in, proj_in, up_in, down_in, tok_in, grad_in, pack, table_in,
                  w1_out, w2_out, w3_out, normed_t_out, grad_t_out, unit_out, q_out, kv_out, kvr_out, do_out,
                  active_out, hidden_out, small_out, bias_out, up_bias_out, a_s1_out, b_s1_out,
                  w1, w2, w3, tok, grad, normed, grad_rel, normed_t, grad_t, unit, small, q, kv, do, active, slope,
                  hidden, cos, sin, table, bias_sum, up_bias_sum, proj_v, down_v, send, recv, local):
    x, y, z, core = coords()
    x_lo, x_hi = lax.rem(x, 2), x // 2
    up, down, far = beside(dy=1), beside(dy=3), beside(dy=2)
    right, left, over, mate = beside(dx=1), beside(dx=3), beside(dx=2), beside(flip=1)
    copies = Copies(send, recv, local)
    here, remote = copies.here, copies.remote
    hcols = pl.ds(pl.multiple_of(core * 1024, 1024), 1024)
    hrows = pl.ds(pl.multiple_of(core * 1024, 1024), 1024)
    prows = pl.ds(pl.multiple_of(core * BLK, BLK), BLK)
    own_block = pl.ds(0, BLK)
    proj_load = here(proj_in.at[prows], proj_v)
    down_load = here(down_in.at[hrows], down_v)
    s1_load = here(s1_in, w1.at[own_block, pl.ds(0, 3 * BLK)])
    up_load = here(up_in.at[:, hcols], w2.at[own_block])
    greet([up, down, far, right, left, over, mate])

    class Part:
        def __init__(self, w, at, n):
            self.w, self.cols, self.moves = w, pl.ds(at, n), []

        def rows(self, j, first=0, count=BLK):
            return self.w.at[pl.ds(j * BLK + first, count), self.cols]

        def to(self, j, k, target, first=0, count=BLK):
            copy = remote(self.rows(j, first, count), self.rows(k, first, count), target)
            self.moves.append(copy)
            return copy

        def along_y(self, base):
            return [self.to(base, base + 3, up), self.to(base, base + 1, down), self.to(base, base + 2, far)]

        def sideways(self):
            return [self.to(0, 4, right, 0, BLK // 2), self.to(0, 4, left, BLK // 2, BLK // 2)]

        def start(self):
            self.y, self.x = self.along_y(0), self.sideways()

        def forward(self):
            for copy in self.y:
                copy.wait_recv()
            self.x += [
                self.to(1, 5, right), self.to(3, 7, left),
                self.to(2, 6, right, 0, BLK // 2), self.to(2, 6, left, BLK // 2, BLK // 2),
            ]

        def forward_y(self):
            for copy in self.x:
                copy.wait_recv()
            self.x = self.along_y(4)

        def arrived(self):
            for copy in self.x:
                copy.wait_recv()

        def all_arrived(self):
            for copy in self.y + self.x:
                copy.wait_recv()

    keys_part, rest_part = Part(w1, 0, 512), Part(w1, 512, 512)
    up_part = Part(w2, 0, 1024)
    down_a, down_b = Part(w3, 0, 512), Part(w3, 512, 512)

    my_rows = pl.ds(pl.multiple_of(core * HALF, HALF), HALF)
    pack_y = [remote(pack, small.at[3], up), remote(pack, small.at[1], down), remote(pack, small.at[2], far)]
    pack_own = here(pack, small.at[0])
    tok_copy = remote(tok_in, tok.at[my_rows], mate)
    grad_copy = remote(grad_in, grad.at[my_rows], mate)
    s1_load.wait()
    keys_part.start()
    mine = [here(tok_in, tok.at[my_rows]), here(grad_in, grad.at[my_rows])]
    table_load = here(table_in, table)

    proj_load.wait()
    w1[0:BLK, 3 * BLK :] = proj_v[...].astype(F32).T.astype(BF16)
    down_load.wait()
    for k in range(4):
        w3[0:BLK, k * BLK : (k + 1) * BLK] = down_v[k * BLK : (k + 1) * BLK, :].astype(F32).T.astype(BF16)
    table_load.wait()
    rope_rows(table, x_hi * ROWS, cos, sin, ROWS)
    for copy in pack_y:
        copy.wait_recv()
    pack_own.wait()
    pack_x = remote(small.at[pl.ds(0, 4)], small.at[pl.ds(4, 4)], right)
    for copy in mine:
        copy.wait()
    tok_copy.wait_recv()
    grad_copy.wait_recv()
    rest_part.start()
    pack_x.wait_recv()

    bias_sum[...] = jnp.zeros_like(bias_sum)
    up_bias_sum[...] = jnp.zeros_like(up_bias_sum)
    tile = 128

    def prepare(first, last):
        @pl.loop(first, last)
        def _(i):
            at = pl.ds(pl.multiple_of(i * tile, tile), tile)
            rows = tok[at, :].astype(F32)
            mean = jnp.mean(rows, axis=-1, keepdims=True)
            centered = rows - mean
            inv = lax.rsqrt(jnp.mean(centered * centered, axis=-1, keepdims=True) + EPSILON)
            for j in range(8):
                src = pl.ds(pl.multiple_of(block_order(y, x_lo, j) * BLK, BLK), BLK)
                dst = pl.ds(j * BLK, BLK)
                gain = jnp.concatenate([small[j, 0:1, :], small[j, 1:2, :]], axis=1)
                shift = jnp.concatenate([small[j, 2:3, :], small[j, 3:4, :]], axis=1)
                u = (tok[at, src].astype(F32) - mean) * inv
                n = u * gain + shift
                normed[at, dst] = n.astype(BF16)
                normed_t[dst, at] = n.T.astype(BF16)
                unit[at, dst] = u.astype(BF16)
                g = grad[at, src]
                g32 = g.astype(F32)
                grad_rel[at, dst] = g
                grad_t[dst, at] = g32.T.astype(BF16)
                bias_sum[:, dst] += jnp.sum(g32, axis=0, keepdims=True)

    prepare(0, 4)
    keys_part.forward()
    prepare(4, 8)
    up_load.wait()
    up_part.start()
    saved = [here(normed_t, normed_t_out), here(grad_t, grad_t_out), here(unit, unit_out), here(small, small_out),
             here(bias_sum, bias_out)]

    biases = small[0, 6:20, :]
    for j in range(1, 8):
        biases = biases + small[j, 6:20, :]
    qkv_bias = jnp.concatenate([biases[j : j + 1] for j in range(6)], axis=1)
    up_bias = jnp.concatenate([biases[j : j + 1] for j in range(6, 14)], axis=1)
    big = 256
    keys_part.arrived()

    @pl.loop(0, ROWS // big)
    def _(i):
        at = pl.ds(pl.multiple_of(i * big, big), big)
        raw = jnp.dot(normed[at, :], w1[:, : 2 * BLK], preferred_element_type=F32) + qkv_bias[:, : 2 * BLK]
        c, s = cos[at, :], sin[at, :]
        for k in range(2):
            lanes = slice(k * 128, (k + 1) * 128)
            kv[at, lanes] = turn(raw[:, lanes], c, s).astype(BF16)
        kv[at, BLK:] = raw[:, BLK:].astype(BF16)

    kv_copy = copies.make(kv, kvr_out, over)

    @pl.when(x_hi == 0)
    def _():
        kv_copy.start()

    rest_part.forward()
    saved.append(here(kv, kv_out))
    rest_part.arrived()
    saved.append(here(w1, w1_out))

    @pl.loop(0, ROWS // big)
    def _(i):
        at = pl.ds(pl.multiple_of(i * big, big), big)
        raw = jnp.dot(normed[at, :], w1[:, 2 * BLK : 3 * BLK], preferred_element_type=F32) + qkv_bias[:, 2 * BLK :]
        c, s = cos[at, :], sin[at, :]
        for k in range(2):
            lanes = slice(k * 128, (k + 1) * 128)
            q[at, lanes] = (turn(raw[:, lanes], c, s).astype(BF16).astype(F32) * (HD**-0.5)).astype(BF16)
        do[at, :] = jnp.dot(grad_rel[at, :], w1[:, 3 * BLK :], preferred_element_type=F32).astype(BF16)

    saved += [here(q, q_out), here(do, do_out)]
    up_part.forward()
    down_a.start()
    down_b.start()
    up_part.arrived()
    saved.append(here(w2, w2_out))

    @pl.loop(0, ROWS // big)
    def _(i):
        at = pl.ds(pl.multiple_of(i * big, big), big)
        v = jnp.dot(normed[at, :], w2[...], preferred_element_type=F32) + up_bias
        sq = v * v
        t = jnp.tanh(GELU_C * v * (1.0 + 0.044715 * sq))
        half = 0.5 * (1.0 + t)
        active[at, :] = (v * half).astype(BF16)
        slope[at, :] = (half + 0.5 * v * (1.0 - t * t) * (GELU_C * (1.0 + 3 * 0.044715 * sq))).astype(BF16)

    saved.append(here(active, active_out))
    down_b.forward_y()

    place = [buf.at[:, pl.ds(k * 1024, 1024)] for buf in (tok, grad) for k in range(2)]

    def partials(left, right, blocks, dst, out):
        for k, j in enumerate(blocks):
            at = pl.ds((k % 4) * BLK, BLK)
            dst[k // 4][at, :] = jnp.dot(left[j * BLK : (j + 1) * BLK, :], right[...], preferred_element_type=F32).astype(BF16)
            saved.append(here(dst[k // 4].at[at], out.at[k]))

    partials(grad_t, active, (4, 5, 6, 7), place[:1], a_s1_out)
    down_a.forward()
    down_a.arrived()
    down_b.all_arrived()
    saved.append(here(w3, w3_out))

    @pl.loop(0, ROWS // big)
    def _(i):
        at = pl.ds(pl.multiple_of(i * big, big), big)
        v = jnp.dot(grad_rel[at, :], w3[...], preferred_element_type=F32) * slope[at, :].astype(F32)
        low = v.astype(BF16)
        hidden[at, :] = low
        up_bias_sum[...] += jnp.sum(low.astype(F32), axis=0, keepdims=True)

    saved += [here(hidden, hidden_out), here(up_bias_sum, up_bias_out)]
    partials(normed_t, hidden, (2, 6, 1, 5, 3, 7), place[1:3], b_s1_out)
    for copy in copies.sent:
        copy.wait_send()

    @pl.when(x_hi == 0)
    def _():
        kv_copy.wait_send()

    @pl.when(x_hi == 1)
    def _():
        kv_copy.wait_recv()

    for copy in saved:
        copy.wait()


def gather_call(*args):
    n = 1024
    low = lambda *shape: jax.ShapeDtypeStruct(shape, BF16)
    wide = lambda *shape: jax.ShapeDtypeStruct(shape, F32)
    vlow = lambda *shape: pltpu.VMEM(shape, BF16)
    vwide = lambda *shape: pltpu.VMEM(shape, F32)
    anywhere = pl.BlockSpec(memory_space=pl.ANY)
    return pl.pallas_call(
        gather_kernel,
        in_specs=[anywhere] * 8,
        out_specs=[anywhere] * 17,
        out_shape=[
            low(D, n), low(D, n), low(D, n), low(D, ROWS), low(D, ROWS), low(ROWS, D), low(ROWS, BLK), low(ROWS, 2 * BLK),
            low(ROWS, 2 * BLK), low(ROWS, BLK), low(ROWS, n), low(ROWS, n), wide(8, PACK, 128), wide(1, D), wide(1, n),
            low(4, BLK, n), low(6, BLK, n),
        ],
        scratch_shapes=[
            vlow(D, n), vlow(D, n), vlow(D, n), vlow(ROWS, D), vlow(ROWS, D), vlow(ROWS, D), vlow(ROWS, D), vlow(D, ROWS),
            vlow(D, ROWS), vlow(ROWS, D), vwide(8, PACK, 128), vlow(ROWS, BLK), vlow(ROWS, 2 * BLK), vlow(ROWS, BLK),
            vlow(ROWS, n), vlow(ROWS, n), vlow(ROWS, n), vwide(ROWS, 128), vwide(ROWS, 128), vwide(192, 128), vwide(1, D),
            vwide(1, n), vlow(BLK, BLK), vlow(n, BLK),
            pltpu.SemaphoreType.DMA((56,)),
            pltpu.SemaphoreType.DMA((56,)),
            pltpu.SemaphoreType.DMA((40,)),
        ],
        compiler_params=params(collective_id=0, has_side_effects=True),
        cost_estimate=cost(2 * ROWS * D * 3 * n, 64 * 1024 * 1024),
        name="gather_phase",
    )(*args)


def grads_kernel(attn, up, down, qkv_out, proj_out, up_out, down_out):
    for core in range(2):
        for k, c in enumerate((1, 2, 0)):
            qkv_out[:, c, core * BLK : (core + 1) * BLK] = attn[core, :, k * BLK : (k + 1) * BLK].astype(F32)
        proj_out[core * BLK : (core + 1) * BLK, :] = attn[core, :, 3 * BLK :].astype(F32).T
        up_out[:, core * 1024 : (core + 1) * 1024] = up[core].astype(F32)
        down_out[core * 1024 : (core + 1) * 1024, :] = down[core].astype(F32).T


def grads_call(attn, up, down):
    tile = 128
    piece = pl.BlockSpec((2, tile, 1024), lambda i: (0, i, 0))
    wide = lambda *shape: jax.ShapeDtypeStruct(shape, F32)
    return pl.pallas_call(
        grads_kernel,
        grid=(BLK // tile,),
        in_specs=[piece] * 3,
        out_specs=[
            pl.BlockSpec((tile, 3, HALF), lambda i: (i, 0, 0)),
            pl.BlockSpec((HALF, tile), lambda i: (0, i)),
            pl.BlockSpec((tile, 2048), lambda i: (i, 0)),
            pl.BlockSpec((2048, tile), lambda i: (0, i)),
        ],
        out_shape=[wide(BLK, 3, HALF), wide(HALF, BLK), wide(BLK, 2048), wide(2048, BLK)],
        compiler_params=params(),
        cost_estimate=cost(0, 10 * 1024 * 1024),
        name="gradients",
    )(attn, up, down)


class Lefts:
    def __init__(self, sources, buf, sems):
        self.sources, self.buf, self.sems = sources, buf, sems
        self.queue, self.count = ([], []), [0, 0]

    def want(self, kind, j):
        if any(held == j for held, _, _ in self.queue[kind]):
            return
        slot = self.count[kind] % 2
        self.count[kind] += 1
        copy = pltpu.make_async_copy(
            self.sources[kind].at[pl.ds(j * BLK, BLK)], self.buf.at[kind, slot], self.sems.at[kind, slot]
        )
        copy.start()
        self.queue[kind].append((j, copy, slot))

    def take(self, kind, j):
        held, copy, slot = self.queue[kind].pop(0)
        assert held == j
        copy.wait()
        return self.buf.at[kind, slot]

    def run(self, jobs, after=()):
        for i, (kinds, j, act) in enumerate(jobs):
            for kind in kinds:
                self.want(kind, j)
            ahead = jobs[i + 1][:2] if i + 1 < len(jobs) else after
            if ahead:
                for kind in ahead[0]:
                    self.want(kind, ahead[1])
            act(*[self.take(kind, j) for kind in kinds])


def product(dst, lefts, rights, adds=()):
    at = 0
    for left, right in zip(lefts, rights):
        cols = slice(at, at + right.shape[1])
        total = jnp.dot(left[...], right[...], preferred_element_type=F32)
        for add in adds:
            total += add[:, cols].astype(F32)
        dst[:, cols] = total.astype(BF16)
        at += right.shape[1]


def row_products(half, a, b, w1, col1, w2, out, wa, wb, sems, unit=None, ub=None, vec=None):
    nt = (((1,), (1,)), ((), ()))
    ka = a.shape[1]
    rows = pl.ds(pl.multiple_of(half * HALF, HALF), HALF)

    def fetch(j, slot):
        at = pl.ds(pl.multiple_of(j * BLK, BLK), BLK)
        found = [
            pltpu.make_async_copy(w1.at[at, pl.ds(col1, ka)], wa.at[slot, :, pl.ds(0, ka)], sems.at[slot, 0]),
            pltpu.make_async_copy(w2.at[at], wb.at[slot], sems.at[slot, 1]),
        ]
        if unit is not None:
            found.append(pltpu.make_async_copy(unit.at[rows, at], ub.at[slot], sems.at[slot, 2]))
        return found

    for copy in fetch(0, 0):
        copy.start()

    @pl.loop(0, 8)
    def _(j):
        slot = lax.rem(j, 2)
        for copy in fetch(j, slot):
            copy.wait()

        @pl.when(j < 7)
        def _():
            for copy in fetch(j + 1, 1 - slot):
                copy.start()

        total = lax.dot_general(a[rows, :], wa[slot, :, :ka], nt, preferred_element_type=F32)
        total += lax.dot_general(b[rows, :], wb[slot], nt, preferred_element_type=F32)
        out[:, pl.ds(pl.multiple_of(j * BLK, BLK), BLK)] = total.astype(BF16)
        if unit is not None:
            vec[j, 0:1, :] = jnp.sum(total * ub[slot].astype(F32), axis=0, keepdims=True)
            vec[j, 1:2, :] = jnp.sum(total, axis=0, keepdims=True)


def add_rows(mine, got):
    @pl.loop(0, 4)
    def _(i):
        at = pl.ds(pl.multiple_of(i * 128, 128), 128)
        mine[at, :] = (mine[at, :].astype(F32) + got[at, :].astype(F32)).astype(BF16)


def reduce_kernel(w1, w2, w3, normed_t, grad_t, unit, q_in, kv_in, kvr_in, do_in, active_in, hidden_in, small_in, bias_in,
                  up_bias_in, a_s1, b_s1, tok_in, grad_in, table_in,
                  layer_out, input_grad, piece1, piece2, piece3, vec_out,
                  a_r1, a_r2, a_x, b_r1, b_r2, b_x, c_r1, c_r2, c_x, d_r1, d_r2, d_x,
                  q, do, keys, vals, keys_t, vals_t, active, hidden, att, raw, small, cos, sin, cos_r, sin_r, table,
                  st, dp, dk, dv, qm, dom, out_t, dq_t, dkv, wa, wb, ub, theirs, br_m, br_c, br_z, br_o, ng_m, ng_c, ng_z, ng_o,
                  turned, tok, grad, left_buf, stage, a_s2, a_m, b_s2, b_m, c_s1, c_s2, c_m, d_s1, d_s2, d_m,
                  vec_t, vec_m, va, va_r, vb_r, units, my, my_r, mx, mx_r, last, last_r, bias_v, up_bias_v, vec_v,
                  send, recv, local, sems, left_sems, stage_sems):
    x, y, z, core = coords()
    x_lo, x_hi = lax.rem(x, 2), x // 2
    other = 1 - core
    up, down, far = beside(dy=1), beside(dy=3), beside(dy=2)
    right, left, over = beside(dx=1), beside(dx=3), beside(dx=2)
    mate = beside(flip=1)
    above, below = beside(dz=1), beside(dz=3)
    along = [above, beside(dz=2), below]
    copies = Copies(send, recv, local)
    here, remote = copies.here, copies.remote
    nt = (((1,), (1,)), ((), ()))

    load_active, load_hidden = here(active_in, active), here(hidden_in, hidden)
    own_keys = pl.ds(pl.multiple_of(x_hi * ROWS, ROWS), ROWS)
    loads = [here(kv_in.at[:, pl.ds(0, BLK)], keys.at[own_keys]), here(kv_in.at[:, pl.ds(BLK, BLK)], vals.at[own_keys])]
    loads += [here(table_in, table), here(q_in, q), here(do_in, do), here(small_in, small), here(bias_in, bias_v),
              here(up_bias_in, up_bias_v)]
    z_rows = pl.ds(pl.multiple_of(z * 128, 128), 128)
    loads += [here(tok_in.at[z_rows], tok), here(grad_in.at[z_rows], grad)]
    far_keys = pltpu.make_async_copy(kvr_in.at[:, pl.ds(0, BLK)], keys.at[pl.ds(0, ROWS)], local.at[copies.locals])
    far_vals = pltpu.make_async_copy(kvr_in.at[:, pl.ds(BLK, BLK)], vals.at[pl.ds(0, ROWS)], local.at[copies.locals + 1])
    copies.locals += 2

    @pl.when(x_hi == 1)
    def _():
        far_keys.start()
        far_vals.start()

    greet([up, down, far, right, left, over, mate] + along)
    b1 = [remote(b_s1.at[pl.ds(2 * k, 2)], b_r1.at[pl.ds(2 * k, 2)], target) for k, target in enumerate((far, up, down))]
    a1 = [remote(a_s1.at[pl.ds(2 * k, 2)], a_r1.at[pl.ds(2 * k, 2)], target) for k, target in enumerate((right, left))]

    lefts = Lefts((normed_t, grad_t), left_buf, left_sems)

    def staged(parts):
        views, found = [], []
        for k, part in enumerate(parts):
            view = stage.at[k, :, pl.ds(0, part.shape[-1])]
            copy = pltpu.make_async_copy(part, view, stage_sems.at[k])
            copy.start()
            found.append(copy)
            views.append(view)
        for copy in found:
            copy.wait()
        return views

    def arrived(moves):
        for copy in moves:
            copy.wait_recv()

    def settle(mine, got, move, piece, cols):
        move.wait_send()
        copies.sent = [copy for copy in copies.sent if copy is not move]
        move.wait_recv()
        (more,) = staged([got])
        mine[...] = (mine[...].astype(F32) + more[...].astype(F32)).astype(BF16)
        spot = piece.at[core, :, cols]
        return here(mine, spot), remote(mine, spot, mate)

    for copy in loads:
        copy.wait()

    @pl.when(x_hi == 1)
    def _():
        far_keys.wait()
        far_vals.wait()

    @pl.loop(0, (x_hi + 1) * (ROWS // KC))
    def _(j):
        at = pl.ds(pl.multiple_of(j * KC, KC), KC)
        keys_t[:, at] = keys[at, :].astype(F32).T.astype(BF16)
        vals_t[:, at] = vals[at, :].astype(F32).T.astype(BF16)
        dk[at, :] = jnp.zeros((KC, BLK), F32)
        dv[at, :] = jnp.zeros((KC, BLK), F32)

    rope_rows(table, x_hi * ROWS, cos, sin, ROWS)
    rope_rows(table, 0, cos_r, sin_r, ROWS)
    lane = lax.broadcasted_iota(jnp.int32, (QT, 128), 1) // HD

    def heads(pair):
        lanes = slice(pair * 128, pair * 128 + 128)
        for t in range(ROWS // QT):
            rows = slice(t * QT, (t + 1) * QT)
            chunks = x_hi * (ROWS // KC) + t * QT // KC + 1
            for side in range(2):
                qm[side] = jnp.where(lane == side, q[rows, lanes], jnp.zeros((), BF16))
                dom[side] = jnp.where(lane == side, do[rows, lanes], jnp.zeros((), BF16))

            def score(j, tops, masked):
                at = pl.ds(pl.multiple_of(j * KC, KC), KC)
                new = []
                for side in range(2):
                    s = lax.dot_general(keys[at, lanes], qm[side], nt, preferred_element_type=F32)
                    if masked:
                        ki = lax.broadcasted_iota(jnp.int32, (KC, QT), 0)
                        qi = lax.broadcasted_iota(jnp.int32, (KC, QT), 1) + t * QT % KC
                        s = jnp.where(ki <= qi, s, MASKED)
                    st[side, at, :] = s
                    new.append(jnp.maximum(tops[side], jnp.max(s, axis=0, keepdims=True)))
                return tuple(new)

            low = jnp.full((1, QT), MASKED, F32)
            tops = lax.fori_loop(0, chunks - 1, lambda j, m: score(j, m, False), (low, low))
            tops = score(chunks - 1, tops, True)

            def weigh(j, carry):
                at = pl.ds(pl.multiple_of(j * KC, KC), KC)
                new = []
                for side in range(2):
                    total, dot = carry[2 * side : 2 * side + 2]
                    p = jnp.exp(st[side, at, :] - tops[side])
                    st[side, at, :] = p
                    d = lax.dot_general(vals[at, lanes], dom[side], nt, preferred_element_type=F32)
                    dp[side, at, :] = d
                    new.append(total + jnp.sum(p, axis=0, keepdims=True))
                    new.append(dot + jnp.sum(p * d, axis=0, keepdims=True))
                return tuple(new)

            zero = jnp.zeros((1, QT), F32)
            sums = lax.fori_loop(0, chunks, weigh, (zero,) * 4)
            inv = [1.0 / sums[0], 1.0 / sums[2]]
            delta = [sums[1] * inv[0], sums[3] * inv[1]]
            out_t[:, rows] = jnp.zeros((128, QT), F32)
            dq_t[:, rows] = jnp.zeros((128, QT), F32)

            def spread(j, _):
                at = pl.ds(pl.multiple_of(j * KC, KC), KC)
                new_v, new_k = dv[at, lanes], dk[at, lanes]
                for side in range(2):
                    hrows = slice((2 * pair + side) * HD, (2 * pair + side + 1) * HD)
                    trows = slice(side * HD, (side + 1) * HD)
                    p = st[side, at, :] * inv[side]
                    p_low = p.astype(BF16)
                    ds = (p * (dp[side, at, :] - delta[side])).astype(BF16)
                    out_t[trows, rows] += jnp.dot(vals_t[hrows, at], p_low, preferred_element_type=F32)
                    dq_t[trows, rows] += jnp.dot(keys_t[hrows, at], ds, preferred_element_type=F32)
                    new_v += jnp.dot(p_low, dom[side], preferred_element_type=F32)
                    new_k += jnp.dot(ds, qm[side], preferred_element_type=F32)
                dv[at, lanes] = new_v
                dk[at, lanes] = new_k
                return 0

            lax.fori_loop(0, chunks, spread, 0)

    def turn_back(v, c, s):
        return v * c - partner(v) * s

    def end_pair(pair):
        lanes = slice(pair * 128, pair * 128 + 128)
        copy = copies.make(dkv.at[pair], dkv.at[pair], over)

        @pl.when(x_hi == 1)
        def _():
            dkv[pair, :, :128] = turn_back(dk[:ROWS, lanes], cos_r[...], sin_r[...]).astype(BF16)
            dkv[pair, :, 128:] = dv[:ROWS, lanes].astype(BF16)
            copy.start()

        for t in range(ROWS // 512):
            rows = slice(t * 512, (t + 1) * 512)
            att[rows, lanes] = out_t[:, rows].T.astype(BF16)
            raw[rows, 2 * BLK + pair * 128 : 2 * BLK + pair * 128 + 128] = turn_back(
                dq_t[:, rows].T * (HD**-0.5), cos[rows, :], sin[rows, :]
            ).astype(BF16)
        return copy

    heads(0)
    pair0 = end_pair(0)

    load_active.wait()
    lefts.want(1, 2)
    arrived(a1)
    s = staged([a_r1.at[2], a_r1.at[3], a_r1.at[1]])
    lefts.run(
        [((1,), j, lambda l, k=k: product(a_s2.at[k], [l], [active], [s[k]])) for k, j in enumerate((2, 3, 1))],
        after=((0, 1), 2),
    )
    a_y = [remote(a_s2.at[k], a_r2.at[k], target) for k, target in enumerate((far, down, up))]

    heads(1)
    pair1 = end_pair(1)

    tail = [raw.at[:, pl.ds(2 * BLK, BLK)], att]
    d1 = []
    for k, (j, target) in enumerate(((2, far), (1, up), (3, down))):
        jobs = [((0, 1), j + 4 * i, lambda a, b, i=i: product(d_s1.at[2 * k + i], [a, b], tail)) for i in range(2)]
        lefts.run(jobs, after=((0, 1), (1, 3)[k]) if k < 2 else ())
        d1.append(remote(d_s1.at[pl.ds(2 * k, 2)], d_r1.at[pl.ds(2 * k, 2)], target))

    row_products(other, att, active, w1, 3 * BLK, w3, theirs, wa, wb, sems)
    br_core = remote(theirs, br_c, mate)
    row_products(core, att, active, w1, 3 * BLK, w3, br_m, wa, wb, sems)

    def z_at(dz, first=0, count=128):
        return pl.ds(pl.multiple_of(lax.rem(z + dz, 4) * 128 + first, 64), count)

    def to_z(total, got, out):
        return [
            remote(total.at[z_at(2, 0, 64)], got.at[0, pl.ds(0, 64)], above),
            remote(total.at[z_at(2, 64, 64)], got.at[0, pl.ds(64, 64)], below),
            remote(total.at[z_at(1, 64, 64)], got.at[1, pl.ds(64, 64)], above),
            remote(total.at[z_at(3, 0, 64)], got.at[2, pl.ds(0, 64)], below),
        ]

    def pass_on(total, got, first, buf):
        first[0].wait_recv()
        buf[0] = (total[z_at(1, 0, 64), :].astype(F32) + got[0, :64, :].astype(F32)).astype(BF16)
        one = remote(buf.at[0], got.at[1, pl.ds(0, 64)], above)
        first[1].wait_recv()
        buf[1] = (total[z_at(3, 64, 64), :].astype(F32) + got[0, 64:, :].astype(F32)).astype(BF16)
        two = remote(buf.at[1], got.at[2, pl.ds(64, 64)], below)
        return [first[2], first[3], one, two]

    def from_z(chunk, rows):
        at = z_at(0)
        return [here(chunk, rows.at[at]), remote(chunk, rows.at[at], above), remote(chunk, rows.at[at], below)]

    def pass_rows(moves, rows):
        moves[1].wait_recv()
        one = remote(rows.at[z_at(3, 0, 64)], rows.at[z_at(3, 0, 64)], above)
        moves[2].wait_recv()
        two = remote(rows.at[z_at(1, 64, 64)], rows.at[z_at(1, 64, 64)], below)
        return moves[0], [one, two]

    br_core.wait_recv()
    add_rows(br_m, br_c)
    br1 = to_z(br_m, br_z, br_o)

    def local_grads(pair, more):
        lanes = slice(pair * 128, pair * 128 + 128)
        k = turn_back(dk[own_keys, lanes], cos[...], sin[...])
        v = dv[own_keys, lanes]
        if more:
            k = k + dkv[pair, :, :128].astype(F32)
            v = v + dkv[pair, :, 128:].astype(F32)
        raw[:, lanes] = k.astype(BF16)
        raw[:, BLK + pair * 128 : BLK + pair * 128 + 128] = v.astype(BF16)

    for pair, copy in enumerate((pair0, pair1)):

        @pl.when(x_hi == 1)
        def _():
            local_grads(pair, False)
            copy.wait_send()

        @pl.when(x_hi == 0)
        def _():
            copy.wait_recv()
            local_grads(pair, True)

    load_hidden.wait()
    br_core.wait_send()
    copies.sent = [copy for copy in copies.sent if copy is not br_core]
    row_products(other, raw, hidden, w1, 0, w2, theirs, wa, wb, sems, unit, ub, vec_t)
    ng_core = remote(theirs, ng_c, mate)
    row_products(core, raw, hidden, w1, 0, w2, ng_m, wa, wb, sems, unit, ub, vec_m)
    lefts.want(0, 4)
    br2 = pass_on(br_m, br_z, br1, turned.at[0])
    ng_core.wait_recv()
    add_rows(ng_m, ng_c)
    ng1 = to_z(ng_m, ng_z, ng_o)

    pairs = raw.at[:, pl.ds(0, 512)]
    lefts.run(
        [((0,), j, lambda l, k=k: product(c_s1.at[k], [l], [pairs])) for k, j in enumerate((4, 5, 6, 7))], after=((0,), 4)
    )
    c1 = [remote(c_s1.at[pl.ds(2 * k, 2)], c_r1.at[pl.ds(2 * k, 2)], target) for k, target in enumerate((right, left))]

    va[...] = jnp.zeros_like(va)
    for j in range(8):
        va[j, 0:2, :] = vec_t[j, 0:2, :] + vec_m[j, 0:2, :]
    va_sent = [remote(va, va_r.at[k], along[k]) for k in range(3)]

    upper, lower = pl.ds(0, BLK // 2), pl.ds(BLK // 2, BLK // 2)
    arrived(b1)
    s = staged([b_r1.at[1], b_r1.at[3], b_r1.at[5]])
    lefts.run([((0,), 4, lambda l: product(b_s2, [l], [hidden], s))], after=((1,), 0))
    b2 = [remote(b_s2.at[upper], b_r2.at[upper], right), remote(b_s2.at[lower], b_r2.at[lower], left)]

    arrived(a_y)
    s = staged([a_r1.at[0], a_r2.at[0], a_r2.at[1], a_r2.at[2]])
    lefts.run([((1,), 0, lambda l: product(a_m, [l], [active], s))], after=((0, 1), 4))
    a3 = remote(a_m, a_x, over)

    arrived(br2)
    tile = 32

    def share(total, got, i, j):
        at = pl.ds(pl.multiple_of(i * tile, tile), tile)
        from_all = pl.ds(pl.multiple_of(z * 128 + i * tile, tile), tile)
        cols = slice(j * BLK, (j + 1) * BLK)
        return total[from_all, cols].astype(F32) + (got[1, at, cols].astype(F32) + got[2, at, cols].astype(F32))

    def line(row, j):
        return jnp.concatenate([small[j, row : row + 1, :], small[j, row + 1 : row + 2, :]], axis=1)

    def spot(j):
        return pl.ds(pl.multiple_of(block_order(y, x_lo, j) * BLK, BLK), BLK)

    @pl.loop(0, 128 // tile)
    def _(i):
        at = pl.ds(pl.multiple_of(i * tile, tile), tile)
        for j in range(8):
            value = tok[at, spot(j)].astype(F32) + share(br_m, br_z, i, j) + line(4, j)
            br_o[at, spot(j)] = value.astype(BF16)

    br3 = from_z(br_o, layer_out)
    ng2 = pass_on(ng_m, ng_z, ng1, turned.at[1])

    arrived(d1)
    s = staged([d_r1.at[1], d_r1.at[3], d_r1.at[5]])
    lefts.run([((0, 1), 4, lambda a, b: product(d_s2, [a, b], tail, s))], after=((0,), 0))
    d2 = [remote(d_s2.at[upper], d_r2.at[upper], right), remote(d_s2.at[lower], d_r2.at[lower], left)]

    arrived(b2)
    s = staged([b_r1.at[0], b_r1.at[2], b_r1.at[4], b_r2])
    lefts.run([((0,), 0, lambda l: product(b_m, [l], [hidden], s))], after=((0,), 2))
    b3 = remote(b_m, b_x, over)

    arrived(c1)
    s = staged([c_r1.at[2], c_r1.at[3], c_r1.at[1]])
    lefts.run(
        [((0,), j, lambda l, k=k: product(c_s2.at[k], [l], [pairs], [s[k]])) for k, j in enumerate((2, 3, 1))],
        after=((0, 1), 0),
    )
    c_y = [remote(c_s2.at[k], c_r2.at[k], target) for k, target in enumerate((far, down, up))]

    for copy in va_sent:
        copy.wait_recv()
    vec_v[0] = (va[...] + va_r[1]) + (va_r[0] + va_r[2])
    vb = remote(vec_v.at[0], vb_r, mate)

    arrived(ng2)

    @pl.loop(0, 128 // tile)
    def _(i):
        at = pl.ds(pl.multiple_of(i * tile, tile), tile)
        rows = tok[at, :].astype(F32)
        mean = jnp.mean(rows, axis=-1, keepdims=True)
        centered = rows - mean
        inv = lax.rsqrt(jnp.mean(centered * centered, axis=-1, keepdims=True) + EPSILON)

        def terms(j):
            u = (tok[at, spot(j)].astype(F32) - mean) * inv
            return u, share(ng_m, ng_z, i, j) * line(0, j)

        first = second = jnp.zeros((tile, 1), F32)
        for j in range(8):
            u, g = terms(j)
            first += jnp.sum(g, axis=-1, keepdims=True)
            second += jnp.sum(g * u, axis=-1, keepdims=True)
        first, second = first / D, second / D
        for j in range(8):
            u, g = terms(j)
            ng_o[at, spot(j)] = (grad[at, spot(j)].astype(F32) + inv * (g - first - u * second)).astype(BF16)

    ng3 = from_z(ng_o, input_grad)
    br_own, br4 = pass_rows(br3, layer_out)

    vb.wait_recv()
    units[...] = jnp.zeros_like(units)
    units[0:3, :] = jnp.sum(raw[...].astype(F32), axis=0, keepdims=True).reshape(3, BLK)
    for j in range(4):
        units[3 + j : 4 + j, :] = up_bias_v[:, j * BLK : (j + 1) * BLK]
    for j in range(8):
        dy, dx = j % 4, j // 4
        my[dy, dx] = vec_v[0, j] + vb_r[j]
        my[dy, dx, 2:3, :] = bias_v[:, j * BLK : (j + 1) * BLK]
    for dy in range(4):
        my[dy, 2] = units[...]
    my_sent = [remote(my.at[1], my_r.at[0], up), remote(my.at[2], my_r.at[1], far), remote(my.at[3], my_r.at[2], down)]

    arrived(d2)
    s = staged([d_r1.at[0], d_r1.at[2], d_r1.at[4], d_r2])
    lefts.run([((0, 1), 0, lambda a, b: product(d_m, [a, b], tail, s))], after=((0,), 0))
    d3 = remote(d_m, d_x, over)
    a4 = settle(a_m, a_x, a3, piece3, pl.ds(0, 1024))

    arrived(c_y)
    s = staged([c_r1.at[0], c_r2.at[0], c_r2.at[1], c_r2.at[2]])
    lefts.run([((0,), 0, lambda l: product(c_m, [l], [pairs], s))])
    c3 = remote(c_m, c_x, over)
    b4 = settle(b_m, b_x, b3, piece2, pl.ds(0, 1024))

    arrived(my_sent)
    here_sum = (my[0] + my_r[1]) + (my_r[0] + my_r[2])
    mx[0, 0] = here_sum[0]
    mx[0, 1] = here_sum[2]
    mx[1, 0] = here_sum[1]
    mx[1, 1] = here_sum[2]
    mx_sent = [remote(mx.at[1], mx_r.at[0], right), remote(mx.at[0], mx_r.at[1], over), remote(mx.at[1], mx_r.at[2], left)]
    ng_own, ng4 = pass_rows(ng3, input_grad)
    d4 = settle(d_m, d_x, d3, piece1, pl.ds(512, 512))

    arrived(mx_sent)
    last[...] = (mx[0] + mx_r[1]) + (mx_r[0] + mx_r[2])
    vec_copy = remote(last.at[1], last_r, mate)
    c4 = settle(c_m, c_x, c3, piece1, pl.ds(0, 512))
    vec_copy.wait_recv()
    last_saved = [here(last, vec_out.at[pl.ds(0, 2)]), here(last_r, vec_out.at[2])]

    for own, copy in (a4, b4, c4, d4):
        own.wait()
        copy.wait_recv()
    br_own.wait()
    ng_own.wait()
    arrived(br4 + ng4)
    for copy in last_saved:
        copy.wait()
    for copy in copies.sent:
        copy.wait_send()


def reduce_call(*args):
    low = lambda *shape: jax.ShapeDtypeStruct(shape, BF16)
    wide = lambda *shape: jax.ShapeDtypeStruct(shape, F32)
    vlow = lambda *shape: pltpu.VMEM(shape, BF16)
    vwide = lambda *shape: pltpu.VMEM(shape, F32)
    anywhere = pl.BlockSpec(memory_space=pl.ANY)
    n = 1024
    outs = [low(HALF, D), low(HALF, D), low(2, BLK, n), low(2, BLK, n), low(2, BLK, n), wide(3, 8, BLK)] + [
        low(4, BLK, n), low(3, BLK, n), low(BLK, n), low(6, BLK, n), low(BLK, n), low(BLK, n),
        low(4, BLK, 512), low(3, BLK, 512), low(BLK, 512), low(6, BLK, 512), low(BLK, 512), low(BLK, 512),
    ]
    result = pl.pallas_call(
        reduce_kernel,
        in_specs=[anywhere] * 20,
        out_specs=[anywhere] * len(outs),
        out_shape=outs,
        scratch_shapes=[
            vlow(ROWS, BLK), vlow(ROWS, BLK), vlow(2 * ROWS, BLK), vlow(2 * ROWS, BLK), vlow(BLK, 2 * ROWS),
            vlow(BLK, 2 * ROWS), vlow(ROWS, n), vlow(ROWS, n), vlow(ROWS, BLK), vlow(ROWS, 3 * BLK),
            vwide(8, PACK, 128), vwide(ROWS, 128), vwide(ROWS, 128), vwide(ROWS, 128), vwide(ROWS, 128), vwide(192, 128),
            vwide(2, 2 * ROWS, QT), vwide(2, 2 * ROWS, QT), vwide(2 * ROWS, BLK), vwide(2 * ROWS, BLK), vlow(2, QT, 128),
            vlow(2, QT, 128), vwide(128, ROWS), vwide(128, ROWS), vlow(2, ROWS, BLK), vlow(2, BLK, 3 * BLK),
            vlow(2, BLK, n), vlow(2, HALF, BLK), vlow(HALF, D), vlow(HALF, D), vlow(HALF, D), vlow(3, 128, D), vlow(128, D),
            vlow(HALF, D), vlow(HALF, D), vlow(3, 128, D), vlow(128, D), vlow(2, 2, 64, D), vlow(128, D), vlow(128, D),
            vlow(2, 2, BLK, ROWS), vlow(4, BLK, n), vlow(3, BLK, n), vlow(BLK, n), vlow(BLK, n), vlow(BLK, n),
            vlow(4, BLK, 512), vlow(3, BLK, 512), vlow(BLK, 512), vlow(6, BLK, 512), vlow(BLK, 512), vlow(BLK, 512),
            vwide(8, 8, BLK), vwide(8, 8, BLK),
            vwide(8, 8, BLK), vwide(3, 8, 8, BLK), vwide(8, 8, BLK), vwide(8, BLK), vwide(4, 3, 8, BLK),
            vwide(3, 3, 8, BLK), vwide(2, 2, 8, BLK), vwide(3, 2, 8, BLK), vwide(2, 8, BLK), vwide(8, BLK),
            vwide(1, D), vwide(1, n), vwide(1, 8, 8, BLK),
            pltpu.SemaphoreType.DMA((72,)),
            pltpu.SemaphoreType.DMA((72,)),
            pltpu.SemaphoreType.DMA((32,)),
            pltpu.SemaphoreType.DMA((2, 3)),
            pltpu.SemaphoreType.DMA((2, 2)),
            pltpu.SemaphoreType.DMA((4,)),
        ],
        compiler_params=params(collective_id=1, has_side_effects=True),
        cost_estimate=cost(2 * ROWS * D * 5 * 1024, 128 * 1024 * 1024),
        name="reduce_phase",
    )(*args)
    return result[:6]


def body(tokens, ln_gain, ln_shift, out_bias, w_qkv, b_qkv, w_out, w_fc1, b_fc1, w_fc2, out_grad):
    f, c = lax.axis_index("fsdp"), lax.axis_index("ctx")
    x_hi, core = c // 2, c % 2
    tokens, out_grad = tokens[0], out_grad[0]

    mine = lax.dynamic_slice_in_dim(w_qkv, core * BLK, BLK, axis=2)
    qkv_shard = jnp.concatenate([mine[:, 1], mine[:, 2], mine[:, 0]], axis=1)

    own = (jnp.arange(HD) // 8 == f)[None, None, :]
    spread = lambda v: jnp.where(own, jnp.tile(v, (1, 1, 8)), jnp.zeros((), BF16)).reshape(-1)
    pack = jnp.concatenate(
        [
            ln_gain,
            ln_shift,
            out_bias,
            spread(jnp.roll(lax.dynamic_slice_in_dim(b_qkv, core * 4, 4, axis=1), -1, axis=0)),
            spread(lax.dynamic_slice_in_dim(b_fc1, core * 16, 16, axis=0)[None]),
            jnp.zeros((512,), BF16),
        ]
    )
    pack = pack.astype(F32).reshape(PACK, 128)

    (w_attn, w_up, w_down, normed_t, grad_t, unit, q, kv, kvr, do, active, hidden_grad, small, bias_grad, up_bias_grad,
     a_first, b_first) = (
        gather_call(qkv_shard, w_out, w_fc1, w_fc2, tokens, out_grad, pack, ROPE)
    )
    layer_out, input_grad, attn_all, up_all, down_all, vec = reduce_call(
        w_attn, w_up, w_down, normed_t, grad_t, unit, q, kv, kvr, do, active, hidden_grad, small, bias_grad, up_bias_grad,
        a_first, b_first, tokens, out_grad, ROPE
    )
    qkv_out, proj_out, up_out, down_out = grads_call(attn_all, up_all, down_all)
    gain_grad, shift_grad, out_bias_grad = vec[0, 0], vec[0, 1], vec[0, 2]
    units = jnp.where(core == 0, vec[1:], vec[:0:-1]).reshape(2, 8 * BLK)
    qkv_bias_out = lax.dynamic_slice_in_dim(
        jnp.roll(units[:, : 3 * BLK].reshape(2, 3, 4, HD), 1, axis=1).transpose(1, 0, 2, 3).reshape(3, 8, HD), f * 8, 8, axis=2
    )
    up_bias_out = lax.dynamic_slice_in_dim(units[:, 3 * BLK : 7 * BLK].reshape(32, HD), f * 8, 8, axis=1)
    return (
        layer_out[None],
        input_grad[None],
        gain_grad,
        shift_grad,
        out_bias_grad,
        qkv_out,
        qkv_bias_out,
        proj_out,
        up_out,
        up_bias_out,
        down_out,
    )


def solution(mesh):
    in_specs = (
        P("fsdp", "ctx", None),
        P("fsdp"),
        P("fsdp"),
        P("fsdp"),
        P("fsdp", None, "tp"),
        P(None, "tp", "fsdp"),
        P("tp", "fsdp"),
        P("fsdp", "tp"),
        P("tp", "fsdp"),
        P("tp", "fsdp"),
        P("fsdp", "ctx", None),
    )
    out_specs = (
        P("fsdp", "ctx", None),
        P("fsdp", "ctx", None),
        P("fsdp"),
        P("fsdp"),
        P("fsdp"),
        P("fsdp", None, "tp"),
        P(None, "tp", "fsdp"),
        P("tp", "fsdp"),
        P("fsdp", "tp"),
        P("tp", "fsdp"),
        P("tp", "fsdp"),
    )
    return jax.shard_map(body, mesh=mesh, in_specs=in_specs, out_specs=out_specs, check_vma=False)
```

```python
import math

import jax
import jax.numpy as jnp
import numpy as np
from jax import lax
from jax.experimental import pallas as pl
from jax.experimental.pallas import tpu as pltpu
from jax.sharding import PartitionSpec as P

D = 2048
HD = 64
ROT = 32
BLK = 256
ROWS = 1024
HALF = 512
EPSILON = 1e-05
MASKED = -1e30
F32 = jnp.float32
BF16 = jnp.bfloat16
VMEM_LIMIT = 62 * 1024 * 1024


def params(**kw):
    return pltpu.CompilerParams(vmem_limit_bytes=VMEM_LIMIT, **kw)


def whole():
    return pl.BlockSpec(memory_space=pltpu.VMEM)


def cost(flops, nbytes, trans=0):
    return pl.CostEstimate(flops=int(flops), bytes_accessed=int(nbytes), transcendentals=int(trans))


def block_order(y, x_lo, j):
    dx, dy = j // 4, j % 4
    return lax.rem(y + dy, 4) * 2 + lax.rem(x_lo + dx, 2)


def partner(v):
    lane = lax.broadcasted_iota(jnp.int32, v.shape, 1)
    up = pltpu.roll(v, v.shape[1] - ROT // 2, 1)
    down = pltpu.roll(v, ROT // 2, 1)
    return jnp.where(lane % HD < ROT // 2, up, down)


QT = 256
KC = 512


def rope_table():
    lane = np.arange(128) % HD
    freq = np.where(lane < ROT, 10000.0 ** (-2.0 * (lane % (ROT // 2)) / ROT), 0.0)
    sign = np.where(lane < ROT // 2, -1.0, 1.0)
    coarse, fine = np.arange(64)[:, None] * 32 * freq, np.arange(32)[:, None] * freq
    parts = [np.cos(coarse), np.sin(coarse) * sign, np.cos(fine), np.sin(fine) * sign]
    return np.concatenate(parts).astype(np.float32)


ROPE = rope_table()
GELU_C = math.sqrt(2.0 / math.pi)


MESH = pl.DeviceIdType.MESH
PACK = 24


def coords():
    f, c, z = lax.axis_index("fsdp"), lax.axis_index("ctx"), lax.axis_index("tp")
    return (c // 2) * 2 + f % 2, f // 2, z, c % 2


def device(x, y, z, core):
    return (y * 2 + lax.rem(x, 2), (x // 2) * 2 + core, z)


def beside(dx=0, dy=0, flip=0, dz=0):
    x, y, z, core = coords()
    return device(
        lax.rem(x + dx + 4, 4), lax.rem(y + dy + 4, 4), lax.rem(z + dz + 4, 4), (1 - core) if flip else core
    )


def greet(targets):
    barrier = pltpu.get_barrier_semaphore()
    for target in targets:
        pl.semaphore_signal(barrier, inc=1, device_id=target, device_id_type=MESH)
    pl.semaphore_wait(barrier, len(targets))


class Copies:
    def __init__(self, send, recv, local):
        self.send, self.recv, self.local = send, recv, local
        self.remotes = self.locals = 0
        self.sent = []

    def make(self, src, dst, target):
        i = self.remotes
        self.remotes += 1
        return pltpu.make_async_remote_copy(
            src, dst, self.send.at[i], self.recv.at[i], device_id=target, device_id_type=MESH
        )

    def remote(self, src, dst, target):
        copy = self.make(src, dst, target)
        copy.start()
        self.sent.append(copy)
        return copy

    def here(self, src, dst):
        copy = pltpu.make_async_copy(src, dst, self.local.at[self.locals])
        self.locals += 1
        copy.start()
        return copy


def rope_rows(table, first, cos, sin, count):
    @pl.loop(0, count // 32)
    def _(i):
        at = pl.ds(pl.multiple_of(i * 32, 32), 32)
        ch, sh = table[pl.ds(first // 32 + i, 1), :], table[pl.ds(64 + first // 32 + i, 1), :]
        cl, sl = table[128:160, :], table[160:192, :]
        cos[at, :] = ch * cl - sh * sl
        sin[at, :] = sh * cl + ch * sl


def turn(v, c, s):
    return v * c + partner(v) * s


def gather_kernel(s1_in, proj_in, up_in, down_in, tok_in, grad_in, pack, table_in,
                  w1_out, w2_out, w3_out, normed_t_out, grad_t_out, unit_out, q_out, kv_out, kvr_out, do_out,
                  active_out, hidden_out, small_out, bias_out, up_bias_out, a_s1_out, b_s1_out,
                  w1, w2, w3, tok, grad, normed, grad_rel, normed_t, grad_t, unit, small, q, kv, do, active, slope,
                  hidden, cos, sin, table, bias_sum, up_bias_sum, proj_v, down_v, send, recv, local):
    x, y, z, core = coords()
    x_lo, x_hi = lax.rem(x, 2), x // 2
    up, down, far = beside(dy=1), beside(dy=3), beside(dy=2)
    right, left, over, mate = beside(dx=1), beside(dx=3), beside(dx=2), beside(flip=1)
    copies = Copies(send, recv, local)
    here, remote = copies.here, copies.remote
    hcols = pl.ds(pl.multiple_of(core * 1024, 1024), 1024)
    hrows = pl.ds(pl.multiple_of(core * 1024, 1024), 1024)
    prows = pl.ds(pl.multiple_of(core * BLK, BLK), BLK)
    own_block = pl.ds(0, BLK)
    proj_load = here(proj_in.at[prows], proj_v)
    down_load = here(down_in.at[hrows], down_v)
    s1_load = here(s1_in, w1.at[own_block, pl.ds(0, 3 * BLK)])
    up_load = here(up_in.at[:, hcols], w2.at[own_block])
    greet([up, down, far, right, left, over, mate])

    class Part:
        def __init__(self, w, at, n):
            self.w, self.cols, self.moves = w, pl.ds(at, n), []

        def rows(self, j, first=0, count=BLK):
            return self.w.at[pl.ds(j * BLK + first, count), self.cols]

        def to(self, j, k, target, first=0, count=BLK):
            copy = remote(self.rows(j, first, count), self.rows(k, first, count), target)
            self.moves.append(copy)
            return copy

        def along_y(self, base):
            return [self.to(base, base + 3, up), self.to(base, base + 1, down), self.to(base, base + 2, far)]

        def sideways(self):
            return [self.to(0, 4, right, 0, BLK // 2), self.to(0, 4, left, BLK // 2, BLK // 2)]

        def begin_x(self):
            self.x = self.sideways()

        def begin_y(self):
            self.y = self.along_y(0)

        def forward(self):
            for copy in self.y:
                copy.wait_recv()
            self.x += [
                self.to(1, 5, right), self.to(3, 7, left),
                self.to(2, 6, right, 0, BLK // 2), self.to(2, 6, left, BLK // 2, BLK // 2),
            ]

        def forward_y(self):
            for copy in self.x:
                copy.wait_recv()
            self.x = self.along_y(4)

        def arrived(self):
            for copy in self.x:
                copy.wait_recv()

        def all_arrived(self):
            for copy in self.y + self.x:
                copy.wait_recv()

    keys_part, rest_part = Part(w1, 0, 512), Part(w1, 512, 512)
    up_part = Part(w2, 0, 1024)
    down_a, down_b = Part(w3, 0, 512), Part(w3, 512, 512)

    my_rows = pl.ds(pl.multiple_of(core * HALF, HALF), HALF)
    pack_y = [remote(pack, small.at[3], up), remote(pack, small.at[1], down), remote(pack, small.at[2], far)]
    pack_own = here(pack, small.at[0])
    tok_copy = remote(tok_in, tok.at[my_rows], mate)
    grad_copy = remote(grad_in, grad.at[my_rows], mate)
    s1_load.wait()
    keys_part.begin_y()
    keys_part.begin_x()
    mine = [here(tok_in, tok.at[my_rows]), here(grad_in, grad.at[my_rows])]
    table_load = here(table_in, table)

    proj_load.wait()
    w1[0:BLK, 3 * BLK :] = proj_v[...].astype(F32).T.astype(BF16)
    down_load.wait()
    for k in range(4):
        w3[0:BLK, k * BLK : (k + 1) * BLK] = down_v[k * BLK : (k + 1) * BLK, :].astype(F32).T.astype(BF16)
    for copy in pack_y:
        copy.wait_recv()
    pack_own.wait()
    pack_x = remote(small.at[pl.ds(0, 4)], small.at[pl.ds(4, 4)], right)
    up_load.wait()
    up_part.begin_x()
    down_b.begin_x()
    table_load.wait()
    rope_rows(table, x_hi * ROWS, cos, sin, ROWS)
    up_part.begin_y()
    down_b.begin_y()
    keys_part.forward()
    down_b.forward_y()
    down_a.begin_y()
    rest_part.begin_y()
    for copy in mine:
        copy.wait()
    tok_copy.wait_recv()
    grad_copy.wait_recv()
    pack_x.wait_recv()

    bias_sum[...] = jnp.zeros_like(bias_sum)
    up_bias_sum[...] = jnp.zeros_like(up_bias_sum)
    tile = 128

    def prepare(first, last):
        @pl.loop(first, last)
        def _(i):
            at = pl.ds(pl.multiple_of(i * tile, tile), tile)
            rows = tok[at, :].astype(F32)
            mean = jnp.mean(rows, axis=-1, keepdims=True)
            centered = rows - mean
            inv = lax.rsqrt(jnp.mean(centered * centered, axis=-1, keepdims=True) + EPSILON)
            for j in range(8):
                src = pl.ds(pl.multiple_of(block_order(y, x_lo, j) * BLK, BLK), BLK)
                dst = pl.ds(j * BLK, BLK)
                gain = jnp.concatenate([small[j, 0:1, :], small[j, 1:2, :]], axis=1)
                shift = jnp.concatenate([small[j, 2:3, :], small[j, 3:4, :]], axis=1)
                u = (tok[at, src].astype(F32) - mean) * inv
                n = u * gain + shift
                normed[at, dst] = n.astype(BF16)
                normed_t[dst, at] = n.T.astype(BF16)
                unit[at, dst] = u.astype(BF16)
                g = grad[at, src]
                g32 = g.astype(F32)
                grad_rel[at, dst] = g
                grad_t[dst, at] = g32.T.astype(BF16)
                bias_sum[:, dst] += jnp.sum(g32, axis=0, keepdims=True)

    prepare(0, 8)
    saved = [here(normed_t, normed_t_out), here(grad_t, grad_t_out), here(unit, unit_out), here(small, small_out),
             here(bias_sum, bias_out)]

    biases = small[0, 6:20, :]
    for j in range(1, 8):
        biases = biases + small[j, 6:20, :]
    qkv_bias = jnp.concatenate([biases[j : j + 1] for j in range(6)], axis=1)
    up_bias = jnp.concatenate([biases[j : j + 1] for j in range(6, 14)], axis=1)
    big = 256
    keys_part.arrived()

    @pl.loop(0, ROWS // big)
    def _(i):
        at = pl.ds(pl.multiple_of(i * big, big), big)
        raw = jnp.dot(normed[at, :], w1[:, : 2 * BLK], preferred_element_type=F32) + qkv_bias[:, : 2 * BLK]
        c, s = cos[at, :], sin[at, :]
        for k in range(2):
            lanes = slice(k * 128, (k + 1) * 128)
            kv[at, lanes] = turn(raw[:, lanes], c, s).astype(BF16)
        kv[at, BLK:] = raw[:, BLK:].astype(BF16)

    kv_copy = copies.make(kv, kvr_out, over)

    @pl.when(x_hi == 0)
    def _():
        kv_copy.start()

    saved.append(here(kv, kv_out))
    rest_part.begin_x()
    down_a.begin_x()
    up_part.forward()
    down_a.forward()
    up_part.arrived()
    saved.append(here(w2, w2_out))

    @pl.loop(0, ROWS // big)
    def _(i):
        at = pl.ds(pl.multiple_of(i * big, big), big)
        v = jnp.dot(normed[at, :], w2[...], preferred_element_type=F32) + up_bias
        sq = v * v
        t = jnp.tanh(GELU_C * v * (1.0 + 0.044715 * sq))
        half = 0.5 * (1.0 + t)
        active[at, :] = (v * half).astype(BF16)
        slope[at, :] = (half + 0.5 * v * (1.0 - t * t) * (GELU_C * (1.0 + 3 * 0.044715 * sq))).astype(BF16)

    saved.append(here(active, active_out))

    place = [buf.at[:, pl.ds(k * 1024, 1024)] for buf in (tok, grad) for k in range(2)]

    def partials(left, right, blocks, dst, out):
        for k, j in enumerate(blocks):
            at = pl.ds((k % 4) * BLK, BLK)
            dst[k // 4][at, :] = jnp.dot(left[j * BLK : (j + 1) * BLK, :], right[...], preferred_element_type=F32).astype(BF16)
            saved.append(here(dst[k // 4].at[at], out.at[k]))

    partials(grad_t, active, (4, 5, 6, 7), place[:1], a_s1_out)
    rest_part.forward()
    down_a.arrived()
    down_b.all_arrived()
    saved.append(here(w3, w3_out))

    @pl.loop(0, ROWS // big)
    def _(i):
        at = pl.ds(pl.multiple_of(i * big, big), big)
        v = jnp.dot(grad_rel[at, :], w3[...], preferred_element_type=F32) * slope[at, :].astype(F32)
        low = v.astype(BF16)
        hidden[at, :] = low
        up_bias_sum[...] += jnp.sum(low.astype(F32), axis=0, keepdims=True)

    saved += [here(hidden, hidden_out), here(up_bias_sum, up_bias_out)]
    partials(normed_t, hidden, (2, 6, 1, 5, 3, 7), place[1:3], b_s1_out)
    rest_part.arrived()
    saved.append(here(w1, w1_out))

    @pl.loop(0, ROWS // big)
    def _(i):
        at = pl.ds(pl.multiple_of(i * big, big), big)
        raw = jnp.dot(normed[at, :], w1[:, 2 * BLK : 3 * BLK], preferred_element_type=F32) + qkv_bias[:, 2 * BLK :]
        c, s = cos[at, :], sin[at, :]
        for k in range(2):
            lanes = slice(k * 128, (k + 1) * 128)
            q[at, lanes] = (turn(raw[:, lanes], c, s).astype(BF16).astype(F32) * (HD**-0.5)).astype(BF16)
        do[at, :] = jnp.dot(grad_rel[at, :], w1[:, 3 * BLK :], preferred_element_type=F32).astype(BF16)

    saved += [here(q, q_out), here(do, do_out)]
    for copy in copies.sent:
        copy.wait_send()

    @pl.when(x_hi == 0)
    def _():
        kv_copy.wait_send()

    @pl.when(x_hi == 1)
    def _():
        kv_copy.wait_recv()

    for copy in saved:
        copy.wait()


def gather_call(*args):
    n = 1024
    low = lambda *shape: jax.ShapeDtypeStruct(shape, BF16)
    wide = lambda *shape: jax.ShapeDtypeStruct(shape, F32)
    vlow = lambda *shape: pltpu.VMEM(shape, BF16)
    vwide = lambda *shape: pltpu.VMEM(shape, F32)
    anywhere = pl.BlockSpec(memory_space=pl.ANY)
    return pl.pallas_call(
        gather_kernel,
        in_specs=[anywhere] * 8,
        out_specs=[anywhere] * 17,
        out_shape=[
            low(D, n), low(D, n), low(D, n), low(D, ROWS), low(D, ROWS), low(ROWS, D), low(ROWS, BLK), low(ROWS, 2 * BLK),
            low(ROWS, 2 * BLK), low(ROWS, BLK), low(ROWS, n), low(ROWS, n), wide(8, PACK, 128), wide(1, D), wide(1, n),
            low(4, BLK, n), low(6, BLK, n),
        ],
        scratch_shapes=[
            vlow(D, n), vlow(D, n), vlow(D, n), vlow(ROWS, D), vlow(ROWS, D), vlow(ROWS, D), vlow(ROWS, D), vlow(D, ROWS),
            vlow(D, ROWS), vlow(ROWS, D), vwide(8, PACK, 128), vlow(ROWS, BLK), vlow(ROWS, 2 * BLK), vlow(ROWS, BLK),
            vlow(ROWS, n), vlow(ROWS, n), vlow(ROWS, n), vwide(ROWS, 128), vwide(ROWS, 128), vwide(192, 128), vwide(1, D),
            vwide(1, n), vlow(BLK, BLK), vlow(n, BLK),
            pltpu.SemaphoreType.DMA((56,)),
            pltpu.SemaphoreType.DMA((56,)),
            pltpu.SemaphoreType.DMA((40,)),
        ],
        compiler_params=params(collective_id=0, has_side_effects=True),
        cost_estimate=cost(2 * ROWS * D * 3 * n, 64 * 1024 * 1024),
        name="gather_phase",
    )(*args)


def grads_kernel(attn, up, down, qkv_out, proj_out, up_out, down_out):
    for core in range(2):
        for k, c in enumerate((1, 2, 0)):
            qkv_out[:, c, core * BLK : (core + 1) * BLK] = attn[core, :, k * BLK : (k + 1) * BLK].astype(F32)
        proj_out[core * BLK : (core + 1) * BLK, :] = attn[core, :, 3 * BLK :].astype(F32).T
        up_out[:, core * 1024 : (core + 1) * 1024] = up[core].astype(F32)
        down_out[core * 1024 : (core + 1) * 1024, :] = down[core].astype(F32).T


def grads_call(attn, up, down):
    tile = 128
    piece = pl.BlockSpec((2, tile, 1024), lambda i: (0, i, 0))
    wide = lambda *shape: jax.ShapeDtypeStruct(shape, F32)
    return pl.pallas_call(
        grads_kernel,
        grid=(BLK // tile,),
        in_specs=[piece] * 3,
        out_specs=[
            pl.BlockSpec((tile, 3, HALF), lambda i: (i, 0, 0)),
            pl.BlockSpec((HALF, tile), lambda i: (0, i)),
            pl.BlockSpec((tile, 2048), lambda i: (i, 0)),
            pl.BlockSpec((2048, tile), lambda i: (0, i)),
        ],
        out_shape=[wide(BLK, 3, HALF), wide(HALF, BLK), wide(BLK, 2048), wide(2048, BLK)],
        compiler_params=params(),
        cost_estimate=cost(0, 10 * 1024 * 1024),
        name="gradients",
    )(attn, up, down)


class Lefts:
    def __init__(self, sources, buf, sems):
        self.sources, self.buf, self.sems = sources, buf, sems
        self.queue, self.count = ([], []), [0, 0]

    def want(self, kind, j):
        if any(held == j for held, _ in self.queue[kind]):
            return
        slot = self.count[kind] % 2
        self.count[kind] += 1
        self.move(kind, j, slot).start()
        self.queue[kind].append((j, slot))

    def take(self, kind, j):
        held, slot = self.queue[kind].pop(0)
        assert held == j
        self.move(kind, j, slot).wait()
        return self.buf.at[kind, slot]

    def move(self, kind, j, slot):
        return pltpu.make_async_copy(
            self.sources[kind].at[pl.ds(j * BLK, BLK)], self.buf.at[kind, slot], self.sems.at[kind, slot]
        )

    def run(self, jobs, after=()):
        for i, (kinds, j, act) in enumerate(jobs):
            for kind in kinds:
                self.want(kind, j)
            ahead = jobs[i + 1][:2] if i + 1 < len(jobs) else after
            if ahead:
                for kind in ahead[0]:
                    self.want(kind, ahead[1])
            act(*[self.take(kind, j) for kind in kinds])


def product(dst, lefts, rights, adds=()):
    at = 0
    for left, right in zip(lefts, rights):
        cols = slice(at, at + right.shape[1])
        total = jnp.dot(left[...], right[...], preferred_element_type=F32)
        for add in adds:
            total += add[:, cols].astype(F32)
        dst[:, cols] = total.astype(BF16)
        at += right.shape[1]


def row_products(half, a, b, w1, col1, w2, out, unit=None, ub=None, sems=None, vec=None):
    nt = (((1,), (1,)), ((), ()))
    ka = a.shape[1]
    rows = pl.ds(pl.multiple_of(half * HALF, HALF), HALF)

    def fetch(j, slot):
        at = pl.ds(pl.multiple_of(j * HALF, HALF), HALF)
        return pltpu.make_async_copy(unit.at[rows, at], ub.at[slot], sems.at[slot])

    if unit is not None:
        fetch(0, 0).start()

    @pl.loop(0, D // HALF)
    def _(j):
        at = pl.ds(pl.multiple_of(j * HALF, HALF), HALF)
        slot = lax.rem(j, 2)
        if unit is not None:
            fetch(j, slot).wait()

            @pl.when(j < D // HALF - 1)
            def _():
                fetch(j + 1, 1 - slot).start()

        total = lax.dot_general(a[rows, :], w1[at, col1 : col1 + ka], nt, preferred_element_type=F32)
        total += lax.dot_general(b[rows, :], w2[at, :], nt, preferred_element_type=F32)
        out[:, at] = total.astype(BF16)
        if unit is not None:
            weighted = jnp.sum(total * ub[slot].astype(F32), axis=0, keepdims=True)
            plain = jnp.sum(total, axis=0, keepdims=True)
            for k in range(2):
                vec[2 * j + k, 0:1, :] = weighted[:, k * BLK : (k + 1) * BLK]
                vec[2 * j + k, 1:2, :] = plain[:, k * BLK : (k + 1) * BLK]


def add_rows(mine, got):
    @pl.loop(0, 4)
    def _(i):
        at = pl.ds(pl.multiple_of(i * 128, 128), 128)
        mine[at, :] = (mine[at, :].astype(F32) + got[at, :].astype(F32)).astype(BF16)


def reduce_kernel(w1, w2, w3, normed_t, grad_t, unit, q_in, kv_in, kvr_in, do_in, active_in, hidden_in, small_in, bias_in,
                  up_bias_in, a_s1, b_s1, tok_in, grad_in, table_in,
                  layer_out, input_grad, piece1, piece2, piece3, vec_out,
                  a_r1, a_r2, a_x, b_p, b_r1, b_r2, b_x, c_r1, d_r1,
                  q, do, active, hidden, att, raw, small, cos, sin, cos_r, sin_r, table,
                  dk, dv, out_t, dq_t, dkv, ub, theirs, br_m, br_c, br_z, br_o, ng_m, ng_c, ng_z, ng_o,
                  turned, tok, grad, left_buf, stage, a_s2, a_m, b_s2, b_m, c_s1, c_s2, c_m, d_s1, d_s2, d_m, c_r2, c_x, d_r2, d_x,
                  vec_t, vec_m, va, va_r, vb_r, units, my, my_r, mx, mx_r, last, last_r, bias_v, up_bias_v, vec_v,
                  send, recv, local, sems, left_sems, stage_sems):
    x, y, z, core = coords()
    x_lo, x_hi = lax.rem(x, 2), x // 2
    other = 1 - core
    up, down, far = beside(dy=1), beside(dy=3), beside(dy=2)
    right, left, over = beside(dx=1), beside(dx=3), beside(dx=2)
    mate = beside(flip=1)
    above, below = beside(dz=1), beside(dz=3)
    along = [above, beside(dz=2), below]
    copies = Copies(send, recv, local)
    here, remote = copies.here, copies.remote
    nt = (((1,), (1,)), ((), ()))

    load_active, load_hidden = here(active_in, active), here(hidden_in, hidden)
    own_keys = pl.ds(pl.multiple_of(x_hi * ROWS, ROWS), ROWS)
    loads = [here(table_in, table), here(q_in, q), here(do_in, do), here(small_in, small), here(bias_in, bias_v),
              here(up_bias_in, up_bias_v)]
    z_rows = pl.ds(pl.multiple_of(z * 128, 128), 128)
    loads += [here(tok_in.at[z_rows], tok), here(grad_in.at[z_rows], grad)]
    greet([up, down, far, right, left, over, mate] + along)
    lo, hi, first, second = pl.ds(0, 512), pl.ds(512, 512), pl.ds(0, 2), pl.ds(2, 2)
    bp = [remote(b_s1.at[first, :, lo], b_p.at[first], up), remote(b_s1.at[first, :, hi], b_p.at[second], down)]
    b1 = [
        remote(b_s1.at[second, :, hi], b_r1.at[first, :, hi], up),
        remote(b_s1.at[pl.ds(4, 2), :, lo], b_r1.at[second, :, lo], down),
    ]
    a1 = [remote(a_s1.at[pl.ds(2 * k, 2)], a_r1.at[pl.ds(2 * k, 2)], target) for k, target in enumerate((right, left))]

    lefts = Lefts((normed_t, grad_t), left_buf, left_sems)

    def staged(parts):
        views, found = [], []
        for k, part in enumerate(parts):
            view = stage.at[k, :, pl.ds(0, part.shape[-1])]
            copy = pltpu.make_async_copy(part, view, stage_sems.at[k])
            copy.start()
            found.append(copy)
            views.append(view)
        for copy in found:
            copy.wait()
        return views

    def arrived(moves):
        for copy in moves:
            copy.wait_recv()

    def settle(mine, got, move, piece, cols, on_hbm):
        move.wait_send()
        copies.sent = [copy for copy in copies.sent if copy is not move]
        move.wait_recv()
        more = staged([got])[0] if on_hbm else got
        mine[...] = (mine[...].astype(F32) + more[...].astype(F32)).astype(BF16)
        spot = piece.at[core, :, cols]
        return here(mine, spot), remote(mine, spot, mate)

    def turn_back(v, c, s):
        return v * c - partner(v) * s

    upper, lower = pl.ds(0, BLK // 2), pl.ds(BLK // 2, BLK // 2)
    pairs_back = [copies.make(dkv.at[k], dkv.at[k], over) for k in range(2)]
    passed = [
        copies.make(c_s1.at[first], b_r1.at[first, :, lo], up),
        copies.make(c_s1.at[second], b_r1.at[second, :, hi], down),
    ]
    a_y = [copies.make(a_s2.at[k], a_r2.at[k], target) for k, target in enumerate((far, down, up))]
    b2 = [copies.make(b_s2.at[upper], b_r2.at[upper], right), copies.make(b_s2.at[lower], b_r2.at[lower], left)]
    copies.sent += passed + a_y + b2

    def attend(keys, vals, keys_t, vals_t, st, dp, qm, dom):
        own = here(kv_in.at[:, pl.ds(0, BLK)], keys.at[own_keys]), here(kv_in.at[:, pl.ds(BLK, BLK)], vals.at[own_keys])
        far_keys = pltpu.make_async_copy(kvr_in.at[:, pl.ds(0, BLK)], keys.at[pl.ds(0, ROWS)], local.at[copies.locals])
        far_vals = pltpu.make_async_copy(kvr_in.at[:, pl.ds(BLK, BLK)], vals.at[pl.ds(0, ROWS)], local.at[copies.locals + 1])
        copies.locals += 2

        @pl.when(x_hi == 1)
        def _():
            far_keys.start()
            far_vals.start()
        for copy in loads + list(own):
            copy.wait()

        @pl.when(x_hi == 1)
        def _():
            far_keys.wait()
            far_vals.wait()

        @pl.loop(0, (x_hi + 1) * (ROWS // KC))
        def _(j):
            at = pl.ds(pl.multiple_of(j * KC, KC), KC)
            keys_t[:, at] = keys[at, :].astype(F32).T.astype(BF16)
            vals_t[:, at] = vals[at, :].astype(F32).T.astype(BF16)
            dk[at, :] = jnp.zeros((KC, BLK), F32)
            dv[at, :] = jnp.zeros((KC, BLK), F32)

        rope_rows(table, x_hi * ROWS, cos, sin, ROWS)
        rope_rows(table, 0, cos_r, sin_r, ROWS)
        lane = lax.broadcasted_iota(jnp.int32, (QT, 128), 1) // HD

        def heads(pair, tiles):
            lanes = slice(pair * 128, pair * 128 + 128)
            for t in tiles:
                rows = slice(t * QT, (t + 1) * QT)
                chunks = x_hi * (ROWS // KC) + t * QT // KC + 1
                for side in range(2):
                    qm[side] = jnp.where(lane == side, q[rows, lanes], jnp.zeros((), BF16))
                    dom[side] = jnp.where(lane == side, do[rows, lanes], jnp.zeros((), BF16))

                def score(j, tops, masked):
                    at = pl.ds(pl.multiple_of(j * KC, KC), KC)
                    new = []
                    for side in range(2):
                        s = lax.dot_general(keys[at, lanes], qm[side], nt, preferred_element_type=F32)
                        if masked:
                            ki = lax.broadcasted_iota(jnp.int32, (KC, QT), 0)
                            qi = lax.broadcasted_iota(jnp.int32, (KC, QT), 1) + t * QT % KC
                            s = jnp.where(ki <= qi, s, MASKED)
                        st[side, at, :] = s
                        new.append(jnp.maximum(tops[side], jnp.max(s, axis=0, keepdims=True)))
                    return tuple(new)

                low = jnp.full((1, QT), MASKED, F32)
                tops = lax.fori_loop(0, chunks - 1, lambda j, m: score(j, m, False), (low, low))
                tops = score(chunks - 1, tops, True)

                def weigh(j, carry):
                    at = pl.ds(pl.multiple_of(j * KC, KC), KC)
                    new = []
                    for side in range(2):
                        total, dot = carry[2 * side : 2 * side + 2]
                        p = jnp.exp(st[side, at, :] - tops[side])
                        st[side, at, :] = p
                        d = lax.dot_general(vals[at, lanes], dom[side], nt, preferred_element_type=F32)
                        dp[side, at, :] = d
                        new.append(total + jnp.sum(p, axis=0, keepdims=True))
                        new.append(dot + jnp.sum(p * d, axis=0, keepdims=True))
                    return tuple(new)

                zero = jnp.zeros((1, QT), F32)
                sums = lax.fori_loop(0, chunks, weigh, (zero,) * 4)
                inv = [1.0 / sums[0], 1.0 / sums[2]]
                delta = [sums[1] * inv[0], sums[3] * inv[1]]
                out_t[:, rows] = jnp.zeros((128, QT), F32)
                dq_t[:, rows] = jnp.zeros((128, QT), F32)

                def spread(j, _):
                    at = pl.ds(pl.multiple_of(j * KC, KC), KC)
                    new_v, new_k = dv[at, lanes], dk[at, lanes]
                    for side in range(2):
                        hrows = slice((2 * pair + side) * HD, (2 * pair + side + 1) * HD)
                        trows = slice(side * HD, (side + 1) * HD)
                        p = st[side, at, :] * inv[side]
                        p_low = p.astype(BF16)
                        ds = (p * (dp[side, at, :] - delta[side])).astype(BF16)
                        out_t[trows, rows] += jnp.dot(vals_t[hrows, at], p_low, preferred_element_type=F32)
                        dq_t[trows, rows] += jnp.dot(keys_t[hrows, at], ds, preferred_element_type=F32)
                        new_v += jnp.dot(p_low, dom[side], preferred_element_type=F32)
                        new_k += jnp.dot(ds, qm[side], preferred_element_type=F32)
                    dv[at, lanes] = new_v
                    dk[at, lanes] = new_k
                    return 0

                lax.fori_loop(0, chunks, spread, 0)

        def end_pair(pair):
            lanes = slice(pair * 128, pair * 128 + 128)
            copy = pairs_back[pair]

            @pl.when(x_hi == 1)
            def _():
                dkv[pair, :, :128] = turn_back(dk[:ROWS, lanes], cos_r[...], sin_r[...]).astype(BF16)
                dkv[pair, :, 128:] = dv[:ROWS, lanes].astype(BF16)
                copy.start()

            for t in range(ROWS // 512):
                rows = slice(t * 512, (t + 1) * 512)
                att[rows, lanes] = out_t[:, rows].T.astype(BF16)
                raw[rows, 2 * BLK + pair * 128 : 2 * BLK + pair * 128 + 128] = turn_back(
                    dq_t[:, rows].T * (HD**-0.5), cos[rows, :], sin[rows, :]
                ).astype(BF16)

        heads(0, (0, 1, 2))

        def pass_blocks(move, own, got, cols, buf):
            move.wait_recv()
            views = staged([b_s1.at[own, :, cols], b_p.at[got], b_s1.at[own + 1, :, cols], b_p.at[got + 1]])
            for k in range(2):
                c_s1[buf + k] = (views[2 * k][...].astype(F32) + views[2 * k + 1][...].astype(F32)).astype(BF16)
            passed[buf // 2].start()

        pass_blocks(bp[0], 2, 0, lo, 0)
        pass_blocks(bp[1], 4, 2, hi, 2)
        heads(0, (3,))
        end_pair(0)

        load_active.wait()
        lefts.want(1, 2)
        arrived(a1)
        s = staged([a_r1.at[2], a_r1.at[3], a_r1.at[1]])
        lefts.run(
            [((1,), j, lambda l, k=k: product(a_s2.at[k], [l], [active], [s[k]])) for k, j in enumerate((2, 3, 1))],
            after=((0,), 4),
        )
        for copy in a_y:
            copy.start()
        heads(1, (0, 1, 2))

        load_hidden.wait()
        arrived(b1 + passed)
        s = staged([b_r1.at[1], b_r1.at[3]])
        lefts.run([((0,), 4, lambda l: product(b_s2, [l], [hidden], s))], after=((0, 1), 2))
        for copy in b2:
            copy.start()
        heads(1, (3,))
        end_pair(1)

    pl.run_scoped(
        attend,
        pltpu.VMEM((2 * ROWS, BLK), BF16),
        pltpu.VMEM((2 * ROWS, BLK), BF16),
        pltpu.VMEM((BLK, 2 * ROWS), BF16),
        pltpu.VMEM((BLK, 2 * ROWS), BF16),
        pltpu.VMEM((2, 2 * ROWS, QT), F32),
        pltpu.VMEM((2, 2 * ROWS, QT), F32),
        pltpu.VMEM((2, QT, 128), BF16),
        pltpu.VMEM((2, QT, 128), BF16),
    )
    def finish(w1v, w2v, w3v):
        w_loads = [here(w1, w1v), here(w3, w3v), here(w2, w2v)]

        def z_at(dz, first=0, count=128):
            return pl.ds(pl.multiple_of(lax.rem(z + dz, 4) * 128 + first, 64), count)

        def to_z(total, got):
            return [
                remote(total.at[z_at(2, 0, 64)], got.at[0, pl.ds(0, 64)], above),
                remote(total.at[z_at(2, 64, 64)], got.at[0, pl.ds(64, 64)], below),
                remote(total.at[z_at(1, 64, 64)], got.at[1, pl.ds(64, 64)], above),
                remote(total.at[z_at(3, 0, 64)], got.at[2, pl.ds(0, 64)], below),
            ]

        def pass_on(total, got, first, buf):
            first[0].wait_recv()
            buf[0] = (total[z_at(1, 0, 64), :].astype(F32) + got[0, :64, :].astype(F32)).astype(BF16)
            one = remote(buf.at[0], got.at[1, pl.ds(0, 64)], above)
            first[1].wait_recv()
            buf[1] = (total[z_at(3, 64, 64), :].astype(F32) + got[0, 64:, :].astype(F32)).astype(BF16)
            two = remote(buf.at[1], got.at[2, pl.ds(64, 64)], below)
            return [first[2], first[3], one, two]

        def from_z(chunk, rows):
            at = z_at(0)
            return [here(chunk, rows.at[at]), remote(chunk, rows.at[at], above), remote(chunk, rows.at[at], below)]

        def pass_rows(moves, rows):
            moves[1].wait_recv()
            one = remote(rows.at[z_at(3, 0, 64)], rows.at[z_at(3, 0, 64)], above)
            moves[2].wait_recv()
            two = remote(rows.at[z_at(1, 64, 64)], rows.at[z_at(1, 64, 64)], below)
            return moves[0], [one, two]

        tail = [raw.at[:, pl.ds(2 * BLK, BLK)], att]
        d1 = []
        for k, (j, target) in enumerate(((2, far), (1, up), (3, down))):
            jobs = [((0, 1), j + 4 * i, lambda a, b, i=i: product(d_s1.at[2 * k + i], [a, b], tail)) for i in range(2)]
            lefts.run(jobs, after=((0, 1), (1, 3)[k]) if k < 2 else ((0,), 0))
            d1.append(remote(d_s1.at[pl.ds(2 * k, 2)], d_r1.at[pl.ds(2 * k, 2)], target))

        for copy in w_loads[:2]:
            copy.wait()
        row_products(other, att, active, w1v, 3 * BLK, w3v, theirs)
        br_core = remote(theirs, br_c, mate)
        row_products(core, att, active, w1v, 3 * BLK, w3v, br_m)

        arrived(b2)
        s = staged([b_r1.at[0], b_r1.at[2], b_r2])
        lefts.run([((0,), 0, lambda l: product(b_m, [l], [hidden], s))], after=((0,), 2))
        b3 = remote(b_m, b_x, over)

        br_core.wait_recv()
        add_rows(br_m, br_c)
        br1 = to_z(br_m, br_z)


        def local_grads(pair, more):
            lanes = slice(pair * 128, pair * 128 + 128)
            k = turn_back(dk[own_keys, lanes], cos[...], sin[...])
            v = dv[own_keys, lanes]
            if more:
                k = k + dkv[pair, :, :128].astype(F32)
                v = v + dkv[pair, :, 128:].astype(F32)
            raw[:, lanes] = k.astype(BF16)
            raw[:, BLK + pair * 128 : BLK + pair * 128 + 128] = v.astype(BF16)

        for pair, copy in enumerate(pairs_back):

            @pl.when(x_hi == 1)
            def _():
                local_grads(pair, False)
                copy.wait_send()

            @pl.when(x_hi == 0)
            def _():
                copy.wait_recv()
                local_grads(pair, True)

        br_core.wait_send()
        copies.sent = [copy for copy in copies.sent if copy is not br_core]
        w_loads[2].wait()
        row_products(other, raw, hidden, w1v, 0, w2v, theirs, unit, ub, sems, vec_t)
        ng_core = remote(theirs, ng_c, mate)

        for copy in passed:
            copy.wait_send()
        copies.sent = [copy for copy in copies.sent if all(copy is not old for old in passed)]
        pairs = raw.at[:, pl.ds(0, 512)]
        c1 = []
        for k, (j, target) in enumerate(((2, far), (1, up), (3, down))):
            jobs = [((0,), j + 4 * i, lambda l, i=i: product(c_s1.at[2 * k + i], [l], [pairs])) for i in range(2)]
            lefts.run(jobs, after=((0,), (1, 3)[k]) if k < 2 else ((1,), 0))
            c1.append(remote(c_s1.at[pl.ds(2 * k, 2)], c_r1.at[pl.ds(2 * k, 2)], target))

        row_products(core, raw, hidden, w1v, 0, w2v, ng_m, unit, ub, sems, vec_m)
        br2 = pass_on(br_m, br_z, br1, turned.at[0])
        ng_core.wait_recv()
        add_rows(ng_m, ng_c)
        ng1 = to_z(ng_m, ng_z)

        arrived(a_y)
        s = staged([a_r1.at[0], a_r2.at[0], a_r2.at[1], a_r2.at[2]])
        lefts.run([((1,), 0, lambda l: product(a_m, [l], [active], s))], after=((0, 1), 4))
        a3 = remote(a_m, a_x, over)

        arrived(d1)
        s = staged([d_r1.at[1], d_r1.at[3], d_r1.at[5]])
        lefts.run([((0, 1), 4, lambda a, b: product(d_s2, [a, b], tail, s))], after=((0, 1), 0))
        d2 = [remote(d_s2.at[upper], d_r2.at[upper], right), remote(d_s2.at[lower], d_r2.at[lower], left)]

        va[...] = jnp.zeros_like(va)
        for j in range(8):
            va[j, 0:2, :] = vec_t[j, 0:2, :] + vec_m[j, 0:2, :]
        va_sent = [remote(va, va_r.at[k], along[k]) for k in range(3)]

        arrived(br2)
        tile = 32

        def share(total, got, i, j):
            at = pl.ds(pl.multiple_of(i * tile, tile), tile)
            from_all = pl.ds(pl.multiple_of(z * 128 + i * tile, tile), tile)
            cols = slice(j * BLK, (j + 1) * BLK)
            return total[from_all, cols].astype(F32) + (got[1, at, cols].astype(F32) + got[2, at, cols].astype(F32))

        def line(row, j):
            return jnp.concatenate([small[j, row : row + 1, :], small[j, row + 1 : row + 2, :]], axis=1)

        def spot(j):
            return pl.ds(pl.multiple_of(block_order(y, x_lo, j) * BLK, BLK), BLK)

        @pl.loop(0, 128 // tile)
        def _(i):
            at = pl.ds(pl.multiple_of(i * tile, tile), tile)
            for j in range(8):
                value = tok[at, spot(j)].astype(F32) + share(br_m, br_z, i, j) + line(4, j)
                br_o[at, spot(j)] = value.astype(BF16)

        ng2 = pass_on(ng_m, ng_z, ng1, turned.at[1])

        br3 = from_z(br_o, layer_out)
        arrived(d2)
        s = staged([d_r1.at[0], d_r1.at[2], d_r1.at[4]]) + [d_r2]
        lefts.run([((0, 1), 0, lambda a, b: product(d_m, [a, b], tail, s))], after=((0,), 4))
        d3 = remote(d_m, d_x, over)

        b4 = settle(b_m, b_x, b3, piece2, pl.ds(0, 1024), True)
        arrived(ng2)

        @pl.loop(0, 128 // tile)
        def _(i):
            at = pl.ds(pl.multiple_of(i * tile, tile), tile)
            rows = tok[at, :].astype(F32)
            mean = jnp.mean(rows, axis=-1, keepdims=True)
            centered = rows - mean
            inv = lax.rsqrt(jnp.mean(centered * centered, axis=-1, keepdims=True) + EPSILON)

            def terms(j):
                u = (tok[at, spot(j)].astype(F32) - mean) * inv
                return u, share(ng_m, ng_z, i, j) * line(0, j)

            first = second = jnp.zeros((tile, 1), F32)
            for j in range(8):
                u, g = terms(j)
                first += jnp.sum(g, axis=-1, keepdims=True)
                second += jnp.sum(g * u, axis=-1, keepdims=True)
            first, second = first / D, second / D
            for j in range(8):
                u, g = terms(j)
                ng_o[at, spot(j)] = (grad[at, spot(j)].astype(F32) + inv * (g - first - u * second)).astype(BF16)

        ng3 = from_z(ng_o, input_grad)
        arrived(c1)
        s = staged([c_r1.at[1], c_r1.at[3], c_r1.at[5]])
        lefts.run([((0,), 4, lambda l: product(c_s2, [l], [pairs], s))], after=((0,), 0))
        c2 = [remote(c_s2.at[upper], c_r2.at[upper], right), remote(c_s2.at[lower], c_r2.at[lower], left)]

        br_own, br4 = pass_rows(br3, layer_out)

        for copy in va_sent:
            copy.wait_recv()
        vec_v[0] = (va[...] + va_r[1]) + (va_r[0] + va_r[2])
        vb = remote(vec_v.at[0], vb_r, mate)

        vb.wait_recv()
        units[...] = jnp.zeros_like(units)
        units[0:3, :] = jnp.sum(raw[...].astype(F32), axis=0, keepdims=True).reshape(3, BLK)
        for j in range(4):
            units[3 + j : 4 + j, :] = up_bias_v[:, j * BLK : (j + 1) * BLK]
        for j in range(8):
            dy, dx = j % 4, j // 4
            my[dy, dx] = vec_v[0, j] + vb_r[j]
            my[dy, dx, 2:3, :] = bias_v[:, j * BLK : (j + 1) * BLK]
        for dy in range(4):
            my[dy, 2] = units[...]
        my_sent = [remote(my.at[1], my_r.at[0], up), remote(my.at[2], my_r.at[1], far), remote(my.at[3], my_r.at[2], down)]

        arrived(c2)
        s = staged([c_r1.at[0], c_r1.at[2], c_r1.at[4]]) + [c_r2]
        lefts.run([((0,), 0, lambda l: product(c_m, [l], [pairs], s))])
        c3 = remote(c_m, c_x, over)

        a4 = settle(a_m, a_x, a3, piece3, pl.ds(0, 1024), True)
        d4 = settle(d_m, d_x, d3, piece1, pl.ds(512, 512), False)

        ng_own, ng4 = pass_rows(ng3, input_grad)
        arrived(my_sent)
        here_sum = (my[0] + my_r[1]) + (my_r[0] + my_r[2])
        mx[0, 0] = here_sum[0]
        mx[0, 1] = here_sum[2]
        mx[1, 0] = here_sum[1]
        mx[1, 1] = here_sum[2]
        mx_sent = [remote(mx.at[1], mx_r.at[0], right), remote(mx.at[0], mx_r.at[1], over), remote(mx.at[1], mx_r.at[2], left)]
        arrived(mx_sent)
        last[...] = (mx[0] + mx_r[1]) + (mx_r[0] + mx_r[2])
        vec_copy = remote(last.at[1], last_r, mate)
        c4 = settle(c_m, c_x, c3, piece1, pl.ds(0, 512), False)
        vec_copy.wait_recv()
        last_saved = [here(last, vec_out.at[pl.ds(0, 2)]), here(last_r, vec_out.at[2])]

        for own, copy in (a4, b4, c4, d4):
            own.wait()
            copy.wait_recv()
        br_own.wait()
        ng_own.wait()
        arrived(br4 + ng4)
        for copy in last_saved:
            copy.wait()
        for copy in copies.sent:
            copy.wait_send()

    pl.run_scoped(
        finish,
        pltpu.VMEM((D, 1024), BF16),
        pltpu.VMEM((D, 1024), BF16),
        pltpu.VMEM((D, 1024), BF16),
    )


def reduce_call(*args):
    low = lambda *shape: jax.ShapeDtypeStruct(shape, BF16)
    wide = lambda *shape: jax.ShapeDtypeStruct(shape, F32)
    vlow = lambda *shape: pltpu.VMEM(shape, BF16)
    vwide = lambda *shape: pltpu.VMEM(shape, F32)
    anywhere = pl.BlockSpec(memory_space=pl.ANY)
    n = 1024
    outs = [low(HALF, D), low(HALF, D), low(2, BLK, n), low(2, BLK, n), low(2, BLK, n), wide(3, 8, BLK)] + [
        low(4, BLK, n), low(3, BLK, n), low(BLK, n), low(4, BLK, 512), low(4, BLK, n), low(BLK, n), low(BLK, n),
        low(6, BLK, 512), low(6, BLK, 512),
    ]
    result = pl.pallas_call(
        reduce_kernel,
        in_specs=[anywhere] * 20,
        out_specs=[anywhere] * len(outs),
        out_shape=outs,
        scratch_shapes=[
            vlow(ROWS, BLK), vlow(ROWS, BLK), vlow(ROWS, n), vlow(ROWS, n), vlow(ROWS, BLK), vlow(ROWS, 3 * BLK),
            vwide(8, PACK, 128), vwide(ROWS, 128), vwide(ROWS, 128), vwide(ROWS, 128), vwide(ROWS, 128), vwide(192, 128),
            vwide(2 * ROWS, BLK), vwide(2 * ROWS, BLK), vwide(128, ROWS), vwide(128, ROWS), vlow(2, ROWS, BLK),
            vlow(2, HALF, HALF), vlow(HALF, D), vlow(HALF, D), vlow(HALF, D), vlow(3, 128, D), vlow(128, D),
            vlow(HALF, D), vlow(HALF, D), vlow(3, 128, D), vlow(128, D), vlow(2, 2, 64, D), vlow(128, D), vlow(128, D),
            vlow(2, 2, BLK, ROWS), vlow(4, BLK, n), vlow(3, BLK, n), vlow(BLK, n), vlow(BLK, n), vlow(BLK, n),
            vlow(6, BLK, 512), vlow(BLK, 512), vlow(BLK, 512), vlow(6, BLK, 512), vlow(BLK, 512), vlow(BLK, 512),
            vlow(BLK, 512), vlow(BLK, 512), vlow(BLK, 512), vlow(BLK, 512), vwide(8, 8, BLK), vwide(8, 8, BLK),
            vwide(8, 8, BLK), vwide(3, 8, 8, BLK), vwide(8, 8, BLK), vwide(8, BLK), vwide(4, 3, 8, BLK),
            vwide(3, 3, 8, BLK), vwide(2, 2, 8, BLK), vwide(3, 2, 8, BLK), vwide(2, 8, BLK), vwide(8, BLK),
            vwide(1, D), vwide(1, n), vwide(1, 8, 8, BLK),
            pltpu.SemaphoreType.DMA((72,)),
            pltpu.SemaphoreType.DMA((72,)),
            pltpu.SemaphoreType.DMA((32,)),
            pltpu.SemaphoreType.DMA((2,)),
            pltpu.SemaphoreType.DMA((2, 2)),
            pltpu.SemaphoreType.DMA((4,)),
        ],
        compiler_params=params(collective_id=1, has_side_effects=True),
        cost_estimate=cost(2 * ROWS * D * 5 * 1024, 128 * 1024 * 1024),
        name="reduce_phase",
    )(*args)
    return result[:6]


def body(tokens, ln_gain, ln_shift, out_bias, w_qkv, b_qkv, w_out, w_fc1, b_fc1, w_fc2, out_grad):
    f, c = lax.axis_index("fsdp"), lax.axis_index("ctx")
    x_hi, core = c // 2, c % 2
    tokens, out_grad = tokens[0], out_grad[0]

    mine = lax.dynamic_slice_in_dim(w_qkv, core * BLK, BLK, axis=2)
    qkv_shard = jnp.concatenate([mine[:, 1], mine[:, 2], mine[:, 0]], axis=1)

    own = (jnp.arange(HD) // 8 == f)[None, None, :]
    spread = lambda v: jnp.where(own, jnp.tile(v, (1, 1, 8)), jnp.zeros((), BF16)).reshape(-1)
    pack = jnp.concatenate(
        [
            ln_gain,
            ln_shift,
            out_bias,
            spread(jnp.roll(lax.dynamic_slice_in_dim(b_qkv, core * 4, 4, axis=1), -1, axis=0)),
            spread(lax.dynamic_slice_in_dim(b_fc1, core * 16, 16, axis=0)[None]),
            jnp.zeros((512,), BF16),
        ]
    )
    pack = pack.astype(F32).reshape(PACK, 128)

    (w_attn, w_up, w_down, normed_t, grad_t, unit, q, kv, kvr, do, active, hidden_grad, small, bias_grad, up_bias_grad,
     a_first, b_first) = (
        gather_call(qkv_shard, w_out, w_fc1, w_fc2, tokens, out_grad, pack, ROPE)
    )
    layer_out, input_grad, attn_all, up_all, down_all, vec = reduce_call(
        w_attn, w_up, w_down, normed_t, grad_t, unit, q, kv, kvr, do, active, hidden_grad, small, bias_grad, up_bias_grad,
        a_first, b_first, tokens, out_grad, ROPE
    )
    qkv_out, proj_out, up_out, down_out = grads_call(attn_all, up_all, down_all)
    gain_grad, shift_grad, out_bias_grad = vec[0, 0], vec[0, 1], vec[0, 2]
    units = jnp.where(core == 0, vec[1:], vec[:0:-1]).reshape(2, 8 * BLK)
    qkv_bias_out = lax.dynamic_slice_in_dim(
        jnp.roll(units[:, : 3 * BLK].reshape(2, 3, 4, HD), 1, axis=1).transpose(1, 0, 2, 3).reshape(3, 8, HD), f * 8, 8, axis=2
    )
    up_bias_out = lax.dynamic_slice_in_dim(units[:, 3 * BLK : 7 * BLK].reshape(32, HD), f * 8, 8, axis=1)
    return (
        layer_out[None],
        input_grad[None],
        gain_grad,
        shift_grad,
        out_bias_grad,
        qkv_out,
        qkv_bias_out,
        proj_out,
        up_out,
        up_bias_out,
        down_out,
    )


def solution(mesh):
    in_specs = (
        P("fsdp", "ctx", None),
        P("fsdp"),
        P("fsdp"),
        P("fsdp"),
        P("fsdp", None, "tp"),
        P(None, "tp", "fsdp"),
        P("tp", "fsdp"),
        P("fsdp", "tp"),
        P("tp", "fsdp"),
        P("tp", "fsdp"),
        P("fsdp", "ctx", None),
    )
    out_specs = (
        P("fsdp", "ctx", None),
        P("fsdp", "ctx", None),
        P("fsdp"),
        P("fsdp"),
        P("fsdp"),
        P("fsdp", None, "tp"),
        P(None, "tp", "fsdp"),
        P("tp", "fsdp"),
        P("fsdp", "tp"),
        P("tp", "fsdp"),
        P("tp", "fsdp"),
    )
    return jax.shard_map(body, mesh=mesh, in_specs=in_specs, out_specs=out_specs, check_vma=False)
```

```python
import math

import jax
import jax.numpy as jnp
import numpy as np
from jax import lax
from jax.experimental import pallas as pl
from jax.experimental.pallas import tpu as pltpu
from jax.sharding import PartitionSpec as P

D = 2048
HD = 64
ROT = 32
BLK = 256
ROWS = 1024
HALF = 512
EPSILON = 1e-05
MASKED = -1e30
F32 = jnp.float32
BF16 = jnp.bfloat16
VMEM_LIMIT = 62 * 1024 * 1024


def params(**kw):
    return pltpu.CompilerParams(vmem_limit_bytes=VMEM_LIMIT, **kw)


def whole():
    return pl.BlockSpec(memory_space=pltpu.VMEM)


def cost(flops, nbytes, trans=0):
    return pl.CostEstimate(flops=int(flops), bytes_accessed=int(nbytes), transcendentals=int(trans))


def block_order(y, x_lo, j):
    dx, dy = j // 4, j % 4
    return lax.rem(y + dy, 4) * 2 + lax.rem(x_lo + dx, 2)


def partner(v):
    lane = lax.broadcasted_iota(jnp.int32, v.shape, 1)
    up = pltpu.roll(v, v.shape[1] - ROT // 2, 1)
    down = pltpu.roll(v, ROT // 2, 1)
    return jnp.where(lane % HD < ROT // 2, up, down)


QT = 256
KC = 512


def rope_table():
    lane = np.arange(128) % HD
    freq = np.where(lane < ROT, 10000.0 ** (-2.0 * (lane % (ROT // 2)) / ROT), 0.0)
    sign = np.where(lane < ROT // 2, -1.0, 1.0)
    coarse, fine = np.arange(64)[:, None] * 32 * freq, np.arange(32)[:, None] * freq
    parts = [np.cos(coarse), np.sin(coarse) * sign, np.cos(fine), np.sin(fine) * sign]
    return np.concatenate(parts).astype(np.float32)


ROPE = rope_table()
GELU_C = math.sqrt(2.0 / math.pi)


MESH = pl.DeviceIdType.MESH
PACK = 24


def coords():
    f, c, z = lax.axis_index("fsdp"), lax.axis_index("ctx"), lax.axis_index("tp")
    return (c // 2) * 2 + f % 2, f // 2, z, c % 2


def device(x, y, z, core):
    return (y * 2 + lax.rem(x, 2), (x // 2) * 2 + core, z)


def beside(dx=0, dy=0, flip=0, dz=0):
    x, y, z, core = coords()
    return device(
        lax.rem(x + dx + 4, 4), lax.rem(y + dy + 4, 4), lax.rem(z + dz + 4, 4), (1 - core) if flip else core
    )


def greet(targets):
    barrier = pltpu.get_barrier_semaphore()
    for target in targets:
        pl.semaphore_signal(barrier, inc=1, device_id=target, device_id_type=MESH)
    pl.semaphore_wait(barrier, len(targets))


class Copies:
    def __init__(self, send, recv, local):
        self.send, self.recv, self.local = send, recv, local
        self.remotes = self.locals = 0
        self.sent = []

    def make(self, src, dst, target):
        i = self.remotes
        self.remotes += 1
        return pltpu.make_async_remote_copy(
            src, dst, self.send.at[i], self.recv.at[i], device_id=target, device_id_type=MESH
        )

    def remote(self, src, dst, target):
        copy = self.make(src, dst, target)
        copy.start()
        self.sent.append(copy)
        return copy

    def here(self, src, dst):
        copy = pltpu.make_async_copy(src, dst, self.local.at[self.locals])
        self.locals += 1
        copy.start()
        return copy


def rope_rows(table, first, cos, sin, count):
    @pl.loop(0, count // 32)
    def _(i):
        at = pl.ds(pl.multiple_of(i * 32, 32), 32)
        ch, sh = table[pl.ds(first // 32 + i, 1), :], table[pl.ds(64 + first // 32 + i, 1), :]
        cl, sl = table[128:160, :], table[160:192, :]
        cos[at, :] = ch * cl - sh * sl
        sin[at, :] = sh * cl + ch * sl


def turn(v, c, s):
    return v * c + partner(v) * s


def gather_kernel(s1_in, proj_in, up_in, down_in, tok_in, grad_in, pack, table_in,
                  w1_out, w2_out, w3_out, normed_t_out, grad_t_out, unit_out, q_out, kv_out, kvr_out, do_out,
                  active_out, hidden_out, small_out, bias_out, up_bias_out, a_s1_out, b_s1_out,
                  w1, w2, w3, tok, grad, normed, grad_rel, normed_t, grad_t, unit, small, q, kv, do, active, slope,
                  hidden, cos, sin, table, bias_sum, up_bias_sum, proj_v, down_v, send, recv, local):
    x, y, z, core = coords()
    x_lo, x_hi = lax.rem(x, 2), x // 2
    up, down, far = beside(dy=1), beside(dy=3), beside(dy=2)
    right, left, over, mate = beside(dx=1), beside(dx=3), beside(dx=2), beside(flip=1)
    copies = Copies(send, recv, local)
    here, remote = copies.here, copies.remote
    hcols = pl.ds(pl.multiple_of(core * 1024, 1024), 1024)
    hrows = pl.ds(pl.multiple_of(core * 1024, 1024), 1024)
    prows = pl.ds(pl.multiple_of(core * BLK, BLK), BLK)
    own_block = pl.ds(0, BLK)
    proj_load = here(proj_in.at[prows], proj_v)
    down_load = here(down_in.at[hrows], down_v)
    s1_loads = [
        here(s1_in.at[c, :, prows], w1.at[own_block, pl.ds(k * BLK, BLK)]) for k, c in enumerate((1, 2, 0))
    ]
    up_load = here(up_in.at[:, hcols], w2.at[own_block])
    greet([up, down, far, right, left, over, mate])

    class Part:
        def __init__(self, w, at, n):
            self.w, self.cols, self.moves = w, pl.ds(at, n), []

        def rows(self, j, first=0, count=BLK):
            return self.w.at[pl.ds(j * BLK + first, count), self.cols]

        def to(self, j, k, target, first=0, count=BLK):
            copy = remote(self.rows(j, first, count), self.rows(k, first, count), target)
            self.moves.append(copy)
            return copy

        def along_y(self, base):
            return [self.to(base, base + 3, up), self.to(base, base + 1, down), self.to(base, base + 2, far)]

        def sideways(self):
            return [self.to(0, 4, right, 0, BLK // 2), self.to(0, 4, left, BLK // 2, BLK // 2)]

        def begin_x(self):
            self.x = self.sideways()

        def begin_y(self):
            self.y = self.along_y(0)

        def forward(self):
            for copy in self.y:
                copy.wait_recv()
            self.x += [
                self.to(1, 5, right), self.to(3, 7, left),
                self.to(2, 6, right, 0, BLK // 2), self.to(2, 6, left, BLK // 2, BLK // 2),
            ]

        def forward_y(self):
            for copy in self.x:
                copy.wait_recv()
            self.x = self.along_y(4)

        def arrived(self):
            for copy in self.x:
                copy.wait_recv()

        def all_arrived(self):
            for copy in self.y + self.x:
                copy.wait_recv()

    keys_part, query_part, proj_part = Part(w1, 0, 512), Part(w1, 512, BLK), Part(w1, 768, BLK)
    up_part = Part(w2, 0, 1024)
    down_a, down_b = Part(w3, 0, 512), Part(w3, 512, 512)

    my_rows = pl.ds(pl.multiple_of(core * HALF, HALF), HALF)
    pack_y = [remote(pack, small.at[3], up), remote(pack, small.at[1], down), remote(pack, small.at[2], far)]
    pack_own = here(pack, small.at[0])
    tok_copy = remote(tok_in, tok.at[my_rows], mate)
    grad_copy = remote(grad_in, grad.at[my_rows], mate)
    for copy in s1_loads:
        copy.wait()
    keys_part.begin_y()
    keys_part.begin_x()
    mine = [here(tok_in, tok.at[my_rows]), here(grad_in, grad.at[my_rows])]
    table_load = here(table_in, table)

    proj_load.wait()
    w1[0:BLK, 3 * BLK :] = proj_v[...].astype(F32).T.astype(BF16)
    down_load.wait()
    for k in range(4):
        w3[0:BLK, k * BLK : (k + 1) * BLK] = down_v[k * BLK : (k + 1) * BLK, :].astype(F32).T.astype(BF16)
    for copy in pack_y:
        copy.wait_recv()
    pack_own.wait()
    pack_x = remote(small.at[pl.ds(0, 4)], small.at[pl.ds(4, 4)], right)
    up_load.wait()
    up_part.begin_x()
    down_b.begin_x()
    proj_part.begin_x()
    table_load.wait()
    rope_rows(table, x_hi * ROWS, cos, sin, ROWS)
    up_part.begin_y()
    down_b.begin_y()
    keys_part.forward()
    down_b.forward_y()
    down_a.begin_y()
    proj_part.begin_y()
    query_part.begin_y()
    for copy in mine:
        copy.wait()
    tok_copy.wait_recv()
    grad_copy.wait_recv()
    pack_x.wait_recv()

    bias_sum[...] = jnp.zeros_like(bias_sum)
    up_bias_sum[...] = jnp.zeros_like(up_bias_sum)
    tile = 128

    def prepare(first, last):
        @pl.loop(first, last)
        def _(i):
            at = pl.ds(pl.multiple_of(i * tile, tile), tile)
            rows = tok[at, :].astype(F32)
            mean = jnp.mean(rows, axis=-1, keepdims=True)
            centered = rows - mean
            inv = lax.rsqrt(jnp.mean(centered * centered, axis=-1, keepdims=True) + EPSILON)
            for j in range(8):
                src = pl.ds(pl.multiple_of(block_order(y, x_lo, j) * BLK, BLK), BLK)
                dst = pl.ds(j * BLK, BLK)
                gain = jnp.concatenate([small[j, 0:1, :], small[j, 1:2, :]], axis=1)
                shift = jnp.concatenate([small[j, 2:3, :], small[j, 3:4, :]], axis=1)
                u = (tok[at, src].astype(F32) - mean) * inv
                n = u * gain + shift
                normed[at, dst] = n.astype(BF16)
                normed_t[dst, at] = n.T.astype(BF16)
                unit[at, dst] = u.astype(BF16)
                g = grad[at, src]
                g32 = g.astype(F32)
                grad_rel[at, dst] = g
                grad_t[dst, at] = g32.T.astype(BF16)
                bias_sum[:, dst] += jnp.sum(g32, axis=0, keepdims=True)

    prepare(0, 8)
    saved = [here(normed_t, normed_t_out), here(grad_t, grad_t_out), here(unit, unit_out), here(small, small_out),
             here(bias_sum, bias_out)]

    biases = small[0, 6:20, :]
    for j in range(1, 8):
        biases = biases + small[j, 6:20, :]
    qkv_bias = jnp.concatenate([biases[j : j + 1] for j in range(6)], axis=1)
    up_bias = jnp.concatenate([biases[j : j + 1] for j in range(6, 14)], axis=1)
    big = 256
    keys_part.arrived()

    @pl.loop(0, ROWS // big)
    def _(i):
        at = pl.ds(pl.multiple_of(i * big, big), big)
        raw = jnp.dot(normed[at, :], w1[:, : 2 * BLK], preferred_element_type=F32) + qkv_bias[:, : 2 * BLK]
        c, s = cos[at, :], sin[at, :]
        for k in range(2):
            lanes = slice(k * 128, (k + 1) * 128)
            kv[at, lanes] = turn(raw[:, lanes], c, s).astype(BF16)
        kv[at, BLK:] = raw[:, BLK:].astype(BF16)

    kv_copy = copies.make(kv, kvr_out, over)

    @pl.when(x_hi == 0)
    def _():
        kv_copy.start()

    saved.append(here(kv, kv_out))
    up_part.forward()
    proj_part.forward_y()
    query_part.begin_x()
    down_a.begin_x()
    up_part.arrived()
    saved.append(here(w2, w2_out))

    @pl.loop(0, ROWS // big)
    def _(i):
        at = pl.ds(pl.multiple_of(i * big, big), big)
        v = jnp.dot(normed[at, :], w2[...], preferred_element_type=F32) + up_bias
        sq = v * v
        t = jnp.tanh(GELU_C * v * (1.0 + 0.044715 * sq))
        half = 0.5 * (1.0 + t)
        active[at, :] = (v * half).astype(BF16)
        slope[at, :] = (half + 0.5 * v * (1.0 - t * t) * (GELU_C * (1.0 + 3 * 0.044715 * sq))).astype(BF16)

    saved.append(here(active, active_out))
    down_a.forward()

    place = [buf.at[:, pl.ds(k * 1024, 1024)] for buf in (tok, grad) for k in range(2)]

    def partials(left, right, blocks, dst, out):
        for k, j in enumerate(blocks):
            at = pl.ds((k % 4) * BLK, BLK)
            dst[k // 4][at, :] = jnp.dot(left[j * BLK : (j + 1) * BLK, :], right[...], preferred_element_type=F32).astype(BF16)
            saved.append(here(dst[k // 4].at[at], out.at[k]))

    partials(grad_t, active, (4, 5, 6, 7), place[:1], a_s1_out)
    query_part.forward()
    down_a.arrived()
    down_b.all_arrived()
    saved.append(here(w3, w3_out))

    @pl.loop(0, ROWS // big)
    def _(i):
        at = pl.ds(pl.multiple_of(i * big, big), big)
        v = jnp.dot(grad_rel[at, :], w3[...], preferred_element_type=F32) * slope[at, :].astype(F32)
        low = v.astype(BF16)
        hidden[at, :] = low
        up_bias_sum[...] += jnp.sum(low.astype(F32), axis=0, keepdims=True)

    saved += [here(hidden, hidden_out), here(up_bias_sum, up_bias_out)]
    partials(normed_t, hidden, (2, 6, 1, 5, 3, 7), place[1:3], b_s1_out)
    query_part.arrived()
    proj_part.all_arrived()
    saved.append(here(w1, w1_out))

    @pl.loop(0, ROWS // big)
    def _(i):
        at = pl.ds(pl.multiple_of(i * big, big), big)
        raw = jnp.dot(normed[at, :], w1[:, 2 * BLK : 3 * BLK], preferred_element_type=F32) + qkv_bias[:, 2 * BLK :]
        c, s = cos[at, :], sin[at, :]
        for k in range(2):
            lanes = slice(k * 128, (k + 1) * 128)
            q[at, lanes] = (turn(raw[:, lanes], c, s).astype(BF16).astype(F32) * (HD**-0.5)).astype(BF16)
        do[at, :] = jnp.dot(grad_rel[at, :], w1[:, 3 * BLK :], preferred_element_type=F32).astype(BF16)

    saved += [here(q, q_out), here(do, do_out)]
    for copy in copies.sent:
        copy.wait_send()

    @pl.when(x_hi == 0)
    def _():
        kv_copy.wait_send()

    @pl.when(x_hi == 1)
    def _():
        kv_copy.wait_recv()

    for copy in saved:
        copy.wait()


def gather_call(*args):
    n = 1024
    low = lambda *shape: jax.ShapeDtypeStruct(shape, BF16)
    wide = lambda *shape: jax.ShapeDtypeStruct(shape, F32)
    vlow = lambda *shape: pltpu.VMEM(shape, BF16)
    vwide = lambda *shape: pltpu.VMEM(shape, F32)
    anywhere = pl.BlockSpec(memory_space=pl.ANY)
    return pl.pallas_call(
        gather_kernel,
        in_specs=[anywhere] * 8,
        out_specs=[anywhere] * 17,
        out_shape=[
            low(D, n), low(D, n), low(D, n), low(D, ROWS), low(D, ROWS), low(ROWS, D), low(ROWS, BLK), low(ROWS, 2 * BLK),
            low(ROWS, 2 * BLK), low(ROWS, BLK), low(ROWS, n), low(ROWS, n), wide(8, PACK, 128), wide(1, D), wide(1, n),
            low(4, BLK, n), low(6, BLK, n),
        ],
        scratch_shapes=[
            vlow(D, n), vlow(D, n), vlow(D, n), vlow(ROWS, D), vlow(ROWS, D), vlow(ROWS, D), vlow(ROWS, D), vlow(D, ROWS),
            vlow(D, ROWS), vlow(ROWS, D), vwide(8, PACK, 128), vlow(ROWS, BLK), vlow(ROWS, 2 * BLK), vlow(ROWS, BLK),
            vlow(ROWS, n), vlow(ROWS, n), vlow(ROWS, n), vwide(ROWS, 128), vwide(ROWS, 128), vwide(192, 128), vwide(1, D),
            vwide(1, n), vlow(BLK, BLK), vlow(n, BLK),
            pltpu.SemaphoreType.DMA((64,)),
            pltpu.SemaphoreType.DMA((64,)),
            pltpu.SemaphoreType.DMA((40,)),
        ],
        compiler_params=params(collective_id=0, has_side_effects=True),
        cost_estimate=cost(2 * ROWS * D * 3 * n, 64 * 1024 * 1024),
        name="gather_phase",
    )(*args)


def grads_kernel(attn, up, down, qkv_out, proj_out, up_out, down_out):
    for core in range(2):
        for k, c in enumerate((1, 2, 0)):
            qkv_out[c, :, core * BLK : (core + 1) * BLK] = attn[core, :, k * BLK : (k + 1) * BLK].astype(F32)
        proj_out[core * BLK : (core + 1) * BLK, :] = attn[core, :, 3 * BLK :].astype(F32).T
        up_out[:, core * 1024 : (core + 1) * 1024] = up[core].astype(F32)
        down_out[core * 1024 : (core + 1) * 1024, :] = down[core].astype(F32).T


def grads_call(attn, up, down):
    tile = 128
    piece = pl.BlockSpec((2, tile, 1024), lambda i: (0, i, 0))
    wide = lambda *shape: jax.ShapeDtypeStruct(shape, F32)
    return pl.pallas_call(
        grads_kernel,
        grid=(BLK // tile,),
        in_specs=[piece] * 3,
        out_specs=[
            pl.BlockSpec((3, tile, HALF), lambda i: (0, i, 0)),
            pl.BlockSpec((HALF, tile), lambda i: (0, i)),
            pl.BlockSpec((tile, 2048), lambda i: (i, 0)),
            pl.BlockSpec((2048, tile), lambda i: (0, i)),
        ],
        out_shape=[wide(3, BLK, HALF), wide(HALF, BLK), wide(BLK, 2048), wide(2048, BLK)],
        compiler_params=params(),
        cost_estimate=cost(0, 10 * 1024 * 1024),
        name="gradients",
    )(attn, up, down)


class Lefts:
    def __init__(self, sources, buf, sems):
        self.sources, self.buf, self.sems = sources, buf, sems
        self.queue, self.count = ([], []), [0, 0]

    def want(self, kind, j):
        if any(held == j for held, _ in self.queue[kind]):
            return
        slot = self.count[kind] % 2
        self.count[kind] += 1
        self.move(kind, j, slot).start()
        self.queue[kind].append((j, slot))

    def take(self, kind, j):
        held, slot = self.queue[kind].pop(0)
        assert held == j
        self.move(kind, j, slot).wait()
        return self.buf.at[kind, slot]

    def move(self, kind, j, slot):
        return pltpu.make_async_copy(
            self.sources[kind].at[pl.ds(j * BLK, BLK)], self.buf.at[kind, slot], self.sems.at[kind, slot]
        )

    def run(self, jobs, after=()):
        for i, (kinds, j, act) in enumerate(jobs):
            for kind in kinds:
                self.want(kind, j)
            ahead = jobs[i + 1][:2] if i + 1 < len(jobs) else after
            if ahead:
                for kind in ahead[0]:
                    self.want(kind, ahead[1])
            act(*[self.take(kind, j) for kind in kinds])


def product(dst, lefts, rights, adds=()):
    at = 0
    for left, right in zip(lefts, rights):
        cols = slice(at, at + right.shape[1])
        total = jnp.dot(left[...], right[...], preferred_element_type=F32)
        for add in adds:
            total += add[:, cols].astype(F32)
        dst[:, cols] = total.astype(BF16)
        at += right.shape[1]


def row_products(half, a, b, w1, col1, w2, out, unit=None, ub=None, sems=None, vec=None):
    nt = (((1,), (1,)), ((), ()))
    ka = a.shape[1]
    rows = pl.ds(pl.multiple_of(half * HALF, HALF), HALF)

    def fetch(j, slot):
        at = pl.ds(pl.multiple_of(j * HALF, HALF), HALF)
        return pltpu.make_async_copy(unit.at[rows, at], ub.at[slot], sems.at[slot])

    if unit is not None:
        fetch(0, 0).start()

    @pl.loop(0, D // HALF)
    def _(j):
        at = pl.ds(pl.multiple_of(j * HALF, HALF), HALF)
        slot = lax.rem(j, 2)
        if unit is not None:
            fetch(j, slot).wait()

            @pl.when(j < D // HALF - 1)
            def _():
                fetch(j + 1, 1 - slot).start()

        total = lax.dot_general(a[rows, :], w1[at, col1 : col1 + ka], nt, preferred_element_type=F32)
        total += lax.dot_general(b[rows, :], w2[at, :], nt, preferred_element_type=F32)
        out[:, at] = total.astype(BF16)
        if unit is not None:
            weighted = jnp.sum(total * ub[slot].astype(F32), axis=0, keepdims=True)
            plain = jnp.sum(total, axis=0, keepdims=True)
            for k in range(2):
                vec[2 * j + k, 0:1, :] = weighted[:, k * BLK : (k + 1) * BLK]
                vec[2 * j + k, 1:2, :] = plain[:, k * BLK : (k + 1) * BLK]


def add_rows(mine, got):
    @pl.loop(0, 4)
    def _(i):
        at = pl.ds(pl.multiple_of(i * 128, 128), 128)
        mine[at, :] = (mine[at, :].astype(F32) + got[at, :].astype(F32)).astype(BF16)


def reduce_kernel(w1, w2, w3, normed_t, grad_t, unit, q_in, kv_in, kvr_in, do_in, active_in, hidden_in, small_in, bias_in,
                  up_bias_in, a_s1, b_s1, tok_in, grad_in, table_in,
                  layer_out, input_grad, piece1, piece2, piece3, vec_out,
                  a_r1, a_r2, a_x, b_p, b_r1, b_r2, b_x, c_r1, d_r1,
                  q, do, active, hidden, att, raw, small, cos, sin, cos_r, sin_r, table,
                  dk, dv, out_t, dq_t, dkv, ub, theirs, br_m, br_c, br_z, br_o, ng_m, ng_c, ng_z, ng_o,
                  turned, tok, grad, left_buf, stage, a_s2, a_m, b_s2, b_m, c_s1, c_s2, c_m, d_s1, d_s2, d_m, c_r2, c_x, d_r2, d_x,
                  vec_t, vec_m, va, va_r, vb_r, units, my, my_r, mx, mx_r, last, last_r, bias_v, up_bias_v, vec_v,
                  send, recv, local, sems, left_sems, stage_sems):
    x, y, z, core = coords()
    x_lo, x_hi = lax.rem(x, 2), x // 2
    other = 1 - core
    up, down, far = beside(dy=1), beside(dy=3), beside(dy=2)
    right, left, over = beside(dx=1), beside(dx=3), beside(dx=2)
    mate = beside(flip=1)
    above, below = beside(dz=1), beside(dz=3)
    along = [above, beside(dz=2), below]
    copies = Copies(send, recv, local)
    here, remote = copies.here, copies.remote
    nt = (((1,), (1,)), ((), ()))

    load_active, load_hidden = here(active_in, active), here(hidden_in, hidden)
    own_keys = pl.ds(pl.multiple_of(x_hi * ROWS, ROWS), ROWS)
    loads = [here(table_in, table), here(q_in, q), here(do_in, do), here(small_in, small), here(bias_in, bias_v),
              here(up_bias_in, up_bias_v)]
    z_rows = pl.ds(pl.multiple_of(z * 128, 128), 128)
    loads += [here(tok_in.at[z_rows], tok), here(grad_in.at[z_rows], grad)]
    greet([up, down, far, right, left, over, mate] + along)
    lo, hi, first, second = pl.ds(0, 512), pl.ds(512, 512), pl.ds(0, 2), pl.ds(2, 2)
    bp = [remote(b_s1.at[first, :, lo], b_p.at[first], up), remote(b_s1.at[first, :, hi], b_p.at[second], down)]
    b1 = [
        remote(b_s1.at[second, :, hi], b_r1.at[first, :, hi], up),
        remote(b_s1.at[pl.ds(4, 2), :, lo], b_r1.at[second, :, lo], down),
    ]
    a1 = [remote(a_s1.at[pl.ds(2 * k, 2)], a_r1.at[pl.ds(2 * k, 2)], target) for k, target in enumerate((right, left))]

    lefts = Lefts((normed_t, grad_t), left_buf, left_sems)

    def staged(parts):
        views, found = [], []
        for k, part in enumerate(parts):
            view = stage.at[k, :, pl.ds(0, part.shape[-1])]
            copy = pltpu.make_async_copy(part, view, stage_sems.at[k])
            copy.start()
            found.append(copy)
            views.append(view)
        for copy in found:
            copy.wait()
        return views

    def arrived(moves):
        for copy in moves:
            copy.wait_recv()

    def settle(mine, got, move, piece, cols, on_hbm):
        move.wait_send()
        copies.sent = [copy for copy in copies.sent if copy is not move]
        move.wait_recv()
        more = staged([got])[0] if on_hbm else got
        mine[...] = (mine[...].astype(F32) + more[...].astype(F32)).astype(BF16)
        spot = piece.at[core, :, cols]
        return here(mine, spot), remote(mine, spot, mate)

    def turn_back(v, c, s):
        return v * c - partner(v) * s

    upper, lower = pl.ds(0, BLK // 2), pl.ds(BLK // 2, BLK // 2)
    pairs_back = [copies.make(dkv.at[k], dkv.at[k], over) for k in range(2)]
    passed = [
        copies.make(c_s1.at[first], b_r1.at[first, :, lo], up),
        copies.make(c_s1.at[second], b_r1.at[second, :, hi], down),
    ]
    a_y = [copies.make(a_s2.at[k], a_r2.at[k], target) for k, target in enumerate((far, down, up))]
    b2 = [copies.make(b_s2.at[upper], b_r2.at[upper], right), copies.make(b_s2.at[lower], b_r2.at[lower], left)]
    copies.sent += passed + a_y + b2

    def attend(keys, vals, keys_t, vals_t, st, dp, qm, dom):
        own = here(kv_in.at[:, pl.ds(0, BLK)], keys.at[own_keys]), here(kv_in.at[:, pl.ds(BLK, BLK)], vals.at[own_keys])
        far_keys = pltpu.make_async_copy(kvr_in.at[:, pl.ds(0, BLK)], keys.at[pl.ds(0, ROWS)], local.at[copies.locals])
        far_vals = pltpu.make_async_copy(kvr_in.at[:, pl.ds(BLK, BLK)], vals.at[pl.ds(0, ROWS)], local.at[copies.locals + 1])
        copies.locals += 2

        @pl.when(x_hi == 1)
        def _():
            far_keys.start()
            far_vals.start()
        for copy in loads + list(own):
            copy.wait()

        @pl.when(x_hi == 1)
        def _():
            far_keys.wait()
            far_vals.wait()

        @pl.loop(0, (x_hi + 1) * (ROWS // KC))
        def _(j):
            at = pl.ds(pl.multiple_of(j * KC, KC), KC)
            keys_t[:, at] = keys[at, :].astype(F32).T.astype(BF16)
            vals_t[:, at] = vals[at, :].astype(F32).T.astype(BF16)
            dk[at, :] = jnp.zeros((KC, BLK), F32)
            dv[at, :] = jnp.zeros((KC, BLK), F32)

        rope_rows(table, x_hi * ROWS, cos, sin, ROWS)
        rope_rows(table, 0, cos_r, sin_r, ROWS)
        lane = lax.broadcasted_iota(jnp.int32, (QT, 128), 1) // HD

        def heads(pair, tiles):
            lanes = slice(pair * 128, pair * 128 + 128)
            for t in tiles:
                rows = slice(t * QT, (t + 1) * QT)
                chunks = x_hi * (ROWS // KC) + t * QT // KC + 1
                for side in range(2):
                    qm[side] = jnp.where(lane == side, q[rows, lanes], jnp.zeros((), BF16))
                    dom[side] = jnp.where(lane == side, do[rows, lanes], jnp.zeros((), BF16))

                def score(j, tops, masked):
                    at = pl.ds(pl.multiple_of(j * KC, KC), KC)
                    new = []
                    for side in range(2):
                        s = lax.dot_general(keys[at, lanes], qm[side], nt, preferred_element_type=F32)
                        if masked:
                            ki = lax.broadcasted_iota(jnp.int32, (KC, QT), 0)
                            qi = lax.broadcasted_iota(jnp.int32, (KC, QT), 1) + t * QT % KC
                            s = jnp.where(ki <= qi, s, MASKED)
                        st[side, at, :] = s
                        new.append(jnp.maximum(tops[side], jnp.max(s, axis=0, keepdims=True)))
                    return tuple(new)

                low = jnp.full((1, QT), MASKED, F32)
                tops = lax.fori_loop(0, chunks - 1, lambda j, m: score(j, m, False), (low, low))
                tops = score(chunks - 1, tops, True)

                def weigh(j, carry):
                    at = pl.ds(pl.multiple_of(j * KC, KC), KC)
                    new = []
                    for side in range(2):
                        total, dot = carry[2 * side : 2 * side + 2]
                        p = jnp.exp(st[side, at, :] - tops[side])
                        st[side, at, :] = p
                        d = lax.dot_general(vals[at, lanes], dom[side], nt, preferred_element_type=F32)
                        dp[side, at, :] = d
                        new.append(total + jnp.sum(p, axis=0, keepdims=True))
                        new.append(dot + jnp.sum(p * d, axis=0, keepdims=True))
                    return tuple(new)

                zero = jnp.zeros((1, QT), F32)
                sums = lax.fori_loop(0, chunks, weigh, (zero,) * 4)
                inv = [1.0 / sums[0], 1.0 / sums[2]]
                delta = [sums[1] * inv[0], sums[3] * inv[1]]
                out_t[:, rows] = jnp.zeros((128, QT), F32)
                dq_t[:, rows] = jnp.zeros((128, QT), F32)

                def spread(j, _):
                    at = pl.ds(pl.multiple_of(j * KC, KC), KC)
                    new_v, new_k = dv[at, lanes], dk[at, lanes]
                    for side in range(2):
                        hrows = slice((2 * pair + side) * HD, (2 * pair + side + 1) * HD)
                        trows = slice(side * HD, (side + 1) * HD)
                        p = st[side, at, :] * inv[side]
                        p_low = p.astype(BF16)
                        ds = (p * (dp[side, at, :] - delta[side])).astype(BF16)
                        out_t[trows, rows] += jnp.dot(vals_t[hrows, at], p_low, preferred_element_type=F32)
                        dq_t[trows, rows] += jnp.dot(keys_t[hrows, at], ds, preferred_element_type=F32)
                        new_v += jnp.dot(p_low, dom[side], preferred_element_type=F32)
                        new_k += jnp.dot(ds, qm[side], preferred_element_type=F32)
                    dv[at, lanes] = new_v
                    dk[at, lanes] = new_k
                    return 0

                lax.fori_loop(0, chunks, spread, 0)

        def end_pair(pair):
            lanes = slice(pair * 128, pair * 128 + 128)
            copy = pairs_back[pair]

            @pl.when(x_hi == 1)
            def _():
                dkv[pair, :, :128] = turn_back(dk[:ROWS, lanes], cos_r[...], sin_r[...]).astype(BF16)
                dkv[pair, :, 128:] = dv[:ROWS, lanes].astype(BF16)
                copy.start()

            for t in range(ROWS // 512):
                rows = slice(t * 512, (t + 1) * 512)
                att[rows, lanes] = out_t[:, rows].T.astype(BF16)
                raw[rows, 2 * BLK + pair * 128 : 2 * BLK + pair * 128 + 128] = turn_back(
                    dq_t[:, rows].T * (HD**-0.5), cos[rows, :], sin[rows, :]
                ).astype(BF16)

        heads(0, (0, 1, 2))

        def pass_blocks(move, own, got, cols, buf):
            move.wait_recv()
            views = staged([b_s1.at[own, :, cols], b_p.at[got], b_s1.at[own + 1, :, cols], b_p.at[got + 1]])
            for k in range(2):
                c_s1[buf + k] = (views[2 * k][...].astype(F32) + views[2 * k + 1][...].astype(F32)).astype(BF16)
            passed[buf // 2].start()

        pass_blocks(bp[0], 2, 0, lo, 0)
        pass_blocks(bp[1], 4, 2, hi, 2)
        heads(0, (3,))
        end_pair(0)

        heads(1, (0, 1, 2))

        heads(1, (3,))
        end_pair(1)

    pl.run_scoped(
        attend,
        pltpu.VMEM((2 * ROWS, BLK), BF16),
        pltpu.VMEM((2 * ROWS, BLK), BF16),
        pltpu.VMEM((BLK, 2 * ROWS), BF16),
        pltpu.VMEM((BLK, 2 * ROWS), BF16),
        pltpu.VMEM((2, 2 * ROWS, QT), F32),
        pltpu.VMEM((2, 2 * ROWS, QT), F32),
        pltpu.VMEM((2, QT, 128), BF16),
        pltpu.VMEM((2, QT, 128), BF16),
    )
    def finish(w1v, w2v, w3v):
        w_loads = [here(w1, w1v), here(w3, w3v), here(w2, w2v)]

        def z_at(dz, first=0, count=128):
            return pl.ds(pl.multiple_of(lax.rem(z + dz, 4) * 128 + first, 64), count)

        def to_z(total, got):
            return [
                remote(total.at[z_at(2, 0, 64)], got.at[0, pl.ds(0, 64)], above),
                remote(total.at[z_at(2, 64, 64)], got.at[0, pl.ds(64, 64)], below),
                remote(total.at[z_at(1, 64, 64)], got.at[1, pl.ds(64, 64)], above),
                remote(total.at[z_at(3, 0, 64)], got.at[2, pl.ds(0, 64)], below),
            ]

        def pass_on(total, got, first, buf):
            first[0].wait_recv()
            buf[0] = (total[z_at(1, 0, 64), :].astype(F32) + got[0, :64, :].astype(F32)).astype(BF16)
            one = remote(buf.at[0], got.at[1, pl.ds(0, 64)], above)
            first[1].wait_recv()
            buf[1] = (total[z_at(3, 64, 64), :].astype(F32) + got[0, 64:, :].astype(F32)).astype(BF16)
            two = remote(buf.at[1], got.at[2, pl.ds(64, 64)], below)
            return [first[2], first[3], one, two]

        def from_z(chunk, rows):
            at = z_at(0)
            return [here(chunk, rows.at[at]), remote(chunk, rows.at[at], above), remote(chunk, rows.at[at], below)]

        def pass_rows(moves, rows):
            moves[1].wait_recv()
            one = remote(rows.at[z_at(3, 0, 64)], rows.at[z_at(3, 0, 64)], above)
            moves[2].wait_recv()
            two = remote(rows.at[z_at(1, 64, 64)], rows.at[z_at(1, 64, 64)], below)
            return moves[0], [one, two]

        load_active.wait()
        load_hidden.wait()
        lefts.want(1, 2)
        arrived(a1)
        s = staged([a_r1.at[2], a_r1.at[3], a_r1.at[1]])
        lefts.run(
            [((1,), j, lambda l, k=k: product(a_s2.at[k], [l], [active], [s[k]])) for k, j in enumerate((2, 3, 1))],
            after=((0, 1), 2),
        )
        for copy in a_y:
            copy.start()
        tail = [raw.at[:, pl.ds(2 * BLK, BLK)], att]
        d1 = []
        for k, (j, target) in enumerate(((2, far), (1, up), (3, down))):
            jobs = [((0, 1), j + 4 * i, lambda a, b, i=i: product(d_s1.at[2 * k + i], [a, b], tail)) for i in range(2)]
            lefts.run(jobs, after=((0, 1), (1, 3)[k]) if k < 2 else ((0,), 2))
            d1.append(remote(d_s1.at[pl.ds(2 * k, 2)], d_r1.at[pl.ds(2 * k, 2)], target))

        for copy in w_loads[:2]:
            copy.wait()
        row_products(other, att, active, w1v, 3 * BLK, w3v, theirs)
        br_core = remote(theirs, br_c, mate)
        row_products(core, att, active, w1v, 3 * BLK, w3v, br_m)

        br_core.wait_recv()
        add_rows(br_m, br_c)
        br1 = to_z(br_m, br_z)


        def local_grads(pair, more):
            lanes = slice(pair * 128, pair * 128 + 128)
            k = turn_back(dk[own_keys, lanes], cos[...], sin[...])
            v = dv[own_keys, lanes]
            if more:
                k = k + dkv[pair, :, :128].astype(F32)
                v = v + dkv[pair, :, 128:].astype(F32)
            raw[:, lanes] = k.astype(BF16)
            raw[:, BLK + pair * 128 : BLK + pair * 128 + 128] = v.astype(BF16)

        for pair, copy in enumerate(pairs_back):

            @pl.when(x_hi == 1)
            def _():
                local_grads(pair, False)
                copy.wait_send()

            @pl.when(x_hi == 0)
            def _():
                copy.wait_recv()
                local_grads(pair, True)

        br_core.wait_send()
        copies.sent = [copy for copy in copies.sent if copy is not br_core]
        w_loads[2].wait()
        row_products(other, raw, hidden, w1v, 0, w2v, theirs, unit, ub, sems, vec_t)
        ng_core = remote(theirs, ng_c, mate)

        row_products(core, raw, hidden, w1v, 0, w2v, ng_m, unit, ub, sems, vec_m)
        br2 = pass_on(br_m, br_z, br1, turned.at[0])
        ng_core.wait_recv()
        add_rows(ng_m, ng_c)
        ng1 = to_z(ng_m, ng_z)

        va[...] = jnp.zeros_like(va)
        for j in range(8):
            va[j, 0:2, :] = vec_t[j, 0:2, :] + vec_m[j, 0:2, :]
        va_sent = [remote(va, va_r.at[k], along[k]) for k in range(3)]

        for copy in passed:
            copy.wait_send()
        copies.sent = [copy for copy in copies.sent if all(copy is not old for old in passed)]
        pairs = raw.at[:, pl.ds(0, 512)]
        c1 = []
        for k, (j, target) in enumerate(((2, far), (1, up), (3, down))):
            jobs = [((0,), j + 4 * i, lambda l, i=i: product(c_s1.at[2 * k + i], [l], [pairs])) for i in range(2)]
            lefts.run(jobs, after=((0,), (1, 3)[k]) if k < 2 else ((0,), 4))
            c1.append(remote(c_s1.at[pl.ds(2 * k, 2)], c_r1.at[pl.ds(2 * k, 2)], target))

        arrived(b1 + passed)
        s = staged([b_r1.at[1], b_r1.at[3]])
        lefts.run([((0,), 4, lambda l: product(b_s2, [l], [hidden], s))], after=((1,), 0))
        for copy in b2:
            copy.start()
        arrived(a_y)
        s = staged([a_r1.at[0], a_r2.at[0], a_r2.at[1], a_r2.at[2]])
        lefts.run([((1,), 0, lambda l: product(a_m, [l], [active], s))], after=((0, 1), 4))
        a3 = remote(a_m, a_x, over)

        arrived(br2)
        tile = 32

        def share(total, got, i, j):
            at = pl.ds(pl.multiple_of(i * tile, tile), tile)
            from_all = pl.ds(pl.multiple_of(z * 128 + i * tile, tile), tile)
            cols = slice(j * BLK, (j + 1) * BLK)
            return total[from_all, cols].astype(F32) + (got[1, at, cols].astype(F32) + got[2, at, cols].astype(F32))

        def line(row, j):
            return jnp.concatenate([small[j, row : row + 1, :], small[j, row + 1 : row + 2, :]], axis=1)

        def spot(j):
            return pl.ds(pl.multiple_of(block_order(y, x_lo, j) * BLK, BLK), BLK)

        @pl.loop(0, 128 // tile)
        def _(i):
            at = pl.ds(pl.multiple_of(i * tile, tile), tile)
            for j in range(8):
                value = tok[at, spot(j)].astype(F32) + share(br_m, br_z, i, j) + line(4, j)
                br_o[at, spot(j)] = value.astype(BF16)

        ng2 = pass_on(ng_m, ng_z, ng1, turned.at[1])

        br3 = from_z(br_o, layer_out)
        for copy in va_sent:
            copy.wait_recv()
        vec_v[0] = (va[...] + va_r[1]) + (va_r[0] + va_r[2])
        vb = remote(vec_v.at[0], vb_r, mate)

        arrived(d1)
        s = staged([d_r1.at[1], d_r1.at[3], d_r1.at[5]])
        lefts.run([((0, 1), 4, lambda a, b: product(d_s2, [a, b], tail, s))], after=((0,), 0))
        d2 = [remote(d_s2.at[upper], d_r2.at[upper], right), remote(d_s2.at[lower], d_r2.at[lower], left)]

        arrived(b2)
        s = staged([b_r1.at[0], b_r1.at[2], b_r2])
        lefts.run([((0,), 0, lambda l: product(b_m, [l], [hidden], s))], after=((0, 1), 0))
        b3 = remote(b_m, b_x, over)

        vb.wait_recv()
        units[...] = jnp.zeros_like(units)
        units[0:3, :] = jnp.sum(raw[...].astype(F32), axis=0, keepdims=True).reshape(3, BLK)
        for j in range(4):
            units[3 + j : 4 + j, :] = up_bias_v[:, j * BLK : (j + 1) * BLK]
        for j in range(8):
            dy, dx = j % 4, j // 4
            my[dy, dx] = vec_v[0, j] + vb_r[j]
            my[dy, dx, 2:3, :] = bias_v[:, j * BLK : (j + 1) * BLK]
        for dy in range(4):
            my[dy, 2] = units[...]
        my_sent = [remote(my.at[1], my_r.at[0], up), remote(my.at[2], my_r.at[1], far), remote(my.at[3], my_r.at[2], down)]

        arrived(ng2)

        @pl.loop(0, 128 // tile)
        def _(i):
            at = pl.ds(pl.multiple_of(i * tile, tile), tile)
            rows = tok[at, :].astype(F32)
            mean = jnp.mean(rows, axis=-1, keepdims=True)
            centered = rows - mean
            inv = lax.rsqrt(jnp.mean(centered * centered, axis=-1, keepdims=True) + EPSILON)

            def terms(j):
                u = (tok[at, spot(j)].astype(F32) - mean) * inv
                return u, share(ng_m, ng_z, i, j) * line(0, j)

            first = second = jnp.zeros((tile, 1), F32)
            for j in range(8):
                u, g = terms(j)
                first += jnp.sum(g, axis=-1, keepdims=True)
                second += jnp.sum(g * u, axis=-1, keepdims=True)
            first, second = first / D, second / D
            for j in range(8):
                u, g = terms(j)
                ng_o[at, spot(j)] = (grad[at, spot(j)].astype(F32) + inv * (g - first - u * second)).astype(BF16)

        ng3 = from_z(ng_o, input_grad)
        arrived(d2)
        s = staged([d_r1.at[0], d_r1.at[2], d_r1.at[4]]) + [d_r2]
        lefts.run([((0, 1), 0, lambda a, b: product(d_m, [a, b], tail, s))], after=((0,), 4))
        d3 = remote(d_m, d_x, over)

        arrived(c1)
        s = staged([c_r1.at[1], c_r1.at[3], c_r1.at[5]])
        lefts.run([((0,), 4, lambda l: product(c_s2, [l], [pairs], s))], after=((0,), 0))
        c2 = [remote(c_s2.at[upper], c_r2.at[upper], right), remote(c_s2.at[lower], c_r2.at[lower], left)]

        br_own, br4 = pass_rows(br3, layer_out)

        arrived(my_sent)
        here_sum = (my[0] + my_r[1]) + (my_r[0] + my_r[2])
        mx[0, 0] = here_sum[0]
        mx[0, 1] = here_sum[2]
        mx[1, 0] = here_sum[1]
        mx[1, 1] = here_sum[2]
        mx_sent = [remote(mx.at[1], mx_r.at[0], right), remote(mx.at[0], mx_r.at[1], over), remote(mx.at[1], mx_r.at[2], left)]
        arrived(c2)
        s = staged([c_r1.at[0], c_r1.at[2], c_r1.at[4]]) + [c_r2]
        lefts.run([((0,), 0, lambda l: product(c_m, [l], [pairs], s))])
        c3 = remote(c_m, c_x, over)

        a4 = settle(a_m, a_x, a3, piece3, pl.ds(0, 1024), True)
        b4 = settle(b_m, b_x, b3, piece2, pl.ds(0, 1024), True)
        d4 = settle(d_m, d_x, d3, piece1, pl.ds(512, 512), False)

        ng_own, ng4 = pass_rows(ng3, input_grad)
        arrived(mx_sent)
        last[...] = (mx[0] + mx_r[1]) + (mx_r[0] + mx_r[2])
        vec_copy = remote(last.at[1], last_r, mate)
        c4 = settle(c_m, c_x, c3, piece1, pl.ds(0, 512), False)
        vec_copy.wait_recv()
        last_saved = [here(last, vec_out.at[pl.ds(0, 2)]), here(last_r, vec_out.at[2])]

        for own, copy in (a4, b4, c4, d4):
            own.wait()
            copy.wait_recv()
        br_own.wait()
        ng_own.wait()
        arrived(br4 + ng4)
        for copy in last_saved:
            copy.wait()
        for copy in copies.sent:
            copy.wait_send()

    pl.run_scoped(
        finish,
        pltpu.VMEM((D, 1024), BF16),
        pltpu.VMEM((D, 1024), BF16),
        pltpu.VMEM((D, 1024), BF16),
    )


def reduce_call(*args):
    low = lambda *shape: jax.ShapeDtypeStruct(shape, BF16)
    wide = lambda *shape: jax.ShapeDtypeStruct(shape, F32)
    vlow = lambda *shape: pltpu.VMEM(shape, BF16)
    vwide = lambda *shape: pltpu.VMEM(shape, F32)
    anywhere = pl.BlockSpec(memory_space=pl.ANY)
    n = 1024
    outs = [low(HALF, D), low(HALF, D), low(2, BLK, n), low(2, BLK, n), low(2, BLK, n), wide(3, 8, BLK)] + [
        low(4, BLK, n), low(3, BLK, n), low(BLK, n), low(4, BLK, 512), low(4, BLK, n), low(BLK, n), low(BLK, n),
        low(6, BLK, 512), low(6, BLK, 512),
    ]
    result = pl.pallas_call(
        reduce_kernel,
        in_specs=[anywhere] * 20,
        out_specs=[anywhere] * len(outs),
        out_shape=outs,
        scratch_shapes=[
            vlow(ROWS, BLK), vlow(ROWS, BLK), vlow(ROWS, n), vlow(ROWS, n), vlow(ROWS, BLK), vlow(ROWS, 3 * BLK),
            vwide(8, PACK, 128), vwide(ROWS, 128), vwide(ROWS, 128), vwide(ROWS, 128), vwide(ROWS, 128), vwide(192, 128),
            vwide(2 * ROWS, BLK), vwide(2 * ROWS, BLK), vwide(128, ROWS), vwide(128, ROWS), vlow(2, ROWS, BLK),
            vlow(2, HALF, HALF), vlow(HALF, D), vlow(HALF, D), vlow(HALF, D), vlow(3, 128, D), vlow(128, D),
            vlow(HALF, D), vlow(HALF, D), vlow(3, 128, D), vlow(128, D), vlow(2, 2, 64, D), vlow(128, D), vlow(128, D),
            vlow(2, 2, BLK, ROWS), vlow(4, BLK, n), vlow(3, BLK, n), vlow(BLK, n), vlow(BLK, n), vlow(BLK, n),
            vlow(6, BLK, 512), vlow(BLK, 512), vlow(BLK, 512), vlow(6, BLK, 512), vlow(BLK, 512), vlow(BLK, 512),
            vlow(BLK, 512), vlow(BLK, 512), vlow(BLK, 512), vlow(BLK, 512), vwide(8, 8, BLK), vwide(8, 8, BLK),
            vwide(8, 8, BLK), vwide(3, 8, 8, BLK), vwide(8, 8, BLK), vwide(8, BLK), vwide(4, 3, 8, BLK),
            vwide(3, 3, 8, BLK), vwide(2, 2, 8, BLK), vwide(3, 2, 8, BLK), vwide(2, 8, BLK), vwide(8, BLK),
            vwide(1, D), vwide(1, n), vwide(1, 8, 8, BLK),
            pltpu.SemaphoreType.DMA((72,)),
            pltpu.SemaphoreType.DMA((72,)),
            pltpu.SemaphoreType.DMA((32,)),
            pltpu.SemaphoreType.DMA((2,)),
            pltpu.SemaphoreType.DMA((2, 2)),
            pltpu.SemaphoreType.DMA((4,)),
        ],
        compiler_params=params(collective_id=1, has_side_effects=True),
        cost_estimate=cost(2 * ROWS * D * 5 * 1024, 128 * 1024 * 1024),
        name="reduce_phase",
    )(*args)
    return result[:6]


def body(tokens, ln_gain, ln_shift, out_bias, w_qkv, b_qkv, w_out, w_fc1, b_fc1, w_fc2, out_grad):
    f, c = lax.axis_index("fsdp"), lax.axis_index("ctx")
    x_hi, core = c // 2, c % 2
    tokens, out_grad = tokens[0], out_grad[0]

    own = (jnp.arange(HD) // 8 == f)[None, None, :]
    spread = lambda v: jnp.where(own, jnp.tile(v, (1, 1, 8)), jnp.zeros((), BF16)).reshape(-1)
    pack = jnp.concatenate(
        [
            ln_gain,
            ln_shift,
            out_bias,
            spread(jnp.roll(lax.dynamic_slice_in_dim(b_qkv, core * 4, 4, axis=1), -1, axis=0)),
            spread(lax.dynamic_slice_in_dim(b_fc1, core * 16, 16, axis=0)[None]),
            jnp.zeros((512,), BF16),
        ]
    )
    pack = pack.astype(F32).reshape(PACK, 128)

    (w_attn, w_up, w_down, normed_t, grad_t, unit, q, kv, kvr, do, active, hidden_grad, small, bias_grad, up_bias_grad,
     a_first, b_first) = (
        gather_call(w_qkv.transpose(1, 0, 2), w_out, w_fc1, w_fc2, tokens, out_grad, pack, ROPE)
    )
    layer_out, input_grad, attn_all, up_all, down_all, vec = reduce_call(
        w_attn, w_up, w_down, normed_t, grad_t, unit, q, kv, kvr, do, active, hidden_grad, small, bias_grad, up_bias_grad,
        a_first, b_first, tokens, out_grad, ROPE
    )
    qkv_out, proj_out, up_out, down_out = grads_call(attn_all, up_all, down_all)
    gain_grad, shift_grad, out_bias_grad = vec[0, 0], vec[0, 1], vec[0, 2]
    units = jnp.where(core == 0, vec[1:], vec[:0:-1]).reshape(2, 8 * BLK)
    qkv_bias_out = lax.dynamic_slice_in_dim(
        jnp.roll(units[:, : 3 * BLK].reshape(2, 3, 4, HD), 1, axis=1).transpose(1, 0, 2, 3).reshape(3, 8, HD), f * 8, 8, axis=2
    )
    up_bias_out = lax.dynamic_slice_in_dim(units[:, 3 * BLK : 7 * BLK].reshape(32, HD), f * 8, 8, axis=1)
    return (
        layer_out[None],
        input_grad[None],
        gain_grad,
        shift_grad,
        out_bias_grad,
        qkv_out.transpose(1, 0, 2),
        qkv_bias_out,
        proj_out,
        up_out,
        up_bias_out,
        down_out,
    )


def solution(mesh):
    in_specs = (
        P("fsdp", "ctx", None),
        P("fsdp"),
        P("fsdp"),
        P("fsdp"),
        P("fsdp", None, "tp"),
        P(None, "tp", "fsdp"),
        P("tp", "fsdp"),
        P("fsdp", "tp"),
        P("tp", "fsdp"),
        P("tp", "fsdp"),
        P("fsdp", "ctx", None),
    )
    out_specs = (
        P("fsdp", "ctx", None),
        P("fsdp", "ctx", None),
        P("fsdp"),
        P("fsdp"),
        P("fsdp"),
        P("fsdp", None, "tp"),
        P(None, "tp", "fsdp"),
        P("tp", "fsdp"),
        P("fsdp", "tp"),
        P("tp", "fsdp"),
        P("tp", "fsdp"),
    )
    return jax.shard_map(body, mesh=mesh, in_specs=in_specs, out_specs=out_specs, check_vma=False)
```

```python
import math

import jax
import jax.numpy as jnp
import numpy as np
from jax import lax
from jax.experimental import pallas as pl
from jax.experimental.pallas import tpu as pltpu
from jax.sharding import PartitionSpec as P

D = 2048
HD = 64
ROT = 32
BLK = 256
ROWS = 1024
HALF = 512
EPSILON = 1e-05
MASKED = -1e30
F32 = jnp.float32
BF16 = jnp.bfloat16
VMEM_LIMIT = 62 * 1024 * 1024


def params(**kw):
    return pltpu.CompilerParams(vmem_limit_bytes=VMEM_LIMIT, **kw)


def whole():
    return pl.BlockSpec(memory_space=pltpu.VMEM)


def cost(flops, nbytes, trans=0):
    return pl.CostEstimate(flops=int(flops), bytes_accessed=int(nbytes), transcendentals=int(trans))


def block_order(y, x_lo, j):
    dx, dy = j // 4, j % 4
    return lax.rem(y + dy, 4) * 2 + lax.rem(x_lo + dx, 2)


def partner(v):
    lane = lax.broadcasted_iota(jnp.int32, v.shape, 1)
    up = pltpu.roll(v, v.shape[1] - ROT // 2, 1)
    down = pltpu.roll(v, ROT // 2, 1)
    return jnp.where(lane % HD < ROT // 2, up, down)


QT = 256
KC = 512


def rope_table():
    lane = np.arange(128) % HD
    freq = np.where(lane < ROT, 10000.0 ** (-2.0 * (lane % (ROT // 2)) / ROT), 0.0)
    sign = np.where(lane < ROT // 2, -1.0, 1.0)
    coarse, fine = np.arange(64)[:, None] * 32 * freq, np.arange(32)[:, None] * freq
    parts = [np.cos(coarse), np.sin(coarse) * sign, np.cos(fine), np.sin(fine) * sign]
    return np.concatenate(parts).astype(np.float32)


ROPE = rope_table()
GELU_C = math.sqrt(2.0 / math.pi)


MESH = pl.DeviceIdType.MESH
PACK = 24


def coords():
    f, c, z = lax.axis_index("fsdp"), lax.axis_index("ctx"), lax.axis_index("tp")
    return (c // 2) * 2 + f % 2, f // 2, z, c % 2


def device(x, y, z, core):
    return (y * 2 + lax.rem(x, 2), (x // 2) * 2 + core, z)


def beside(dx=0, dy=0, flip=0, dz=0):
    x, y, z, core = coords()
    return device(
        lax.rem(x + dx + 4, 4), lax.rem(y + dy + 4, 4), lax.rem(z + dz + 4, 4), (1 - core) if flip else core
    )


def greet(targets):
    barrier = pltpu.get_barrier_semaphore()
    for target in targets:
        pl.semaphore_signal(barrier, inc=1, device_id=target, device_id_type=MESH)
    pl.semaphore_wait(barrier, len(targets))


class Copies:
    def __init__(self, send, recv, local):
        self.send, self.recv, self.local = send, recv, local
        self.remotes = self.locals = 0
        self.sent = []

    def make(self, src, dst, target):
        i = self.remotes
        self.remotes += 1
        return pltpu.make_async_remote_copy(
            src, dst, self.send.at[i], self.recv.at[i], device_id=target, device_id_type=MESH
        )

    def remote(self, src, dst, target):
        copy = self.make(src, dst, target)
        copy.start()
        self.sent.append(copy)
        return copy

    def here(self, src, dst):
        copy = pltpu.make_async_copy(src, dst, self.local.at[self.locals])
        self.locals += 1
        copy.start()
        return copy


def rope_rows(table, first, cos, sin, count):
    @pl.loop(0, count // 32)
    def _(i):
        at = pl.ds(pl.multiple_of(i * 32, 32), 32)
        ch, sh = table[pl.ds(first // 32 + i, 1), :], table[pl.ds(64 + first // 32 + i, 1), :]
        cl, sl = table[128:160, :], table[160:192, :]
        cos[at, :] = ch * cl - sh * sl
        sin[at, :] = sh * cl + ch * sl


def turn(v, c, s):
    return v * c + partner(v) * s


def gather_kernel(s1_in, proj_in, up_in, down_in, tok_in, grad_in, pack, table_in,
                  w1_out, w2_out, w3_out, normed_t_out, grad_t_out, unit_out, q_out, kv_out, kvr_out, do_out,
                  active_out, hidden_out, small_out, bias_out, up_bias_out, a_s1_out, b_s1_out,
                  w1, w2, w3, tok, grad, normed, grad_rel, normed_t, grad_t, unit, small, q, kv, do, active, slope,
                  hidden, cos, sin, table, bias_sum, up_bias_sum, proj_v, down_v, send, recv, local):
    x, y, z, core = coords()
    x_lo, x_hi = lax.rem(x, 2), x // 2
    up, down, far = beside(dy=1), beside(dy=3), beside(dy=2)
    right, left, over, mate = beside(dx=1), beside(dx=3), beside(dx=2), beside(flip=1)
    copies = Copies(send, recv, local)
    here, remote = copies.here, copies.remote
    hcols = pl.ds(pl.multiple_of(core * 1024, 1024), 1024)
    hrows = pl.ds(pl.multiple_of(core * 1024, 1024), 1024)
    prows = pl.ds(pl.multiple_of(core * BLK, BLK), BLK)
    own_block = pl.ds(0, BLK)
    proj_load = here(proj_in.at[prows], proj_v)
    down_load = here(down_in.at[hrows], down_v)
    s1_loads = [
        here(s1_in.at[c, :, prows], w1.at[own_block, pl.ds(k * BLK, BLK)]) for k, c in enumerate((1, 2, 0))
    ]
    up_load = here(up_in.at[:, hcols], w2.at[own_block])
    greet([up, down, far, right, left, over, mate])

    class Part:
        def __init__(self, w, at, n):
            self.w, self.cols, self.moves = w, pl.ds(at, n), []

        def rows(self, j, first=0, count=BLK):
            return self.w.at[pl.ds(j * BLK + first, count), self.cols]

        def to(self, j, k, target, first=0, count=BLK):
            copy = remote(self.rows(j, first, count), self.rows(k, first, count), target)
            self.moves.append(copy)
            return copy

        def along_y(self, base):
            return [self.to(base, base + 3, up), self.to(base, base + 1, down), self.to(base, base + 2, far)]

        def sideways(self):
            return [self.to(0, 4, right, 0, BLK // 2), self.to(0, 4, left, BLK // 2, BLK // 2)]

        def begin_x(self):
            self.x = self.sideways()

        def begin_y(self):
            self.y = self.along_y(0)

        def forward(self):
            for copy in self.y:
                copy.wait_recv()
            self.x += [
                self.to(1, 5, right), self.to(3, 7, left),
                self.to(2, 6, right, 0, BLK // 2), self.to(2, 6, left, BLK // 2, BLK // 2),
            ]

        def forward_y(self):
            for copy in self.x:
                copy.wait_recv()
            self.x = self.along_y(4)

        def arrived(self):
            for copy in self.x:
                copy.wait_recv()

        def all_arrived(self):
            for copy in self.y + self.x:
                copy.wait_recv()

    keys_part, query_part, proj_part = Part(w1, 0, 512), Part(w1, 512, BLK), Part(w1, 768, BLK)
    up_part = Part(w2, 0, 1024)
    down_a, down_b = Part(w3, 0, 512), Part(w3, 512, 512)

    my_rows = pl.ds(pl.multiple_of(core * HALF, HALF), HALF)
    pack_y = [remote(pack, small.at[3], up), remote(pack, small.at[1], down), remote(pack, small.at[2], far)]
    pack_own = here(pack, small.at[0])
    tok_copy = remote(tok_in, tok.at[my_rows], mate)
    grad_copy = remote(grad_in, grad.at[my_rows], mate)
    for copy in s1_loads:
        copy.wait()
    keys_part.begin_y()
    keys_part.begin_x()
    mine = [here(tok_in, tok.at[my_rows]), here(grad_in, grad.at[my_rows])]
    table_load = here(table_in, table)

    proj_load.wait()
    w1[0:BLK, 3 * BLK :] = proj_v[...].astype(F32).T.astype(BF16)
    down_load.wait()
    for k in range(4):
        w3[0:BLK, k * BLK : (k + 1) * BLK] = down_v[k * BLK : (k + 1) * BLK, :].astype(F32).T.astype(BF16)
    for copy in pack_y:
        copy.wait_recv()
    pack_own.wait()
    pack_x = remote(small.at[pl.ds(0, 4)], small.at[pl.ds(4, 4)], right)
    up_load.wait()
    up_part.begin_x()
    down_b.begin_x()
    proj_part.begin_x()
    table_load.wait()
    rope_rows(table, x_hi * ROWS, cos, sin, ROWS)
    up_part.begin_y()
    down_b.begin_y()
    keys_part.forward()
    down_b.forward_y()
    down_a.begin_y()
    proj_part.begin_y()
    query_part.begin_y()
    for copy in mine:
        copy.wait()
    tok_copy.wait_recv()
    grad_copy.wait_recv()
    pack_x.wait_recv()

    bias_sum[...] = jnp.zeros_like(bias_sum)
    up_bias_sum[...] = jnp.zeros_like(up_bias_sum)
    tile = 128

    def prepare(first, last):
        @pl.loop(first, last)
        def _(i):
            at = pl.ds(pl.multiple_of(i * tile, tile), tile)
            rows = tok[at, :].astype(F32)
            mean = jnp.mean(rows, axis=-1, keepdims=True)
            centered = rows - mean
            inv = lax.rsqrt(jnp.mean(centered * centered, axis=-1, keepdims=True) + EPSILON)
            for j in range(8):
                src = pl.ds(pl.multiple_of(block_order(y, x_lo, j) * BLK, BLK), BLK)
                dst = pl.ds(j * BLK, BLK)
                gain = jnp.concatenate([small[j, 0:1, :], small[j, 1:2, :]], axis=1)
                shift = jnp.concatenate([small[j, 2:3, :], small[j, 3:4, :]], axis=1)
                u = (tok[at, src].astype(F32) - mean) * inv
                n = u * gain + shift
                normed[at, dst] = n.astype(BF16)
                normed_t[dst, at] = n.T.astype(BF16)
                unit[at, dst] = u.astype(BF16)
                g = grad[at, src]
                g32 = g.astype(F32)
                grad_rel[at, dst] = g
                grad_t[dst, at] = g32.T.astype(BF16)
                bias_sum[:, dst] += jnp.sum(g32, axis=0, keepdims=True)

    prepare(0, 8)
    saved = [here(normed_t, normed_t_out), here(grad_t, grad_t_out), here(unit, unit_out), here(small, small_out),
             here(bias_sum, bias_out)]

    biases = small[0, 6:20, :]
    for j in range(1, 8):
        biases = biases + small[j, 6:20, :]
    qkv_bias = jnp.concatenate([biases[j : j + 1] for j in range(6)], axis=1)
    up_bias = jnp.concatenate([biases[j : j + 1] for j in range(6, 14)], axis=1)
    big = 256
    keys_part.arrived()

    @pl.loop(0, ROWS // big)
    def _(i):
        at = pl.ds(pl.multiple_of(i * big, big), big)
        raw = jnp.dot(normed[at, :], w1[:, : 2 * BLK], preferred_element_type=F32) + qkv_bias[:, : 2 * BLK]
        c, s = cos[at, :], sin[at, :]
        for k in range(2):
            lanes = slice(k * 128, (k + 1) * 128)
            kv[at, lanes] = turn(raw[:, lanes], c, s).astype(BF16)
        kv[at, BLK:] = raw[:, BLK:].astype(BF16)

    kv_copy = copies.make(kv, kvr_out, over)

    @pl.when(x_hi == 0)
    def _():
        kv_copy.start()

    saved.append(here(kv, kv_out))
    up_part.forward()
    proj_part.forward_y()
    query_part.begin_x()
    down_a.begin_x()
    up_part.arrived()
    saved.append(here(w2, w2_out))

    @pl.loop(0, ROWS // big)
    def _(i):
        at = pl.ds(pl.multiple_of(i * big, big), big)
        v = jnp.dot(normed[at, :], w2[...], preferred_element_type=F32) + up_bias
        sq = v * v
        t = jnp.tanh(GELU_C * v * (1.0 + 0.044715 * sq))
        half = 0.5 * (1.0 + t)
        active[at, :] = (v * half).astype(BF16)
        slope[at, :] = (half + 0.5 * v * (1.0 - t * t) * (GELU_C * (1.0 + 3 * 0.044715 * sq))).astype(BF16)

    saved.append(here(active, active_out))
    down_a.forward()

    place = [buf.at[:, pl.ds(k * 1024, 1024)] for buf in (tok, grad) for k in range(2)]

    def partials(left, right, blocks, dst, out):
        for k, j in enumerate(blocks):
            at = pl.ds((k % 4) * BLK, BLK)
            dst[k // 4][at, :] = jnp.dot(left[j * BLK : (j + 1) * BLK, :], right[...], preferred_element_type=F32).astype(BF16)
            saved.append(here(dst[k // 4].at[at], out.at[k]))

    partials(grad_t, active, (4, 5, 6, 7), place[:1], a_s1_out)
    query_part.forward()
    down_a.arrived()
    down_b.all_arrived()
    saved.append(here(w3, w3_out))

    @pl.loop(0, ROWS // big)
    def _(i):
        at = pl.ds(pl.multiple_of(i * big, big), big)
        v = jnp.dot(grad_rel[at, :], w3[...], preferred_element_type=F32) * slope[at, :].astype(F32)
        low = v.astype(BF16)
        hidden[at, :] = low
        up_bias_sum[...] += jnp.sum(low.astype(F32), axis=0, keepdims=True)

    saved += [here(hidden, hidden_out), here(up_bias_sum, up_bias_out)]
    partials(normed_t, hidden, (2, 6, 1, 5, 3, 7), place[1:3], b_s1_out)
    query_part.arrived()
    proj_part.all_arrived()
    saved.append(here(w1, w1_out))

    @pl.loop(0, ROWS // big)
    def _(i):
        at = pl.ds(pl.multiple_of(i * big, big), big)
        raw = jnp.dot(normed[at, :], w1[:, 2 * BLK : 3 * BLK], preferred_element_type=F32) + qkv_bias[:, 2 * BLK :]
        c, s = cos[at, :], sin[at, :]
        for k in range(2):
            lanes = slice(k * 128, (k + 1) * 128)
            q[at, lanes] = (turn(raw[:, lanes], c, s).astype(BF16).astype(F32) * (HD**-0.5)).astype(BF16)
        do[at, :] = jnp.dot(grad_rel[at, :], w1[:, 3 * BLK :], preferred_element_type=F32).astype(BF16)

    saved += [here(q, q_out), here(do, do_out)]
    for copy in copies.sent:
        copy.wait_send()

    @pl.when(x_hi == 0)
    def _():
        kv_copy.wait_send()

    @pl.when(x_hi == 1)
    def _():
        kv_copy.wait_recv()

    for copy in saved:
        copy.wait()


def gather_call(*args):
    n = 1024
    low = lambda *shape: jax.ShapeDtypeStruct(shape, BF16)
    wide = lambda *shape: jax.ShapeDtypeStruct(shape, F32)
    vlow = lambda *shape: pltpu.VMEM(shape, BF16)
    vwide = lambda *shape: pltpu.VMEM(shape, F32)
    anywhere = pl.BlockSpec(memory_space=pl.ANY)
    return pl.pallas_call(
        gather_kernel,
        in_specs=[anywhere] * 8,
        out_specs=[anywhere] * 17,
        out_shape=[
            low(D, n), low(D, n), low(D, n), low(D, ROWS), low(D, ROWS), low(ROWS, D), low(ROWS, BLK), low(ROWS, 2 * BLK),
            low(ROWS, 2 * BLK), low(ROWS, BLK), low(ROWS, n), low(ROWS, n), wide(8, PACK, 128), wide(1, D), wide(1, n),
            low(4, BLK, n), low(6, BLK, n),
        ],
        scratch_shapes=[
            vlow(D, n), vlow(D, n), vlow(D, n), vlow(ROWS, D), vlow(ROWS, D), vlow(ROWS, D), vlow(ROWS, D), vlow(D, ROWS),
            vlow(D, ROWS), vlow(ROWS, D), vwide(8, PACK, 128), vlow(ROWS, BLK), vlow(ROWS, 2 * BLK), vlow(ROWS, BLK),
            vlow(ROWS, n), vlow(ROWS, n), vlow(ROWS, n), vwide(ROWS, 128), vwide(ROWS, 128), vwide(192, 128), vwide(1, D),
            vwide(1, n), vlow(BLK, BLK), vlow(n, BLK),
            pltpu.SemaphoreType.DMA((64,)),
            pltpu.SemaphoreType.DMA((64,)),
            pltpu.SemaphoreType.DMA((40,)),
        ],
        compiler_params=params(collective_id=0, has_side_effects=True),
        cost_estimate=cost(2 * ROWS * D * 3 * n, 64 * 1024 * 1024),
        name="gather_phase",
    )(*args)


def grads_kernel(attn, up, down, rows_a, rows_b, qkv_out, proj_out, up_out, down_out, rows_a_out, rows_b_out):
    rows_a_out[...] = rows_a[...]
    rows_b_out[...] = rows_b[...]
    for core in range(2):
        for k, c in enumerate((1, 2, 0)):
            qkv_out[c, :, core * BLK : (core + 1) * BLK] = attn[core, :, k * BLK : (k + 1) * BLK].astype(F32)
        proj_out[core * BLK : (core + 1) * BLK, :] = attn[core, :, 3 * BLK :].astype(F32).T
        up_out[:, core * 1024 : (core + 1) * 1024] = up[core].astype(F32)
        down_out[core * 1024 : (core + 1) * 1024, :] = down[core].astype(F32).T


def grads_call(attn, up, down, rows_a, rows_b):
    tile = 128
    piece = pl.BlockSpec((2, tile, 1024), lambda i: (0, i, 0))
    rows = pl.BlockSpec((HALF * tile // BLK, D), lambda i: (i, 0))
    wide = lambda *shape: jax.ShapeDtypeStruct(shape, F32)
    return pl.pallas_call(
        grads_kernel,
        grid=(BLK // tile,),
        in_specs=[piece] * 3 + [rows] * 2,
        out_specs=[
            pl.BlockSpec((3, tile, HALF), lambda i: (0, i, 0)),
            pl.BlockSpec((HALF, tile), lambda i: (0, i)),
            pl.BlockSpec((tile, 2048), lambda i: (i, 0)),
            pl.BlockSpec((2048, tile), lambda i: (0, i)),
            rows,
            rows,
        ],
        out_shape=[wide(3, BLK, HALF), wide(HALF, BLK), wide(BLK, 2048), wide(2048, BLK)]
        + [jax.ShapeDtypeStruct((HALF, D), BF16)] * 2,
        compiler_params=params(),
        cost_estimate=cost(0, 10 * 1024 * 1024),
        name="gradients",
    )(attn, up, down, rows_a, rows_b)


class Lefts:
    def __init__(self, sources, buf, sems):
        self.sources, self.buf, self.sems = sources, buf, sems
        self.queue, self.count = ([], []), [0, 0]

    def want(self, kind, j):
        if any(held == j for held, _ in self.queue[kind]):
            return
        slot = self.count[kind] % 2
        self.count[kind] += 1
        self.move(kind, j, slot).start()
        self.queue[kind].append((j, slot))

    def take(self, kind, j):
        held, slot = self.queue[kind].pop(0)
        assert held == j
        self.move(kind, j, slot).wait()
        return self.buf.at[kind, slot]

    def move(self, kind, j, slot):
        return pltpu.make_async_copy(
            self.sources[kind].at[pl.ds(j * BLK, BLK)], self.buf.at[kind, slot], self.sems.at[kind, slot]
        )

    def run(self, jobs, after=()):
        for i, (kinds, j, act) in enumerate(jobs):
            for kind in kinds:
                self.want(kind, j)
            ahead = jobs[i + 1][:2] if i + 1 < len(jobs) else after
            if ahead:
                for kind in ahead[0]:
                    self.want(kind, ahead[1])
            act(*[self.take(kind, j) for kind in kinds])


def product(dst, lefts, rights, adds=()):
    at = 0
    for left, right in zip(lefts, rights):
        cols = slice(at, at + right.shape[1])
        total = jnp.dot(left[...], right[...], preferred_element_type=F32)
        for add in adds:
            total += add[:, cols].astype(F32)
        dst[:, cols] = total.astype(BF16)
        at += right.shape[1]


def row_products(half, a, b, w1, col1, w2, out, unit=None, ub=None, sems=None, vec=None):
    nt = (((1,), (1,)), ((), ()))
    ka = a.shape[1]
    rows = pl.ds(pl.multiple_of(half * HALF, HALF), HALF)

    def fetch(j, slot):
        at = pl.ds(pl.multiple_of(j * HALF, HALF), HALF)
        return pltpu.make_async_copy(unit.at[rows, at], ub.at[slot], sems.at[slot])

    if unit is not None:
        fetch(0, 0).start()

    @pl.loop(0, D // HALF)
    def _(j):
        at = pl.ds(pl.multiple_of(j * HALF, HALF), HALF)
        slot = lax.rem(j, 2)
        if unit is not None:
            fetch(j, slot).wait()

            @pl.when(j < D // HALF - 1)
            def _():
                fetch(j + 1, 1 - slot).start()

        total = lax.dot_general(a[rows, :], w1[at, col1 : col1 + ka], nt, preferred_element_type=F32)
        total += lax.dot_general(b[rows, :], w2[at, :], nt, preferred_element_type=F32)
        out[:, at] = total.astype(BF16)
        if unit is not None:
            weighted = jnp.sum(total * ub[slot].astype(F32), axis=0, keepdims=True)
            plain = jnp.sum(total, axis=0, keepdims=True)
            for k in range(2):
                vec[2 * j + k, 0:1, :] = weighted[:, k * BLK : (k + 1) * BLK]
                vec[2 * j + k, 1:2, :] = plain[:, k * BLK : (k + 1) * BLK]


def add_rows(mine, got):
    @pl.loop(0, 4)
    def _(i):
        at = pl.ds(pl.multiple_of(i * 128, 128), 128)
        mine[at, :] = (mine[at, :].astype(F32) + got[at, :].astype(F32)).astype(BF16)


def reduce_kernel(w1, w2, w3, normed_t, grad_t, unit, q_in, kv_in, kvr_in, do_in, active_in, hidden_in, small_in, bias_in,
                  up_bias_in, a_s1, b_s1, tok_in, grad_in, table_in,
                  layer_out, input_grad, piece1, piece2, piece3, vec_out,
                  a_r1, a_r2, a_x, b_p, b_r1, b_r2, b_x, c_r1, d_r1,
                  q, do, active, hidden, att, raw, small, cos, sin, cos_r, sin_r, table,
                  dk, dv, out_t, dq_t, dkv, ub, theirs, br_m, br_c, br_z, br_o, ng_m, ng_c, ng_z, ng_o,
                  turned, tok, grad, left_buf, stage, a_s2, a_m, b_s2, b_m, c_s1, c_s2, c_m, d_s1, d_s2, d_m, c_r2, c_x, d_r2, d_x,
                  vec_t, vec_m, va, va_r, vb_r, units, my, my_r, mx, mx_r, last, last_r, bias_v, up_bias_v, vec_v,
                  send, recv, local, sems, left_sems, stage_sems):
    x, y, z, core = coords()
    x_lo, x_hi = lax.rem(x, 2), x // 2
    other = 1 - core
    up, down, far = beside(dy=1), beside(dy=3), beside(dy=2)
    right, left, over = beside(dx=1), beside(dx=3), beside(dx=2)
    mate = beside(flip=1)
    above, below = beside(dz=1), beside(dz=3)
    along = [above, beside(dz=2), below]
    copies = Copies(send, recv, local)
    here, remote = copies.here, copies.remote
    nt = (((1,), (1,)), ((), ()))

    load_active, load_hidden = here(active_in, active), here(hidden_in, hidden)
    own_keys = pl.ds(pl.multiple_of(x_hi * ROWS, ROWS), ROWS)
    loads = [here(table_in, table), here(q_in, q), here(do_in, do), here(small_in, small), here(bias_in, bias_v),
              here(up_bias_in, up_bias_v)]
    z_rows = pl.ds(pl.multiple_of(z * 128, 128), 128)
    loads += [here(tok_in.at[z_rows], tok), here(grad_in.at[z_rows], grad)]
    greet([up, down, far, right, left, over, mate] + along)
    lo, hi, first, second = pl.ds(0, 512), pl.ds(512, 512), pl.ds(0, 2), pl.ds(2, 2)
    bp = [remote(b_s1.at[first, :, lo], b_p.at[first], up), remote(b_s1.at[first, :, hi], b_p.at[second], down)]
    b1 = [
        remote(b_s1.at[second, :, hi], b_r1.at[first, :, hi], up),
        remote(b_s1.at[pl.ds(4, 2), :, lo], b_r1.at[second, :, lo], down),
    ]
    a1 = [remote(a_s1.at[pl.ds(2 * k, 2)], a_r1.at[pl.ds(2 * k, 2)], target) for k, target in enumerate((right, left))]

    lefts = Lefts((normed_t, grad_t), left_buf, left_sems)

    def staged(parts):
        views, found = [], []
        for k, part in enumerate(parts):
            view = stage.at[k, :, pl.ds(0, part.shape[-1])]
            copy = pltpu.make_async_copy(part, view, stage_sems.at[k])
            copy.start()
            found.append(copy)
            views.append(view)
        for copy in found:
            copy.wait()
        return views

    def arrived(moves):
        for copy in moves:
            copy.wait_recv()

    def settle(mine, got, move, piece, cols, on_hbm):
        move.wait_send()
        copies.sent = [copy for copy in copies.sent if copy is not move]
        move.wait_recv()
        more = staged([got])[0] if on_hbm else got
        mine[...] = (mine[...].astype(F32) + more[...].astype(F32)).astype(BF16)
        spot = piece.at[core, :, cols]
        return here(mine, spot), remote(mine, spot, mate)

    def turn_back(v, c, s):
        return v * c - partner(v) * s

    upper, lower = pl.ds(0, BLK // 2), pl.ds(BLK // 2, BLK // 2)
    pairs_back = [copies.make(dkv.at[k], dkv.at[k], over) for k in range(2)]
    passed = [
        copies.make(c_s1.at[first], b_r1.at[first, :, lo], up),
        copies.make(c_s1.at[second], b_r1.at[second, :, hi], down),
    ]
    a_y = [copies.make(a_s2.at[k], a_r2.at[k], target) for k, target in enumerate((far, down, up))]
    b2 = [copies.make(b_s2.at[upper], b_r2.at[upper], right), copies.make(b_s2.at[lower], b_r2.at[lower], left)]
    copies.sent += passed + a_y + b2

    def attend(keys, vals, keys_t, vals_t, st, dp, qm, dom):
        own = here(kv_in.at[:, pl.ds(0, BLK)], keys.at[own_keys]), here(kv_in.at[:, pl.ds(BLK, BLK)], vals.at[own_keys])
        far_keys = pltpu.make_async_copy(kvr_in.at[:, pl.ds(0, BLK)], keys.at[pl.ds(0, ROWS)], local.at[copies.locals])
        far_vals = pltpu.make_async_copy(kvr_in.at[:, pl.ds(BLK, BLK)], vals.at[pl.ds(0, ROWS)], local.at[copies.locals + 1])
        copies.locals += 2

        @pl.when(x_hi == 1)
        def _():
            far_keys.start()
            far_vals.start()
        for copy in loads + list(own):
            copy.wait()

        @pl.when(x_hi == 1)
        def _():
            far_keys.wait()
            far_vals.wait()

        @pl.loop(0, (x_hi + 1) * (ROWS // KC))
        def _(j):
            at = pl.ds(pl.multiple_of(j * KC, KC), KC)
            keys_t[:, at] = keys[at, :].astype(F32).T.astype(BF16)
            vals_t[:, at] = vals[at, :].astype(F32).T.astype(BF16)
            dk[at, :] = jnp.zeros((KC, BLK), F32)
            dv[at, :] = jnp.zeros((KC, BLK), F32)

        rope_rows(table, x_hi * ROWS, cos, sin, ROWS)
        rope_rows(table, 0, cos_r, sin_r, ROWS)
        lane = lax.broadcasted_iota(jnp.int32, (QT, 128), 1) // HD

        def heads(pair, tiles):
            lanes = slice(pair * 128, pair * 128 + 128)
            for t in tiles:
                rows = slice(t * QT, (t + 1) * QT)
                full = x_hi * (ROWS // KC) + t * QT // KC
                rest = (t + 1) * QT - t * QT // KC * KC
                diagonal = pl.ds(pl.multiple_of(full * KC, KC), rest)

                def chunk(j):
                    return pl.ds(pl.multiple_of(j * KC, KC), KC)

                for side in range(2):
                    qm[side] = jnp.where(lane == side, q[rows, lanes], jnp.zeros((), BF16))
                    dom[side] = jnp.where(lane == side, do[rows, lanes], jnp.zeros((), BF16))

                def score(at, tops, masked):
                    new = []
                    for side in range(2):
                        s = lax.dot_general(keys[at, lanes], qm[side], nt, preferred_element_type=F32)
                        if masked:
                            ki = lax.broadcasted_iota(jnp.int32, (rest, QT), 0)
                            qi = lax.broadcasted_iota(jnp.int32, (rest, QT), 1) + t * QT % KC
                            s = jnp.where(ki <= qi, s, MASKED)
                        st[side, at, :] = s
                        new.append(jnp.maximum(tops[side], jnp.max(s, axis=0, keepdims=True)))
                    return tuple(new)

                low = jnp.full((1, QT), MASKED, F32)
                tops = lax.fori_loop(0, full, lambda j, m: score(chunk(j), m, False), (low, low))
                tops = score(diagonal, tops, True)

                def weigh(at, carry):
                    new = []
                    for side in range(2):
                        total, dot = carry[2 * side : 2 * side + 2]
                        p = jnp.exp(st[side, at, :] - tops[side])
                        st[side, at, :] = p
                        d = lax.dot_general(vals[at, lanes], dom[side], nt, preferred_element_type=F32)
                        dp[side, at, :] = d
                        new.append(total + jnp.sum(p, axis=0, keepdims=True))
                        new.append(dot + jnp.sum(p * d, axis=0, keepdims=True))
                    return tuple(new)

                zero = jnp.zeros((1, QT), F32)
                sums = weigh(diagonal, lax.fori_loop(0, full, lambda j, m: weigh(chunk(j), m), (zero,) * 4))
                inv = [1.0 / sums[0], 1.0 / sums[2]]
                delta = [sums[1] * inv[0], sums[3] * inv[1]]
                out_t[:, rows] = jnp.zeros((128, QT), F32)
                dq_t[:, rows] = jnp.zeros((128, QT), F32)

                def spread(at):
                    new_v, new_k = dv[at, lanes], dk[at, lanes]
                    for side in range(2):
                        hrows = slice((2 * pair + side) * HD, (2 * pair + side + 1) * HD)
                        trows = slice(side * HD, (side + 1) * HD)
                        p = st[side, at, :] * inv[side]
                        p_low = p.astype(BF16)
                        ds = (p * (dp[side, at, :] - delta[side])).astype(BF16)
                        out_t[trows, rows] += jnp.dot(vals_t[hrows, at], p_low, preferred_element_type=F32)
                        dq_t[trows, rows] += jnp.dot(keys_t[hrows, at], ds, preferred_element_type=F32)
                        new_v += jnp.dot(p_low, dom[side], preferred_element_type=F32)
                        new_k += jnp.dot(ds, qm[side], preferred_element_type=F32)
                    dv[at, lanes] = new_v
                    dk[at, lanes] = new_k

                @pl.loop(0, full)
                def _(j):
                    spread(chunk(j))

                spread(diagonal)

        def end_pair(pair):
            lanes = slice(pair * 128, pair * 128 + 128)
            copy = pairs_back[pair]

            @pl.when(x_hi == 1)
            def _():
                dkv[pair, :, :128] = turn_back(dk[:ROWS, lanes], cos_r[...], sin_r[...]).astype(BF16)
                dkv[pair, :, 128:] = dv[:ROWS, lanes].astype(BF16)
                copy.start()

            for t in range(ROWS // 512):
                rows = slice(t * 512, (t + 1) * 512)
                att[rows, lanes] = out_t[:, rows].T.astype(BF16)
                raw[rows, 2 * BLK + pair * 128 : 2 * BLK + pair * 128 + 128] = turn_back(
                    dq_t[:, rows].T * (HD**-0.5), cos[rows, :], sin[rows, :]
                ).astype(BF16)

        heads(0, (0, 1, 2))

        def pass_blocks(move, own, got, cols, buf):
            move.wait_recv()
            views = staged([b_s1.at[own, :, cols], b_p.at[got], b_s1.at[own + 1, :, cols], b_p.at[got + 1]])
            for k in range(2):
                c_s1[buf + k] = (views[2 * k][...].astype(F32) + views[2 * k + 1][...].astype(F32)).astype(BF16)
            passed[buf // 2].start()

        pass_blocks(bp[0], 2, 0, lo, 0)
        pass_blocks(bp[1], 4, 2, hi, 2)
        heads(0, (3,))
        end_pair(0)

        heads(1, (0, 1, 2))

        heads(1, (3,))
        end_pair(1)

    pl.run_scoped(
        attend,
        pltpu.VMEM((2 * ROWS, BLK), BF16),
        pltpu.VMEM((2 * ROWS, BLK), BF16),
        pltpu.VMEM((BLK, 2 * ROWS), BF16),
        pltpu.VMEM((BLK, 2 * ROWS), BF16),
        pltpu.VMEM((2, 2 * ROWS, QT), F32),
        pltpu.VMEM((2, 2 * ROWS, QT), F32),
        pltpu.VMEM((2, QT, 128), BF16),
        pltpu.VMEM((2, QT, 128), BF16),
    )
    def finish(w1v, w2v, w3v):
        w_loads = [here(w1, w1v), here(w3, w3v), here(w2, w2v)]

        def z_at(dz, first=0, count=128):
            return pl.ds(pl.multiple_of(lax.rem(z + dz, 4) * 128 + first, 64), count)

        def to_z(total, got):
            return [
                remote(total.at[z_at(2, 0, 64)], got.at[0, pl.ds(0, 64)], above),
                remote(total.at[z_at(2, 64, 64)], got.at[0, pl.ds(64, 64)], below),
                remote(total.at[z_at(1, 64, 64)], got.at[1, pl.ds(64, 64)], above),
                remote(total.at[z_at(3, 0, 64)], got.at[2, pl.ds(0, 64)], below),
            ]

        def pass_on(total, got, first, buf):
            first[0].wait_recv()
            buf[0] = (total[z_at(1, 0, 64), :].astype(F32) + got[0, :64, :].astype(F32)).astype(BF16)
            one = remote(buf.at[0], got.at[1, pl.ds(0, 64)], above)
            first[1].wait_recv()
            buf[1] = (total[z_at(3, 64, 64), :].astype(F32) + got[0, 64:, :].astype(F32)).astype(BF16)
            two = remote(buf.at[1], got.at[2, pl.ds(64, 64)], below)
            return [first[2], first[3], one, two]

        def from_z(chunk, rows):
            at = z_at(0)
            return [here(chunk, rows.at[at]), remote(chunk, rows.at[at], above), remote(chunk, rows.at[at], below)]

        def pass_rows(moves, rows):
            moves[1].wait_recv()
            one = remote(rows.at[z_at(3, 0, 64)], rows.at[z_at(3, 0, 64)], above)
            moves[2].wait_recv()
            two = remote(rows.at[z_at(1, 64, 64)], rows.at[z_at(1, 64, 64)], below)
            return moves[0], [one, two]

        load_active.wait()
        load_hidden.wait()
        lefts.want(1, 2)
        arrived(a1)
        s = staged([a_r1.at[2], a_r1.at[3], a_r1.at[1]])
        lefts.run(
            [((1,), j, lambda l, k=k: product(a_s2.at[k], [l], [active], [s[k]])) for k, j in enumerate((2, 3, 1))],
            after=((0, 1), 2),
        )
        for copy in a_y:
            copy.start()
        tail = [raw.at[:, pl.ds(2 * BLK, BLK)], att]
        d1 = []
        for k, (j, target) in enumerate(((2, far), (1, up), (3, down))):
            jobs = [((0, 1), j + 4 * i, lambda a, b, i=i: product(d_s1.at[2 * k + i], [a, b], tail)) for i in range(2)]
            lefts.run(jobs, after=((0, 1), (1, 3)[k]) if k < 2 else ((0,), 2))
            d1.append(remote(d_s1.at[pl.ds(2 * k, 2)], d_r1.at[pl.ds(2 * k, 2)], target))

        for copy in w_loads[:2]:
            copy.wait()
        row_products(other, att, active, w1v, 3 * BLK, w3v, theirs)
        br_core = remote(theirs, br_c, mate)
        row_products(core, att, active, w1v, 3 * BLK, w3v, br_m)

        br_core.wait_recv()
        add_rows(br_m, br_c)
        br1 = to_z(br_m, br_z)


        def local_grads(pair, more):
            lanes = slice(pair * 128, pair * 128 + 128)
            k = turn_back(dk[own_keys, lanes], cos[...], sin[...])
            v = dv[own_keys, lanes]
            if more:
                k = k + dkv[pair, :, :128].astype(F32)
                v = v + dkv[pair, :, 128:].astype(F32)
            raw[:, lanes] = k.astype(BF16)
            raw[:, BLK + pair * 128 : BLK + pair * 128 + 128] = v.astype(BF16)

        for pair, copy in enumerate(pairs_back):

            @pl.when(x_hi == 1)
            def _():
                local_grads(pair, False)
                copy.wait_send()

            @pl.when(x_hi == 0)
            def _():
                copy.wait_recv()
                local_grads(pair, True)

        br_core.wait_send()
        copies.sent = [copy for copy in copies.sent if copy is not br_core]
        w_loads[2].wait()
        row_products(other, raw, hidden, w1v, 0, w2v, theirs, unit, ub, sems, vec_t)
        ng_core = remote(theirs, ng_c, mate)

        row_products(core, raw, hidden, w1v, 0, w2v, ng_m, unit, ub, sems, vec_m)
        br2 = pass_on(br_m, br_z, br1, turned.at[0])
        ng_core.wait_recv()
        add_rows(ng_m, ng_c)
        ng1 = to_z(ng_m, ng_z)

        va[...] = jnp.zeros_like(va)
        for j in range(8):
            va[j, 0:2, :] = vec_t[j, 0:2, :] + vec_m[j, 0:2, :]
        va_sent = [remote(va, va_r.at[k], along[k]) for k in range(3)]

        for copy in passed:
            copy.wait_send()
        copies.sent = [copy for copy in copies.sent if all(copy is not old for old in passed)]
        pairs = raw.at[:, pl.ds(0, 512)]
        c1 = []
        for k, (j, target) in enumerate(((2, far), (1, up), (3, down))):
            jobs = [((0,), j + 4 * i, lambda l, i=i: product(c_s1.at[2 * k + i], [l], [pairs])) for i in range(2)]
            lefts.run(jobs, after=((0,), (1, 3)[k]) if k < 2 else ((0,), 4))
            c1.append(remote(c_s1.at[pl.ds(2 * k, 2)], c_r1.at[pl.ds(2 * k, 2)], target))

        arrived(b1 + passed)
        s = staged([b_r1.at[1], b_r1.at[3]])
        lefts.run([((0,), 4, lambda l: product(b_s2, [l], [hidden], s))], after=((1,), 0))
        for copy in b2:
            copy.start()
        arrived(a_y)
        s = staged([a_r1.at[0], a_r2.at[0], a_r2.at[1], a_r2.at[2]])
        lefts.run([((1,), 0, lambda l: product(a_m, [l], [active], s))], after=((0, 1), 4))
        a3 = remote(a_m, a_x, over)

        arrived(br2)
        tile = 32

        def share(total, got, i, j):
            at = pl.ds(pl.multiple_of(i * tile, tile), tile)
            from_all = pl.ds(pl.multiple_of(z * 128 + i * tile, tile), tile)
            cols = slice(j * BLK, (j + 1) * BLK)
            return total[from_all, cols].astype(F32) + (got[1, at, cols].astype(F32) + got[2, at, cols].astype(F32))

        def line(row, j):
            return jnp.concatenate([small[j, row : row + 1, :], small[j, row + 1 : row + 2, :]], axis=1)

        def spot(j):
            return pl.ds(pl.multiple_of(block_order(y, x_lo, j) * BLK, BLK), BLK)

        @pl.loop(0, 128 // tile)
        def _(i):
            at = pl.ds(pl.multiple_of(i * tile, tile), tile)
            for j in range(8):
                value = tok[at, spot(j)].astype(F32) + share(br_m, br_z, i, j) + line(4, j)
                br_o[at, spot(j)] = value.astype(BF16)

        ng2 = pass_on(ng_m, ng_z, ng1, turned.at[1])

        br3 = from_z(br_o, layer_out)
        arrived(d1)
        s = staged([d_r1.at[1], d_r1.at[3], d_r1.at[5]])
        lefts.run([((0, 1), 4, lambda a, b: product(d_s2, [a, b], tail, s))], after=((0,), 0))
        d2 = [remote(d_s2.at[upper], d_r2.at[upper], right), remote(d_s2.at[lower], d_r2.at[lower], left)]

        arrived(b2)
        s = staged([b_r1.at[0], b_r1.at[2], b_r2])
        lefts.run([((0,), 0, lambda l: product(b_m, [l], [hidden], s))], after=((0, 1), 0))
        b3 = remote(b_m, b_x, over)

        arrived(ng2)

        @pl.loop(0, 128 // tile)
        def _(i):
            at = pl.ds(pl.multiple_of(i * tile, tile), tile)
            rows = tok[at, :].astype(F32)
            mean = jnp.mean(rows, axis=-1, keepdims=True)
            centered = rows - mean
            inv = lax.rsqrt(jnp.mean(centered * centered, axis=-1, keepdims=True) + EPSILON)

            def terms(j):
                u = (tok[at, spot(j)].astype(F32) - mean) * inv
                return u, share(ng_m, ng_z, i, j) * line(0, j)

            first = second = jnp.zeros((tile, 1), F32)
            for j in range(8):
                u, g = terms(j)
                first += jnp.sum(g, axis=-1, keepdims=True)
                second += jnp.sum(g * u, axis=-1, keepdims=True)
            first, second = first / D, second / D
            for j in range(8):
                u, g = terms(j)
                ng_o[at, spot(j)] = (grad[at, spot(j)].astype(F32) + inv * (g - first - u * second)).astype(BF16)

        ng3 = from_z(ng_o, input_grad)
        for copy in va_sent:
            copy.wait_recv()
        vec_v[0] = (va[...] + va_r[1]) + (va_r[0] + va_r[2])
        vb = remote(vec_v.at[0], vb_r, mate)

        arrived(d2)
        s = staged([d_r1.at[0], d_r1.at[2], d_r1.at[4]]) + [d_r2]
        lefts.run([((0, 1), 0, lambda a, b: product(d_m, [a, b], tail, s))], after=((0,), 4))
        d3 = remote(d_m, d_x, over)

        vb.wait_recv()
        units[...] = jnp.zeros_like(units)
        units[0:3, :] = jnp.sum(raw[...].astype(F32), axis=0, keepdims=True).reshape(3, BLK)
        for j in range(4):
            units[3 + j : 4 + j, :] = up_bias_v[:, j * BLK : (j + 1) * BLK]
        for j in range(8):
            dy, dx = j % 4, j // 4
            my[dy, dx] = vec_v[0, j] + vb_r[j]
            my[dy, dx, 2:3, :] = bias_v[:, j * BLK : (j + 1) * BLK]
        for dy in range(4):
            my[dy, 2] = units[...]
        my_sent = [remote(my.at[1], my_r.at[0], up), remote(my.at[2], my_r.at[1], far), remote(my.at[3], my_r.at[2], down)]

        arrived(c1)
        s = staged([c_r1.at[1], c_r1.at[3], c_r1.at[5]])
        lefts.run([((0,), 4, lambda l: product(c_s2, [l], [pairs], s))], after=((0,), 0))
        c2 = [remote(c_s2.at[upper], c_r2.at[upper], right), remote(c_s2.at[lower], c_r2.at[lower], left)]

        br_own, br4 = pass_rows(br3, layer_out)

        a4 = settle(a_m, a_x, a3, piece3, pl.ds(0, 1024), True)
        b4 = settle(b_m, b_x, b3, piece2, pl.ds(0, 1024), True)
        arrived(c2)
        s = staged([c_r1.at[0], c_r1.at[2], c_r1.at[4]]) + [c_r2]
        lefts.run([((0,), 0, lambda l: product(c_m, [l], [pairs], s))])
        c3 = remote(c_m, c_x, over)

        d4 = settle(d_m, d_x, d3, piece1, pl.ds(512, 512), False)

        arrived(my_sent)
        here_sum = (my[0] + my_r[1]) + (my_r[0] + my_r[2])
        mx[0, 0] = here_sum[0]
        mx[0, 1] = here_sum[2]
        mx[1, 0] = here_sum[1]
        mx[1, 1] = here_sum[2]
        mx_sent = [remote(mx.at[1], mx_r.at[0], right), remote(mx.at[0], mx_r.at[1], over), remote(mx.at[1], mx_r.at[2], left)]
        ng_own, ng4 = pass_rows(ng3, input_grad)
        arrived(mx_sent)
        last[...] = (mx[0] + mx_r[1]) + (mx_r[0] + mx_r[2])
        vec_copy = remote(last.at[1], last_r, mate)
        c4 = settle(c_m, c_x, c3, piece1, pl.ds(0, 512), False)
        vec_copy.wait_recv()
        last_saved = [here(last, vec_out.at[pl.ds(0, 2)]), here(last_r, vec_out.at[2])]

        for own, copy in (a4, b4, c4, d4):
            own.wait()
            copy.wait_recv()
        br_own.wait()
        ng_own.wait()
        arrived(br4 + ng4)
        for copy in last_saved:
            copy.wait()
        for copy in copies.sent:
            copy.wait_send()

    pl.run_scoped(
        finish,
        pltpu.VMEM((D, 1024), BF16),
        pltpu.VMEM((D, 1024), BF16),
        pltpu.VMEM((D, 1024), BF16),
    )


def reduce_call(*args):
    low = lambda *shape: jax.ShapeDtypeStruct(shape, BF16)
    wide = lambda *shape: jax.ShapeDtypeStruct(shape, F32)
    vlow = lambda *shape: pltpu.VMEM(shape, BF16)
    vwide = lambda *shape: pltpu.VMEM(shape, F32)
    anywhere = pl.BlockSpec(memory_space=pl.ANY)
    n = 1024
    outs = [low(HALF, D), low(HALF, D), low(2, BLK, n), low(2, BLK, n), low(2, BLK, n), wide(3, 8, BLK)] + [
        low(4, BLK, n), low(3, BLK, n), low(BLK, n), low(4, BLK, 512), low(4, BLK, n), low(BLK, n), low(BLK, n),
        low(6, BLK, 512), low(6, BLK, 512),
    ]
    result = pl.pallas_call(
        reduce_kernel,
        in_specs=[anywhere] * 20,
        out_specs=[anywhere] * len(outs),
        out_shape=outs,
        scratch_shapes=[
            vlow(ROWS, BLK), vlow(ROWS, BLK), vlow(ROWS, n), vlow(ROWS, n), vlow(ROWS, BLK), vlow(ROWS, 3 * BLK),
            vwide(8, PACK, 128), vwide(ROWS, 128), vwide(ROWS, 128), vwide(ROWS, 128), vwide(ROWS, 128), vwide(192, 128),
            vwide(2 * ROWS, BLK), vwide(2 * ROWS, BLK), vwide(128, ROWS), vwide(128, ROWS), vlow(2, ROWS, BLK),
            vlow(2, HALF, HALF), vlow(HALF, D), vlow(HALF, D), vlow(HALF, D), vlow(3, 128, D), vlow(128, D),
            vlow(HALF, D), vlow(HALF, D), vlow(3, 128, D), vlow(128, D), vlow(2, 2, 64, D), vlow(128, D), vlow(128, D),
            vlow(2, 2, BLK, ROWS), vlow(4, BLK, n), vlow(3, BLK, n), vlow(BLK, n), vlow(BLK, n), vlow(BLK, n),
            vlow(6, BLK, 512), vlow(BLK, 512), vlow(BLK, 512), vlow(6, BLK, 512), vlow(BLK, 512), vlow(BLK, 512),
            vlow(BLK, 512), vlow(BLK, 512), vlow(BLK, 512), vlow(BLK, 512), vwide(8, 8, BLK), vwide(8, 8, BLK),
            vwide(8, 8, BLK), vwide(3, 8, 8, BLK), vwide(8, 8, BLK), vwide(8, BLK), vwide(4, 3, 8, BLK),
            vwide(3, 3, 8, BLK), vwide(2, 2, 8, BLK), vwide(3, 2, 8, BLK), vwide(2, 8, BLK), vwide(8, BLK),
            vwide(1, D), vwide(1, n), vwide(1, 8, 8, BLK),
            pltpu.SemaphoreType.DMA((72,)),
            pltpu.SemaphoreType.DMA((72,)),
            pltpu.SemaphoreType.DMA((32,)),
            pltpu.SemaphoreType.DMA((2,)),
            pltpu.SemaphoreType.DMA((2, 2)),
            pltpu.SemaphoreType.DMA((4,)),
        ],
        compiler_params=params(collective_id=1, has_side_effects=True),
        cost_estimate=cost(2 * ROWS * D * 5 * 1024, 128 * 1024 * 1024),
        name="reduce_phase",
    )(*args)
    return result[:6]


def body(tokens, ln_gain, ln_shift, out_bias, w_qkv, b_qkv, w_out, w_fc1, b_fc1, w_fc2, out_grad):
    f, c = lax.axis_index("fsdp"), lax.axis_index("ctx")
    x_hi, core = c // 2, c % 2
    tokens, out_grad = tokens[0], out_grad[0]

    own = (jnp.arange(HD) // 8 == f)[None, None, :]
    spread = lambda v: jnp.where(own, jnp.tile(v, (1, 1, 8)), jnp.zeros((), BF16)).reshape(-1)
    pack = jnp.concatenate(
        [
            ln_gain,
            ln_shift,
            out_bias,
            spread(jnp.roll(lax.dynamic_slice_in_dim(b_qkv, core * 4, 4, axis=1), -1, axis=0)),
            spread(lax.dynamic_slice_in_dim(b_fc1, core * 16, 16, axis=0)[None]),
            jnp.zeros((512,), BF16),
        ]
    )
    pack = pack.astype(F32).reshape(PACK, 128)

    (w_attn, w_up, w_down, normed_t, grad_t, unit, q, kv, kvr, do, active, hidden_grad, small, bias_grad, up_bias_grad,
     a_first, b_first) = (
        gather_call(w_qkv.transpose(1, 0, 2), w_out, w_fc1, w_fc2, tokens, out_grad, pack, ROPE)
    )
    layer_out, input_grad, attn_all, up_all, down_all, vec = reduce_call(
        w_attn, w_up, w_down, normed_t, grad_t, unit, q, kv, kvr, do, active, hidden_grad, small, bias_grad, up_bias_grad,
        a_first, b_first, tokens, out_grad, ROPE
    )
    qkv_out, proj_out, up_out, down_out, layer_out, input_grad = grads_call(
        attn_all, up_all, down_all, layer_out, input_grad
    )
    gain_grad, shift_grad, out_bias_grad = vec[0, 0], vec[0, 1], vec[0, 2]
    units = jnp.where(core == 0, vec[1:], vec[:0:-1]).reshape(2, 8 * BLK)
    qkv_bias_out = lax.dynamic_slice_in_dim(
        jnp.roll(units[:, : 3 * BLK].reshape(2, 3, 4, HD), 1, axis=1).transpose(1, 0, 2, 3).reshape(3, 8, HD), f * 8, 8, axis=2
    )
    up_bias_out = lax.dynamic_slice_in_dim(units[:, 3 * BLK : 7 * BLK].reshape(32, HD), f * 8, 8, axis=1)
    return (
        layer_out[None],
        input_grad[None],
        gain_grad,
        shift_grad,
        out_bias_grad,
        qkv_out.transpose(1, 0, 2),
        qkv_bias_out,
        proj_out,
        up_out,
        up_bias_out,
        down_out,
    )


def solution(mesh):
    in_specs = (
        P("fsdp", "ctx", None),
        P("fsdp"),
        P("fsdp"),
        P("fsdp"),
        P("fsdp", None, "tp"),
        P(None, "tp", "fsdp"),
        P("tp", "fsdp"),
        P("fsdp", "tp"),
        P("tp", "fsdp"),
        P("tp", "fsdp"),
        P("fsdp", "ctx", None),
    )
    out_specs = (
        P("fsdp", "ctx", None),
        P("fsdp", "ctx", None),
        P("fsdp"),
        P("fsdp"),
        P("fsdp"),
        P("fsdp", None, "tp"),
        P(None, "tp", "fsdp"),
        P("tp", "fsdp"),
        P("fsdp", "tp"),
        P("tp", "fsdp"),
        P("tp", "fsdp"),
    )
    return jax.shard_map(body, mesh=mesh, in_specs=in_specs, out_specs=out_specs, check_vma=False)
```

```python
import math

import jax
import jax.numpy as jnp
import numpy as np
from jax import lax
from jax.experimental import pallas as pl
from jax.experimental.pallas import tpu as pltpu
from jax.sharding import PartitionSpec as P

D = 2048
HD = 64
ROT = 32
BLK = 256
ROWS = 1024
HALF = 512
EPSILON = 1e-05
MASKED = -1e30
F32 = jnp.float32
BF16 = jnp.bfloat16
VMEM_LIMIT = 62 * 1024 * 1024


def params(**kw):
    return pltpu.CompilerParams(vmem_limit_bytes=VMEM_LIMIT, **kw)


def whole():
    return pl.BlockSpec(memory_space=pltpu.VMEM)


def cost(flops, nbytes, trans=0):
    return pl.CostEstimate(flops=int(flops), bytes_accessed=int(nbytes), transcendentals=int(trans))


def block_order(y, x_lo, j):
    dx, dy = j // 4, j % 4
    return lax.rem(y + dy, 4) * 2 + lax.rem(x_lo + dx, 2)


def partner(v):
    lane = lax.broadcasted_iota(jnp.int32, v.shape, 1)
    up = pltpu.roll(v, v.shape[1] - ROT // 2, 1)
    down = pltpu.roll(v, ROT // 2, 1)
    return jnp.where(lane % HD < ROT // 2, up, down)


QT = 256
KC = 512


def rope_table():
    lane = np.arange(128) % HD
    freq = np.where(lane < ROT, 10000.0 ** (-2.0 * (lane % (ROT // 2)) / ROT), 0.0)
    sign = np.where(lane < ROT // 2, -1.0, 1.0)
    coarse, fine = np.arange(64)[:, None] * 32 * freq, np.arange(32)[:, None] * freq
    parts = [np.cos(coarse), np.sin(coarse) * sign, np.cos(fine), np.sin(fine) * sign]
    return np.concatenate(parts).astype(np.float32)


ROPE = rope_table()
GELU_C = math.sqrt(2.0 / math.pi)


MESH = pl.DeviceIdType.MESH
PACK = 24


def coords():
    f, c, z = lax.axis_index("fsdp"), lax.axis_index("ctx"), lax.axis_index("tp")
    return (c // 2) * 2 + f % 2, f // 2, z, c % 2


def device(x, y, z, core):
    return (y * 2 + lax.rem(x, 2), (x // 2) * 2 + core, z)


def beside(dx=0, dy=0, flip=0, dz=0):
    x, y, z, core = coords()
    return device(
        lax.rem(x + dx + 4, 4), lax.rem(y + dy + 4, 4), lax.rem(z + dz + 4, 4), (1 - core) if flip else core
    )


def greet(targets):
    barrier = pltpu.get_barrier_semaphore()
    for target in targets:
        pl.semaphore_signal(barrier, inc=1, device_id=target, device_id_type=MESH)
    pl.semaphore_wait(barrier, len(targets))


class Copies:
    def __init__(self, send, recv, local):
        self.send, self.recv, self.local = send, recv, local
        self.remotes = self.locals = 0
        self.sent = []

    def make(self, src, dst, target):
        i = self.remotes
        self.remotes += 1
        return pltpu.make_async_remote_copy(
            src, dst, self.send.at[i], self.recv.at[i], device_id=target, device_id_type=MESH
        )

    def remote(self, src, dst, target):
        copy = self.make(src, dst, target)
        copy.start()
        self.sent.append(copy)
        return copy

    def here(self, src, dst):
        copy = pltpu.make_async_copy(src, dst, self.local.at[self.locals])
        self.locals += 1
        copy.start()
        return copy


def rope_rows(table, first, cos, sin, count):
    @pl.loop(0, count // 32)
    def _(i):
        at = pl.ds(pl.multiple_of(i * 32, 32), 32)
        ch, sh = table[pl.ds(first // 32 + i, 1), :], table[pl.ds(64 + first // 32 + i, 1), :]
        cl, sl = table[128:160, :], table[160:192, :]
        cos[at, :] = ch * cl - sh * sl
        sin[at, :] = sh * cl + ch * sl


def turn(v, c, s):
    return v * c + partner(v) * s


def gather_kernel(s1_in, proj_in, up_in, down_in, tok_in, grad_in, pack, table_in,
                  w1_out, w2_out, w3_out, normed_t_out, grad_t_out, unit_out, q_out, kv_out, kvr_out, do_out,
                  active_out, hidden_out, small_out, bias_out, up_bias_out, a_s1_out, b_s1_out,
                  w1, w2, w3, tok, grad, normed, grad_rel, normed_t, grad_t, unit, small, q, kv, do, active, slope,
                  hidden, cos, sin, table, bias_sum, up_bias_sum, proj_v, down_v, send, recv, local):
    x, y, z, core = coords()
    x_lo, x_hi = lax.rem(x, 2), x // 2
    up, down, far = beside(dy=1), beside(dy=3), beside(dy=2)
    right, left, over, mate = beside(dx=1), beside(dx=3), beside(dx=2), beside(flip=1)
    copies = Copies(send, recv, local)
    here, remote = copies.here, copies.remote
    hcols = pl.ds(pl.multiple_of(core * 1024, 1024), 1024)
    hrows = pl.ds(pl.multiple_of(core * 1024, 1024), 1024)
    prows = pl.ds(pl.multiple_of(core * BLK, BLK), BLK)
    own_block = pl.ds(0, BLK)
    proj_load = here(proj_in.at[prows], proj_v)
    down_load = here(down_in.at[hrows], down_v)
    s1_loads = [
        here(s1_in.at[c, :, prows], w1.at[own_block, pl.ds(k * BLK, BLK)]) for k, c in enumerate((1, 2, 0))
    ]
    up_load = here(up_in.at[:, hcols], w2.at[own_block])
    greet([up, down, far, right, left, over, mate])

    class Part:
        def __init__(self, w, at, n):
            self.w, self.cols, self.moves = w, pl.ds(at, n), []

        def rows(self, j, first=0, count=BLK):
            return self.w.at[pl.ds(j * BLK + first, count), self.cols]

        def to(self, j, k, target, first=0, count=BLK):
            copy = remote(self.rows(j, first, count), self.rows(k, first, count), target)
            self.moves.append(copy)
            return copy

        def along_y(self, base):
            return [self.to(base, base + 3, up), self.to(base, base + 1, down), self.to(base, base + 2, far)]

        def sideways(self):
            return [self.to(0, 4, right, 0, BLK // 2), self.to(0, 4, left, BLK // 2, BLK // 2)]

        def begin_x(self):
            self.x = self.sideways()

        def begin_y(self):
            self.y = self.along_y(0)

        def forward(self):
            for copy in self.y:
                copy.wait_recv()
            self.x += [
                self.to(1, 5, right), self.to(3, 7, left),
                self.to(2, 6, right, 0, BLK // 2), self.to(2, 6, left, BLK // 2, BLK // 2),
            ]

        def forward_y(self):
            for copy in self.x:
                copy.wait_recv()
            self.x = self.along_y(4)

        def arrived(self):
            for copy in self.x:
                copy.wait_recv()

        def all_arrived(self):
            for copy in self.y + self.x:
                copy.wait_recv()

    keys_part, query_part, proj_part = Part(w1, 0, 512), Part(w1, 512, BLK), Part(w1, 768, BLK)
    up_part = Part(w2, 0, 1024)
    down_a, down_b = Part(w3, 0, 512), Part(w3, 512, 512)

    my_rows = pl.ds(pl.multiple_of(core * HALF, HALF), HALF)
    pack_y = [remote(pack, small.at[3], up), remote(pack, small.at[1], down), remote(pack, small.at[2], far)]
    pack_own = here(pack, small.at[0])
    tok_copy = remote(tok_in, tok.at[my_rows], mate)
    grad_copy = remote(grad_in, grad.at[my_rows], mate)
    for copy in s1_loads:
        copy.wait()
    keys_part.begin_y()
    keys_part.begin_x()
    mine = [here(tok_in, tok.at[my_rows]), here(grad_in, grad.at[my_rows])]
    table_load = here(table_in, table)

    proj_load.wait()
    w1[0:BLK, 3 * BLK :] = proj_v[...].astype(F32).T.astype(BF16)
    down_load.wait()
    for k in range(4):
        w3[0:BLK, k * BLK : (k + 1) * BLK] = down_v[k * BLK : (k + 1) * BLK, :].astype(F32).T.astype(BF16)
    for copy in pack_y:
        copy.wait_recv()
    pack_own.wait()
    pack_x = remote(small.at[pl.ds(0, 4)], small.at[pl.ds(4, 4)], right)
    up_load.wait()
    up_part.begin_x()
    down_b.begin_x()
    proj_part.begin_x()
    table_load.wait()
    rope_rows(table, x_hi * ROWS, cos, sin, ROWS)
    up_part.begin_y()
    down_b.begin_y()
    keys_part.forward()
    down_b.forward_y()
    down_a.begin_y()
    proj_part.begin_y()
    query_part.begin_y()
    for copy in mine:
        copy.wait()
    tok_copy.wait_recv()
    grad_copy.wait_recv()
    pack_x.wait_recv()

    bias_sum[...] = jnp.zeros_like(bias_sum)
    up_bias_sum[...] = jnp.zeros_like(up_bias_sum)
    tile = 128

    def prepare(first, last):
        @pl.loop(first, last)
        def _(i):
            at = pl.ds(pl.multiple_of(i * tile, tile), tile)
            rows = tok[at, :].astype(F32)
            mean = jnp.mean(rows, axis=-1, keepdims=True)
            centered = rows - mean
            inv = lax.rsqrt(jnp.mean(centered * centered, axis=-1, keepdims=True) + EPSILON)
            for j in range(8):
                src = pl.ds(pl.multiple_of(block_order(y, x_lo, j) * BLK, BLK), BLK)
                dst = pl.ds(j * BLK, BLK)
                gain = jnp.concatenate([small[j, 0:1, :], small[j, 1:2, :]], axis=1)
                shift = jnp.concatenate([small[j, 2:3, :], small[j, 3:4, :]], axis=1)
                u = (tok[at, src].astype(F32) - mean) * inv
                n = u * gain + shift
                normed[at, dst] = n.astype(BF16)
                normed_t[dst, at] = n.T.astype(BF16)
                unit[at, dst] = u.astype(BF16)
                g = grad[at, src]
                g32 = g.astype(F32)
                grad_rel[at, dst] = g
                grad_t[dst, at] = g32.T.astype(BF16)
                bias_sum[:, dst] += jnp.sum(g32, axis=0, keepdims=True)

    prepare(0, 8)
    saved = [here(normed_t, normed_t_out), here(grad_t, grad_t_out), here(unit, unit_out), here(small, small_out),
             here(bias_sum, bias_out)]

    biases = small[0, 6:20, :]
    for j in range(1, 8):
        biases = biases + small[j, 6:20, :]
    qkv_bias = jnp.concatenate([biases[j : j + 1] for j in range(6)], axis=1)
    up_bias = jnp.concatenate([biases[j : j + 1] for j in range(6, 14)], axis=1)
    big = 256
    keys_part.arrived()

    @pl.loop(0, ROWS // big)
    def _(i):
        at = pl.ds(pl.multiple_of(i * big, big), big)
        raw = jnp.dot(normed[at, :], w1[:, : 2 * BLK], preferred_element_type=F32) + qkv_bias[:, : 2 * BLK]
        c, s = cos[at, :], sin[at, :]
        for k in range(2):
            lanes = slice(k * 128, (k + 1) * 128)
            kv[at, lanes] = turn(raw[:, lanes], c, s).astype(BF16)
        kv[at, BLK:] = raw[:, BLK:].astype(BF16)

    kv_copy = copies.make(kv, kvr_out, over)

    @pl.when(x_hi == 0)
    def _():
        kv_copy.start()

    saved.append(here(kv, kv_out))
    up_part.forward()
    proj_part.forward_y()
    query_part.begin_x()
    down_a.begin_x()
    up_part.arrived()
    saved.append(here(w2, w2_out))

    @pl.loop(0, ROWS // big)
    def _(i):
        at = pl.ds(pl.multiple_of(i * big, big), big)
        v = jnp.dot(normed[at, :], w2[...], preferred_element_type=F32) + up_bias
        sq = v * v
        t = jnp.tanh(GELU_C * v * (1.0 + 0.044715 * sq))
        half = 0.5 * (1.0 + t)
        active[at, :] = (v * half).astype(BF16)
        slope[at, :] = (half + 0.5 * v * (1.0 - t * t) * (GELU_C * (1.0 + 3 * 0.044715 * sq))).astype(BF16)

    saved.append(here(active, active_out))
    down_a.forward()

    place = [buf.at[:, pl.ds(k * 1024, 1024)] for buf in (tok, grad) for k in range(2)]

    def partials(left, right, blocks, dst, out):
        for k, j in enumerate(blocks):
            at = pl.ds((k % 4) * BLK, BLK)
            dst[k // 4][at, :] = jnp.dot(left[j * BLK : (j + 1) * BLK, :], right[...], preferred_element_type=F32).astype(BF16)
            saved.append(here(dst[k // 4].at[at], out.at[k]))

    partials(grad_t, active, (4, 5, 6, 7), place[:1], a_s1_out)
    query_part.forward()
    down_a.arrived()
    down_b.all_arrived()
    saved.append(here(w3, w3_out))

    @pl.loop(0, ROWS // big)
    def _(i):
        at = pl.ds(pl.multiple_of(i * big, big), big)
        v = jnp.dot(grad_rel[at, :], w3[...], preferred_element_type=F32) * slope[at, :].astype(F32)
        low = v.astype(BF16)
        hidden[at, :] = low
        up_bias_sum[...] += jnp.sum(low.astype(F32), axis=0, keepdims=True)

    saved += [here(hidden, hidden_out), here(up_bias_sum, up_bias_out)]
    partials(normed_t, hidden, (2, 6, 1, 5, 3, 7), place[1:3], b_s1_out)
    query_part.arrived()
    proj_part.all_arrived()
    saved.append(here(w1, w1_out))

    @pl.loop(0, ROWS // big)
    def _(i):
        at = pl.ds(pl.multiple_of(i * big, big), big)
        raw = jnp.dot(normed[at, :], w1[:, 2 * BLK : 3 * BLK], preferred_element_type=F32) + qkv_bias[:, 2 * BLK :]
        c, s = cos[at, :], sin[at, :]
        for k in range(2):
            lanes = slice(k * 128, (k + 1) * 128)
            q[at, lanes] = (turn(raw[:, lanes], c, s).astype(BF16).astype(F32) * (HD**-0.5)).astype(BF16)
        do[at, :] = jnp.dot(grad_rel[at, :], w1[:, 3 * BLK :], preferred_element_type=F32).astype(BF16)

    saved += [here(q, q_out), here(do, do_out)]
    for copy in copies.sent:
        copy.wait_send()

    @pl.when(x_hi == 0)
    def _():
        kv_copy.wait_send()

    @pl.when(x_hi == 1)
    def _():
        kv_copy.wait_recv()

    for copy in saved:
        copy.wait()


def gather_call(*args):
    n = 1024
    low = lambda *shape: jax.ShapeDtypeStruct(shape, BF16)
    wide = lambda *shape: jax.ShapeDtypeStruct(shape, F32)
    vlow = lambda *shape: pltpu.VMEM(shape, BF16)
    vwide = lambda *shape: pltpu.VMEM(shape, F32)
    anywhere = pl.BlockSpec(memory_space=pl.ANY)
    return pl.pallas_call(
        gather_kernel,
        in_specs=[anywhere] * 8,
        out_specs=[anywhere] * 17,
        out_shape=[
            low(D, n), low(D, n), low(D, n), low(D, ROWS), low(D, ROWS), low(ROWS, D), low(ROWS, BLK), low(ROWS, 2 * BLK),
            low(ROWS, 2 * BLK), low(ROWS, BLK), low(ROWS, n), low(ROWS, n), wide(8, PACK, 128), wide(1, D), wide(1, n),
            low(4, BLK, n), low(6, BLK, n),
        ],
        scratch_shapes=[
            vlow(D, n), vlow(D, n), vlow(D, n), vlow(ROWS, D), vlow(ROWS, D), vlow(ROWS, D), vlow(ROWS, D), vlow(D, ROWS),
            vlow(D, ROWS), vlow(ROWS, D), vwide(8, PACK, 128), vlow(ROWS, BLK), vlow(ROWS, 2 * BLK), vlow(ROWS, BLK),
            vlow(ROWS, n), vlow(ROWS, n), vlow(ROWS, n), vwide(ROWS, 128), vwide(ROWS, 128), vwide(192, 128), vwide(1, D),
            vwide(1, n), vlow(BLK, BLK), vlow(n, BLK),
            pltpu.SemaphoreType.DMA((64,)),
            pltpu.SemaphoreType.DMA((64,)),
            pltpu.SemaphoreType.DMA((40,)),
        ],
        compiler_params=params(collective_id=0, has_side_effects=True),
        cost_estimate=cost(2 * ROWS * D * 3 * n, 64 * 1024 * 1024),
        name="gather_phase",
    )(*args)


def grads_kernel(attn, up, down, rows_a, rows_b, qkv_out, proj_out, up_out, down_out, rows_a_out, rows_b_out):
    rows_a_out[...] = rows_a[...]
    rows_b_out[...] = rows_b[...]
    for core in range(2):
        for k, c in enumerate((1, 2, 0)):
            qkv_out[c, :, core * BLK : (core + 1) * BLK] = attn[core, :, k * BLK : (k + 1) * BLK].astype(F32)
        proj_out[core * BLK : (core + 1) * BLK, :] = attn[core, :, 3 * BLK :].astype(F32).T
        up_out[:, core * 1024 : (core + 1) * 1024] = up[core].astype(F32)
        down_out[core * 1024 : (core + 1) * 1024, :] = down[core].astype(F32).T


def grads_call(attn, up, down, rows_a, rows_b):
    tile = 128
    piece = pl.BlockSpec((2, tile, 1024), lambda i: (0, i, 0))
    rows = pl.BlockSpec((HALF * tile // BLK, D), lambda i: (i, 0))
    wide = lambda *shape: jax.ShapeDtypeStruct(shape, F32)
    return pl.pallas_call(
        grads_kernel,
        grid=(BLK // tile,),
        in_specs=[piece] * 3 + [rows] * 2,
        out_specs=[
            pl.BlockSpec((3, tile, HALF), lambda i: (0, i, 0)),
            pl.BlockSpec((HALF, tile), lambda i: (0, i)),
            pl.BlockSpec((tile, 2048), lambda i: (i, 0)),
            pl.BlockSpec((2048, tile), lambda i: (0, i)),
            rows,
            rows,
        ],
        out_shape=[wide(3, BLK, HALF), wide(HALF, BLK), wide(BLK, 2048), wide(2048, BLK)]
        + [jax.ShapeDtypeStruct((HALF, D), BF16)] * 2,
        compiler_params=params(),
        cost_estimate=cost(0, 10 * 1024 * 1024),
        name="gradients",
    )(attn, up, down, rows_a, rows_b)


class Lefts:
    def __init__(self, sources, buf, sems):
        self.sources, self.buf, self.sems = sources, buf, sems
        self.queue, self.count = ([], []), [0, 0]

    def want(self, kind, j):
        if any(held == j for held, _ in self.queue[kind]):
            return
        slot = self.count[kind] % 2
        self.count[kind] += 1
        self.move(kind, j, slot).start()
        self.queue[kind].append((j, slot))

    def take(self, kind, j):
        held, slot = self.queue[kind].pop(0)
        assert held == j
        self.move(kind, j, slot).wait()
        return self.buf.at[kind, slot]

    def move(self, kind, j, slot):
        return pltpu.make_async_copy(
            self.sources[kind].at[pl.ds(j * BLK, BLK)], self.buf.at[kind, slot], self.sems.at[kind, slot]
        )

    def run(self, jobs, after=()):
        for i, (kinds, j, act) in enumerate(jobs):
            for kind in kinds:
                self.want(kind, j)
            ahead = jobs[i + 1][:2] if i + 1 < len(jobs) else after
            if ahead:
                for kind in ahead[0]:
                    self.want(kind, ahead[1])
            act(*[self.take(kind, j) for kind in kinds])


def product(dst, lefts, rights, adds=()):
    at = 0
    for left, right in zip(lefts, rights):
        cols = slice(at, at + right.shape[1])
        total = jnp.dot(left[...], right[...], preferred_element_type=F32)
        for add in adds:
            total += add[:, cols].astype(F32)
        dst[:, cols] = total.astype(BF16)
        at += right.shape[1]


def row_products(half, a, b, w1, col1, w2, out, unit=None, ub=None, sems=None, vec=None):
    nt = (((1,), (1,)), ((), ()))
    ka = a.shape[1]
    rows = pl.ds(pl.multiple_of(half * HALF, HALF), HALF)

    def fetch(j, slot):
        at = pl.ds(pl.multiple_of(j * HALF, HALF), HALF)
        return pltpu.make_async_copy(unit.at[rows, at], ub.at[slot], sems.at[slot])

    if unit is not None:
        fetch(0, 0).start()

    @pl.loop(0, D // HALF)
    def _(j):
        at = pl.ds(pl.multiple_of(j * HALF, HALF), HALF)
        slot = lax.rem(j, 2)
        if unit is not None:
            fetch(j, slot).wait()

            @pl.when(j < D // HALF - 1)
            def _():
                fetch(j + 1, 1 - slot).start()

        total = lax.dot_general(a[rows, :], w1[at, col1 : col1 + ka], nt, preferred_element_type=F32)
        total += lax.dot_general(b[rows, :], w2[at, :], nt, preferred_element_type=F32)
        out[:, at] = total.astype(BF16)
        if unit is not None:
            weighted = jnp.sum(total * ub[slot].astype(F32), axis=0, keepdims=True)
            plain = jnp.sum(total, axis=0, keepdims=True)
            for k in range(2):
                vec[2 * j + k, 0:1, :] = weighted[:, k * BLK : (k + 1) * BLK]
                vec[2 * j + k, 1:2, :] = plain[:, k * BLK : (k + 1) * BLK]


def add_rows(mine, got):
    @pl.loop(0, 4)
    def _(i):
        at = pl.ds(pl.multiple_of(i * 128, 128), 128)
        mine[at, :] = (mine[at, :].astype(F32) + got[at, :].astype(F32)).astype(BF16)


def reduce_kernel(w1, w2, w3, normed_t, grad_t, unit, q_in, kv_in, kvr_in, do_in, active_in, hidden_in, small_in, bias_in,
                  up_bias_in, a_s1, b_s1, tok_in, grad_in, table_in,
                  layer_out, input_grad, piece1, piece2, piece3, vec_out,
                  a_r1, a_r2, a_x, b_p, b_r1, b_r2, b_x, c_r1, d_r1,
                  q, do, active, hidden, att, raw, small, cos, sin, cos_r, sin_r, table,
                  dk, dv, out_t, dq_t, dkv, ub, theirs, br_m, br_c, br_z, br_o, ng_m, ng_c, ng_z, ng_o,
                  turned, tok, grad, left_buf, stage, a_s2, a_m, b_s2, b_m, c_s1, c_s2, c_m, d_s1, d_s2, d_m, c_r2, c_x, d_r2, d_x,
                  vec_t, vec_m, va, va_r, vb_r, units, my, my_r, mx, mx_r, last, last_r, bias_v, up_bias_v, vec_v,
                  send, recv, local, sems, left_sems, stage_sems):
    x, y, z, core = coords()
    x_lo, x_hi = lax.rem(x, 2), x // 2
    other = 1 - core
    up, down, far = beside(dy=1), beside(dy=3), beside(dy=2)
    right, left, over = beside(dx=1), beside(dx=3), beside(dx=2)
    mate = beside(flip=1)
    above, below = beside(dz=1), beside(dz=3)
    along = [above, beside(dz=2), below]
    copies = Copies(send, recv, local)
    here, remote = copies.here, copies.remote
    nt = (((1,), (1,)), ((), ()))

    load_active, load_hidden = here(active_in, active), here(hidden_in, hidden)
    own_keys = pl.ds(pl.multiple_of(x_hi * ROWS, ROWS), ROWS)
    loads = [here(table_in, table), here(q_in, q), here(do_in, do), here(small_in, small), here(bias_in, bias_v),
              here(up_bias_in, up_bias_v)]
    z_rows = pl.ds(pl.multiple_of(z * 128, 128), 128)
    loads += [here(tok_in.at[z_rows], tok), here(grad_in.at[z_rows], grad)]
    greet([up, down, far, right, left, over, mate] + along)
    lo, hi, first, second = pl.ds(0, 512), pl.ds(512, 512), pl.ds(0, 2), pl.ds(2, 2)
    bp = [remote(b_s1.at[first, :, lo], b_p.at[first], up), remote(b_s1.at[first, :, hi], b_p.at[second], down)]
    b1 = [
        remote(b_s1.at[second, :, hi], b_r1.at[first, :, hi], up),
        remote(b_s1.at[pl.ds(4, 2), :, lo], b_r1.at[second, :, lo], down),
    ]
    a1 = [remote(a_s1.at[pl.ds(2 * k, 2)], a_r1.at[pl.ds(2 * k, 2)], target) for k, target in enumerate((right, left))]

    lefts = Lefts((normed_t, grad_t), left_buf, left_sems)

    def staged(parts):
        views, found = [], []
        for k, part in enumerate(parts):
            view = stage.at[k, :, pl.ds(0, part.shape[-1])]
            copy = pltpu.make_async_copy(part, view, stage_sems.at[k])
            copy.start()
            found.append(copy)
            views.append(view)
        for copy in found:
            copy.wait()
        return views

    def arrived(moves):
        for copy in moves:
            copy.wait_recv()

    def settle(mine, got, move, piece, cols, on_hbm):
        move.wait_send()
        copies.sent = [copy for copy in copies.sent if copy is not move]
        move.wait_recv()
        more = staged([got])[0] if on_hbm else got
        mine[...] = (mine[...].astype(F32) + more[...].astype(F32)).astype(BF16)
        spot = piece.at[core, :, cols]
        return here(mine, spot), remote(mine, spot, mate)

    def turn_back(v, c, s):
        return v * c - partner(v) * s

    upper, lower = pl.ds(0, BLK // 2), pl.ds(BLK // 2, BLK // 2)
    pairs_back = [copies.make(dkv.at[k], dkv.at[k], over) for k in range(2)]
    passed = [
        copies.make(c_s1.at[first], b_r1.at[first, :, lo], up),
        copies.make(c_s1.at[second], b_r1.at[second, :, hi], down),
    ]
    a_y = [copies.make(a_s2.at[k], a_r2.at[k], target) for k, target in enumerate((far, down, up))]
    b2 = [copies.make(b_s2.at[upper], b_r2.at[upper], right), copies.make(b_s2.at[lower], b_r2.at[lower], left)]
    copies.sent += passed + a_y + b2

    def attend(keys, vals, keys_t, vals_t, st, dp, qm, dom):
        own = here(kv_in.at[:, pl.ds(0, BLK)], keys.at[own_keys]), here(kv_in.at[:, pl.ds(BLK, BLK)], vals.at[own_keys])
        far_keys = pltpu.make_async_copy(kvr_in.at[:, pl.ds(0, BLK)], keys.at[pl.ds(0, ROWS)], local.at[copies.locals])
        far_vals = pltpu.make_async_copy(kvr_in.at[:, pl.ds(BLK, BLK)], vals.at[pl.ds(0, ROWS)], local.at[copies.locals + 1])
        copies.locals += 2

        @pl.when(x_hi == 1)
        def _():
            far_keys.start()
            far_vals.start()
        for copy in loads + list(own):
            copy.wait()

        @pl.when(x_hi == 1)
        def _():
            far_keys.wait()
            far_vals.wait()

        @pl.loop(0, (x_hi + 1) * (ROWS // KC))
        def _(j):
            at = pl.ds(pl.multiple_of(j * KC, KC), KC)
            keys_t[:, at] = keys[at, :].astype(F32).T.astype(BF16)
            vals_t[:, at] = vals[at, :].astype(F32).T.astype(BF16)
            dk[at, :] = jnp.zeros((KC, BLK), F32)
            dv[at, :] = jnp.zeros((KC, BLK), F32)

        rope_rows(table, x_hi * ROWS, cos, sin, ROWS)
        rope_rows(table, 0, cos_r, sin_r, ROWS)
        lane = lax.broadcasted_iota(jnp.int32, (QT, 128), 1) // HD

        def heads(pair, tiles):
            lanes = slice(pair * 128, pair * 128 + 128)
            for t in tiles:
                rows = slice(t * QT, (t + 1) * QT)
                full = x_hi * (ROWS // KC) + t * QT // KC
                rest = (t + 1) * QT - t * QT // KC * KC
                diagonal = pl.ds(pl.multiple_of(full * KC, KC), rest)

                def chunk(j):
                    return pl.ds(pl.multiple_of(j * KC, KC), KC)

                for side in range(2):
                    qm[side] = jnp.where(lane == side, q[rows, lanes], jnp.zeros((), BF16))
                    dom[side] = jnp.where(lane == side, do[rows, lanes], jnp.zeros((), BF16))

                def score(at, tops, masked):
                    new = []
                    for side in range(2):
                        s = lax.dot_general(keys[at, lanes], qm[side], nt, preferred_element_type=F32)
                        if masked:
                            ki = lax.broadcasted_iota(jnp.int32, (rest, QT), 0)
                            qi = lax.broadcasted_iota(jnp.int32, (rest, QT), 1) + t * QT % KC
                            s = jnp.where(ki <= qi, s, MASKED)
                        st[side, at, :] = s
                        new.append(jnp.maximum(tops[side], jnp.max(s, axis=0, keepdims=True)))
                    return tuple(new)

                low = jnp.full((1, QT), MASKED, F32)
                tops = lax.fori_loop(0, full, lambda j, m: score(chunk(j), m, False), (low, low))
                tops = score(diagonal, tops, True)

                def weigh(at, carry):
                    new = []
                    for side in range(2):
                        total, dot = carry[2 * side : 2 * side + 2]
                        p = jnp.exp(st[side, at, :] - tops[side])
                        st[side, at, :] = p
                        d = lax.dot_general(vals[at, lanes], dom[side], nt, preferred_element_type=F32)
                        dp[side, at, :] = d
                        new.append(total + jnp.sum(p, axis=0, keepdims=True))
                        new.append(dot + jnp.sum(p * d, axis=0, keepdims=True))
                    return tuple(new)

                zero = jnp.zeros((1, QT), F32)
                sums = weigh(diagonal, lax.fori_loop(0, full, lambda j, m: weigh(chunk(j), m), (zero,) * 4))
                inv = [1.0 / sums[0], 1.0 / sums[2]]
                delta = [sums[1] * inv[0], sums[3] * inv[1]]
                out_t[:, rows] = jnp.zeros((128, QT), F32)
                dq_t[:, rows] = jnp.zeros((128, QT), F32)

                def spread(at):
                    new_v, new_k = dv[at, lanes], dk[at, lanes]
                    for side in range(2):
                        hrows = slice((2 * pair + side) * HD, (2 * pair + side + 1) * HD)
                        trows = slice(side * HD, (side + 1) * HD)
                        p = st[side, at, :] * inv[side]
                        p_low = p.astype(BF16)
                        ds = (p * (dp[side, at, :] - delta[side])).astype(BF16)
                        out_t[trows, rows] += jnp.dot(vals_t[hrows, at], p_low, preferred_element_type=F32)
                        dq_t[trows, rows] += jnp.dot(keys_t[hrows, at], ds, preferred_element_type=F32)
                        new_v += jnp.dot(p_low, dom[side], preferred_element_type=F32)
                        new_k += jnp.dot(ds, qm[side], preferred_element_type=F32)
                    dv[at, lanes] = new_v
                    dk[at, lanes] = new_k

                @pl.loop(0, full)
                def _(j):
                    spread(chunk(j))

                spread(diagonal)

        def end_pair(pair):
            lanes = slice(pair * 128, pair * 128 + 128)
            copy = pairs_back[pair]

            @pl.when(x_hi == 1)
            def _():
                dkv[pair, :, :128] = turn_back(dk[:ROWS, lanes], cos_r[...], sin_r[...]).astype(BF16)
                dkv[pair, :, 128:] = dv[:ROWS, lanes].astype(BF16)
                copy.start()

            for t in range(ROWS // 512):
                rows = slice(t * 512, (t + 1) * 512)
                att[rows, lanes] = out_t[:, rows].T.astype(BF16)
                raw[rows, 2 * BLK + pair * 128 : 2 * BLK + pair * 128 + 128] = turn_back(
                    dq_t[:, rows].T * (HD**-0.5), cos[rows, :], sin[rows, :]
                ).astype(BF16)

        heads(0, (0, 1, 2))

        def pass_blocks(move, own, got, cols, buf):
            move.wait_recv()
            views = staged([b_s1.at[own, :, cols], b_p.at[got], b_s1.at[own + 1, :, cols], b_p.at[got + 1]])
            for k in range(2):
                c_s1[buf + k] = (views[2 * k][...].astype(F32) + views[2 * k + 1][...].astype(F32)).astype(BF16)
            passed[buf // 2].start()

        pass_blocks(bp[0], 2, 0, lo, 0)
        pass_blocks(bp[1], 4, 2, hi, 2)
        heads(0, (3,))
        end_pair(0)

        heads(1, (0, 1, 2))

        heads(1, (3,))
        end_pair(1)

    pl.run_scoped(
        attend,
        pltpu.VMEM((2 * ROWS, BLK), BF16),
        pltpu.VMEM((2 * ROWS, BLK), BF16),
        pltpu.VMEM((BLK, 2 * ROWS), BF16),
        pltpu.VMEM((BLK, 2 * ROWS), BF16),
        pltpu.VMEM((2, 2 * ROWS, QT), F32),
        pltpu.VMEM((2, 2 * ROWS, QT), F32),
        pltpu.VMEM((2, QT, 128), BF16),
        pltpu.VMEM((2, QT, 128), BF16),
    )
    def finish(w1v, w2v, w3v):
        w_loads = [here(w1, w1v), here(w3, w3v), here(w2, w2v)]

        def z_at(dz, first=0, count=128):
            return pl.ds(pl.multiple_of(lax.rem(z + dz, 4) * 128 + first, 64), count)

        def to_z(total, got):
            return [
                remote(total.at[z_at(2, 0, 64)], got.at[0, pl.ds(0, 64)], above),
                remote(total.at[z_at(2, 64, 64)], got.at[0, pl.ds(64, 64)], below),
                remote(total.at[z_at(1, 64, 64)], got.at[1, pl.ds(64, 64)], above),
                remote(total.at[z_at(3, 0, 64)], got.at[2, pl.ds(0, 64)], below),
            ]

        def pass_on(total, got, first, buf):
            first[0].wait_recv()
            buf[0] = (total[z_at(1, 0, 64), :].astype(F32) + got[0, :64, :].astype(F32)).astype(BF16)
            one = remote(buf.at[0], got.at[1, pl.ds(0, 64)], above)
            first[1].wait_recv()
            buf[1] = (total[z_at(3, 64, 64), :].astype(F32) + got[0, 64:, :].astype(F32)).astype(BF16)
            two = remote(buf.at[1], got.at[2, pl.ds(64, 64)], below)
            return [first[2], first[3], one, two]

        def from_z(chunk, rows):
            at = z_at(0)
            return [here(chunk, rows.at[at]), remote(chunk, rows.at[at], above), remote(chunk, rows.at[at], below)]

        def pass_rows(moves, rows):
            moves[1].wait_recv()
            one = remote(rows.at[z_at(3, 0, 64)], rows.at[z_at(3, 0, 64)], above)
            moves[2].wait_recv()
            two = remote(rows.at[z_at(1, 64, 64)], rows.at[z_at(1, 64, 64)], below)
            return moves[0], [one, two]

        load_active.wait()
        load_hidden.wait()
        lefts.want(1, 2)
        arrived(a1)
        s = staged([a_r1.at[2], a_r1.at[3], a_r1.at[1]])
        lefts.run(
            [((1,), j, lambda l, k=k: product(a_s2.at[k], [l], [active], [s[k]])) for k, j in enumerate((2, 3, 1))],
            after=((0, 1), 2),
        )
        for copy in a_y:
            copy.start()
        tail = [raw.at[:, pl.ds(2 * BLK, BLK)], att]
        d1 = []
        for k, (j, target) in enumerate(((2, far), (1, up), (3, down))):
            jobs = [((0, 1), j + 4 * i, lambda a, b, i=i: product(d_s1.at[2 * k + i], [a, b], tail)) for i in range(2)]
            lefts.run(jobs, after=((0, 1), (1, 3)[k]) if k < 2 else ((0,), 2))
            d1.append(remote(d_s1.at[pl.ds(2 * k, 2)], d_r1.at[pl.ds(2 * k, 2)], target))

        for copy in w_loads[:2]:
            copy.wait()
        row_products(other, att, active, w1v, 3 * BLK, w3v, theirs)
        br_core = remote(theirs, br_c, mate)
        row_products(core, att, active, w1v, 3 * BLK, w3v, br_m)

        br_core.wait_recv()
        add_rows(br_m, br_c)
        br1 = to_z(br_m, br_z)


        def local_grads(pair, more):
            lanes = slice(pair * 128, pair * 128 + 128)
            k = turn_back(dk[own_keys, lanes], cos[...], sin[...])
            v = dv[own_keys, lanes]
            if more:
                k = k + dkv[pair, :, :128].astype(F32)
                v = v + dkv[pair, :, 128:].astype(F32)
            raw[:, lanes] = k.astype(BF16)
            raw[:, BLK + pair * 128 : BLK + pair * 128 + 128] = v.astype(BF16)

        for pair, copy in enumerate(pairs_back):

            @pl.when(x_hi == 1)
            def _():
                local_grads(pair, False)
                copy.wait_send()

            @pl.when(x_hi == 0)
            def _():
                copy.wait_recv()
                local_grads(pair, True)

        br_core.wait_send()
        copies.sent = [copy for copy in copies.sent if copy is not br_core]
        w_loads[2].wait()
        row_products(other, raw, hidden, w1v, 0, w2v, theirs, unit, ub, sems, vec_t)
        ng_core = remote(theirs, ng_c, mate)

        row_products(core, raw, hidden, w1v, 0, w2v, ng_m, unit, ub, sems, vec_m)
        br2 = pass_on(br_m, br_z, br1, turned.at[0])
        ng_core.wait_recv()
        add_rows(ng_m, ng_c)
        ng1 = to_z(ng_m, ng_z)

        va[...] = jnp.zeros_like(va)
        for j in range(8):
            va[j, 0:2, :] = vec_t[j, 0:2, :] + vec_m[j, 0:2, :]
        va_sent = [remote(va, va_r.at[k], along[k]) for k in range(3)]

        for copy in passed:
            copy.wait_send()
        copies.sent = [copy for copy in copies.sent if all(copy is not old for old in passed)]
        pairs = raw.at[:, pl.ds(0, 512)]
        c1 = []
        for k, (j, target) in enumerate(((2, far), (1, up), (3, down))):
            jobs = [((0,), j + 4 * i, lambda l, i=i: product(c_s1.at[2 * k + i], [l], [pairs])) for i in range(2)]
            lefts.run(jobs, after=((0,), (1, 3)[k]) if k < 2 else ((0,), 4))
            c1.append(remote(c_s1.at[pl.ds(2 * k, 2)], c_r1.at[pl.ds(2 * k, 2)], target))

        arrived(b1 + passed)
        s = staged([b_r1.at[1], b_r1.at[3]])
        lefts.run([((0,), 4, lambda l: product(b_s2, [l], [hidden], s))], after=((1,), 0))
        for copy in b2:
            copy.start()
        arrived(a_y)
        s = staged([a_r1.at[0], a_r2.at[0], a_r2.at[1], a_r2.at[2]])
        lefts.run([((1,), 0, lambda l: product(a_m, [l], [active], s))], after=((0, 1), 4))
        a3 = remote(a_m, a_x, over)

        arrived(br2)
        tile = 32

        def share(total, got, i, j):
            at = pl.ds(pl.multiple_of(i * tile, tile), tile)
            from_all = pl.ds(pl.multiple_of(z * 128 + i * tile, tile), tile)
            cols = slice(j * BLK, (j + 1) * BLK)
            return total[from_all, cols].astype(F32) + (got[1, at, cols].astype(F32) + got[2, at, cols].astype(F32))

        def line(row, j):
            return jnp.concatenate([small[j, row : row + 1, :], small[j, row + 1 : row + 2, :]], axis=1)

        def spot(j):
            return pl.ds(pl.multiple_of(block_order(y, x_lo, j) * BLK, BLK), BLK)

        @pl.loop(0, 128 // tile)
        def _(i):
            at = pl.ds(pl.multiple_of(i * tile, tile), tile)
            for j in range(8):
                value = tok[at, spot(j)].astype(F32) + share(br_m, br_z, i, j) + line(4, j)
                br_o[at, spot(j)] = value.astype(BF16)

        ng2 = pass_on(ng_m, ng_z, ng1, turned.at[1])

        br3 = from_z(br_o, layer_out)
        arrived(d1)
        s = staged([d_r1.at[1], d_r1.at[3], d_r1.at[5]])
        lefts.run([((0, 1), 4, lambda a, b: product(d_s2, [a, b], tail, s))], after=((0,), 0))
        d2 = [remote(d_s2.at[upper], d_r2.at[upper], right), remote(d_s2.at[lower], d_r2.at[lower], left)]

        arrived(b2)
        s = staged([b_r1.at[0], b_r1.at[2], b_r2])
        lefts.run([((0,), 0, lambda l: product(b_m, [l], [hidden], s))], after=((0, 1), 0))
        b3 = remote(b_m, b_x, over)

        arrived(ng2)

        @pl.loop(0, 128 // tile)
        def _(i):
            at = pl.ds(pl.multiple_of(i * tile, tile), tile)
            rows = tok[at, :].astype(F32)
            mean = jnp.mean(rows, axis=-1, keepdims=True)
            centered = rows - mean
            inv = lax.rsqrt(jnp.mean(centered * centered, axis=-1, keepdims=True) + EPSILON)

            def terms(j):
                u = (tok[at, spot(j)].astype(F32) - mean) * inv
                return u, share(ng_m, ng_z, i, j) * line(0, j)

            first = second = jnp.zeros((tile, 1), F32)
            for j in range(8):
                u, g = terms(j)
                first += jnp.sum(g, axis=-1, keepdims=True)
                second += jnp.sum(g * u, axis=-1, keepdims=True)
            first, second = first / D, second / D
            for j in range(8):
                u, g = terms(j)
                ng_o[at, spot(j)] = (grad[at, spot(j)].astype(F32) + inv * (g - first - u * second)).astype(BF16)

        ng3 = from_z(ng_o, input_grad)
        for copy in va_sent:
            copy.wait_recv()
        vec_v[0] = (va[...] + va_r[1]) + (va_r[0] + va_r[2])
        vb = remote(vec_v.at[0], vb_r, mate)

        arrived(d2)
        s = staged([d_r1.at[0], d_r1.at[2], d_r1.at[4]]) + [d_r2]
        lefts.run([((0, 1), 0, lambda a, b: product(d_m, [a, b], tail, s))], after=((0,), 4))
        d3 = remote(d_m, d_x, over)

        vb.wait_recv()
        units[...] = jnp.zeros_like(units)
        units[0:3, :] = jnp.sum(raw[...].astype(F32), axis=0, keepdims=True).reshape(3, BLK)
        for j in range(4):
            units[3 + j : 4 + j, :] = up_bias_v[:, j * BLK : (j + 1) * BLK]
        for j in range(8):
            dy, dx = j % 4, j // 4
            my[dy, dx] = vec_v[0, j] + vb_r[j]
            my[dy, dx, 2:3, :] = bias_v[:, j * BLK : (j + 1) * BLK]
        for dy in range(4):
            my[dy, 2] = units[...]
        my_sent = [remote(my.at[1], my_r.at[0], up), remote(my.at[2], my_r.at[1], far), remote(my.at[3], my_r.at[2], down)]

        arrived(c1)
        s = staged([c_r1.at[1], c_r1.at[3], c_r1.at[5]])
        lefts.run([((0,), 4, lambda l: product(c_s2, [l], [pairs], s))], after=((0,), 0))
        c2 = [remote(c_s2.at[upper], c_r2.at[upper], right), remote(c_s2.at[lower], c_r2.at[lower], left)]

        br_own, br4 = pass_rows(br3, layer_out)

        a4 = settle(a_m, a_x, a3, piece3, pl.ds(0, 1024), True)
        b4 = settle(b_m, b_x, b3, piece2, pl.ds(0, 1024), True)
        arrived(c2)
        s = staged([c_r1.at[0], c_r1.at[2], c_r1.at[4]]) + [c_r2]
        lefts.run([((0,), 0, lambda l: product(c_m, [l], [pairs], s))])
        c3 = remote(c_m, c_x, over)

        ng_own, ng4 = pass_rows(ng3, input_grad)
        d4 = settle(d_m, d_x, d3, piece1, pl.ds(512, 512), False)

        arrived(my_sent)
        here_sum = (my[0] + my_r[1]) + (my_r[0] + my_r[2])
        mx[0, 0] = here_sum[0]
        mx[0, 1] = here_sum[2]
        mx[1, 0] = here_sum[1]
        mx[1, 1] = here_sum[2]
        mx_sent = [remote(mx.at[1], mx_r.at[0], right), remote(mx.at[0], mx_r.at[1], over), remote(mx.at[1], mx_r.at[2], left)]
        arrived(mx_sent)
        last[...] = (mx[0] + mx_r[1]) + (mx_r[0] + mx_r[2])
        vec_copy = remote(last.at[1], last_r, mate)
        c4 = settle(c_m, c_x, c3, piece1, pl.ds(0, 512), False)
        vec_copy.wait_recv()
        last_saved = [here(last, vec_out.at[pl.ds(0, 2)]), here(last_r, vec_out.at[2])]

        for own, copy in (a4, b4, c4, d4):
            own.wait()
            copy.wait_recv()
        br_own.wait()
        ng_own.wait()
        arrived(br4 + ng4)
        for copy in last_saved:
            copy.wait()
        for copy in copies.sent:
            copy.wait_send()

    pl.run_scoped(
        finish,
        pltpu.VMEM((D, 1024), BF16),
        pltpu.VMEM((D, 1024), BF16),
        pltpu.VMEM((D, 1024), BF16),
    )


def reduce_call(*args):
    low = lambda *shape: jax.ShapeDtypeStruct(shape, BF16)
    wide = lambda *shape: jax.ShapeDtypeStruct(shape, F32)
    vlow = lambda *shape: pltpu.VMEM(shape, BF16)
    vwide = lambda *shape: pltpu.VMEM(shape, F32)
    anywhere = pl.BlockSpec(memory_space=pl.ANY)
    n = 1024
    outs = [low(HALF, D), low(HALF, D), low(2, BLK, n), low(2, BLK, n), low(2, BLK, n), wide(3, 8, BLK)] + [
        low(4, BLK, n), low(3, BLK, n), low(BLK, n), low(4, BLK, 512), low(4, BLK, n), low(BLK, n), low(BLK, n),
        low(6, BLK, 512), low(6, BLK, 512),
    ]
    result = pl.pallas_call(
        reduce_kernel,
        in_specs=[anywhere] * 20,
        out_specs=[anywhere] * len(outs),
        out_shape=outs,
        scratch_shapes=[
            vlow(ROWS, BLK), vlow(ROWS, BLK), vlow(ROWS, n), vlow(ROWS, n), vlow(ROWS, BLK), vlow(ROWS, 3 * BLK),
            vwide(8, PACK, 128), vwide(ROWS, 128), vwide(ROWS, 128), vwide(ROWS, 128), vwide(ROWS, 128), vwide(192, 128),
            vwide(2 * ROWS, BLK), vwide(2 * ROWS, BLK), vwide(128, ROWS), vwide(128, ROWS), vlow(2, ROWS, BLK),
            vlow(2, HALF, HALF), vlow(HALF, D), vlow(HALF, D), vlow(HALF, D), vlow(3, 128, D), vlow(128, D),
            vlow(HALF, D), vlow(HALF, D), vlow(3, 128, D), vlow(128, D), vlow(2, 2, 64, D), vlow(128, D), vlow(128, D),
            vlow(2, 2, BLK, ROWS), vlow(4, BLK, n), vlow(3, BLK, n), vlow(BLK, n), vlow(BLK, n), vlow(BLK, n),
            vlow(6, BLK, 512), vlow(BLK, 512), vlow(BLK, 512), vlow(6, BLK, 512), vlow(BLK, 512), vlow(BLK, 512),
            vlow(BLK, 512), vlow(BLK, 512), vlow(BLK, 512), vlow(BLK, 512), vwide(8, 8, BLK), vwide(8, 8, BLK),
            vwide(8, 8, BLK), vwide(3, 8, 8, BLK), vwide(8, 8, BLK), vwide(8, BLK), vwide(4, 3, 8, BLK),
            vwide(3, 3, 8, BLK), vwide(2, 2, 8, BLK), vwide(3, 2, 8, BLK), vwide(2, 8, BLK), vwide(8, BLK),
            vwide(1, D), vwide(1, n), vwide(1, 8, 8, BLK),
            pltpu.SemaphoreType.DMA((72,)),
            pltpu.SemaphoreType.DMA((72,)),
            pltpu.SemaphoreType.DMA((32,)),
            pltpu.SemaphoreType.DMA((2,)),
            pltpu.SemaphoreType.DMA((2, 2)),
            pltpu.SemaphoreType.DMA((4,)),
        ],
        compiler_params=params(collective_id=1, has_side_effects=True),
        cost_estimate=cost(2 * ROWS * D * 5 * 1024, 128 * 1024 * 1024),
        name="reduce_phase",
    )(*args)
    return result[:6]


def body(tokens, ln_gain, ln_shift, out_bias, w_qkv, b_qkv, w_out, w_fc1, b_fc1, w_fc2, out_grad):
    f, c = lax.axis_index("fsdp"), lax.axis_index("ctx")
    x_hi, core = c // 2, c % 2
    tokens, out_grad = tokens[0], out_grad[0]

    own = (jnp.arange(HD) // 8 == f)[None, None, :]
    spread = lambda v: jnp.where(own, jnp.tile(v, (1, 1, 8)), jnp.zeros((), BF16)).reshape(-1)
    pack = jnp.concatenate(
        [
            ln_gain,
            ln_shift,
            out_bias,
            spread(jnp.roll(lax.dynamic_slice_in_dim(b_qkv, core * 4, 4, axis=1), -1, axis=0)),
            spread(lax.dynamic_slice_in_dim(b_fc1, core * 16, 16, axis=0)[None]),
            jnp.zeros((512,), BF16),
        ]
    )
    pack = pack.astype(F32).reshape(PACK, 128)

    (w_attn, w_up, w_down, normed_t, grad_t, unit, q, kv, kvr, do, active, hidden_grad, small, bias_grad, up_bias_grad,
     a_first, b_first) = (
        gather_call(w_qkv.transpose(1, 0, 2), w_out, w_fc1, w_fc2, tokens, out_grad, pack, ROPE)
    )
    layer_out, input_grad, attn_all, up_all, down_all, vec = reduce_call(
        w_attn, w_up, w_down, normed_t, grad_t, unit, q, kv, kvr, do, active, hidden_grad, small, bias_grad, up_bias_grad,
        a_first, b_first, tokens, out_grad, ROPE
    )
    qkv_out, proj_out, up_out, down_out, layer_out, input_grad = grads_call(
        attn_all, up_all, down_all, layer_out, input_grad
    )
    gain_grad, shift_grad, out_bias_grad = vec[0, 0], vec[0, 1], vec[0, 2]
    units = jnp.where(core == 0, vec[1:], vec[:0:-1]).reshape(2, 8 * BLK)
    qkv_bias_out = lax.dynamic_slice_in_dim(
        jnp.roll(units[:, : 3 * BLK].reshape(2, 3, 4, HD), 1, axis=1).transpose(1, 0, 2, 3).reshape(3, 8, HD), f * 8, 8, axis=2
    )
    up_bias_out = lax.dynamic_slice_in_dim(units[:, 3 * BLK : 7 * BLK].reshape(32, HD), f * 8, 8, axis=1)
    return (
        layer_out[None],
        input_grad[None],
        gain_grad,
        shift_grad,
        out_bias_grad,
        qkv_out.transpose(1, 0, 2),
        qkv_bias_out,
        proj_out,
        up_out,
        up_bias_out,
        down_out,
    )


def solution(mesh):
    in_specs = (
        P("fsdp", "ctx", None),
        P("fsdp"),
        P("fsdp"),
        P("fsdp"),
        P("fsdp", None, "tp"),
        P(None, "tp", "fsdp"),
        P("tp", "fsdp"),
        P("fsdp", "tp"),
        P("tp", "fsdp"),
        P("tp", "fsdp"),
        P("fsdp", "ctx", None),
    )
    out_specs = (
        P("fsdp", "ctx", None),
        P("fsdp", "ctx", None),
        P("fsdp"),
        P("fsdp"),
        P("fsdp"),
        P("fsdp", None, "tp"),
        P(None, "tp", "fsdp"),
        P("tp", "fsdp"),
        P("fsdp", "tp"),
        P("tp", "fsdp"),
        P("tp", "fsdp"),
    )
    return jax.shard_map(body, mesh=mesh, in_specs=in_specs, out_specs=out_specs, check_vma=False)
```
